32 devices in a mesh: gx: 4 (over z), gy: 2 (over y), gz: 4 (over x, core).
Axes of the slice: x: 2, y: 2, z: 4, core: 2. Of those that a mesh axis runs over, the one named last changes fastest.
Arguments:
- fields: float32 [4, 32, 64, 512], P(None, 'gx', 'gy', 'gz'), may hold values from -6 to 6
- velocity: float32 [3, 32, 64, 512], P(None, 'gx', 'gy', 'gz'), may hold values from -3 to 3
- diffusivity: float32 [4], replicated, may hold values from 0.05 to 0.5
- coupling: float32 [4, 4], replicated, may hold values from -1 to 1
- factor_x: float32 [32, 32], P('gx'), may hold values from -1 to 1, as said below
- factor_y: float32 [64, 32], P('gy'), may hold values from -1 to 1, as said below
- factor_z: float32 [512, 32], P('gz'), may hold values from -1 to 1, as said below
Outputs:
- core_tensor: float32 [4, 32, 32, 32], P(None, 'gx', 'gy', 'gz')
The draws below stay inside these ranges and needn't reach their ends.
Inputs may be any that keep to these rules, and one draw needn't show every extreme that they name: `factor_x`: the columns of each factor are orthonormal. `factor_y`: the columns of each factor are orthonormal. `factor_z`: the columns of each factor are orthonormal.
All inputs are finite; a program needn't handle non-finite values.
Results may differ from the reference program's by a relative error of at most 0.0003.
Values sent between devices are 32-bit elements; how exact they have to be, the bound alone decides.
A program may use at most 64 MiB of HBM per device.

```python
import math
import jax
import jax.numpy as jnp
from jax import lax

VARS = 4
R = 32
STEPS = 2
NX = 32
NY = 64
NZ = 512


def orthonormal(key, rows, salt):
    normal_draw = jax.random.normal(jax.random.fold_in(key, salt), (rows, R), jnp.float32)
    basis, upper = jnp.linalg.qr(normal_draw)
    return basis


def draw_factor_x(key, part):
    return orthonormal(key, NX, 11)


def draw_factor_y(key, part):
    return orthonormal(key, NY, 23)


def draw_factor_z(key, part):
    return orthonormal(key, NZ, 37)


def draw_fields(key, part):
    base = jax.random.fold_in(key, 51)
    rough_key = jax.random.fold_in(base, 1)
    phase_key = jax.random.fold_in(base, 2)
    shape = (VARS, NX, NY, NZ)
    rough = 0.8 * jnp.clip(jax.random.normal(rough_key, shape, jnp.float32), -3.5, 3.5)
    amplitude = 0.8
    phases = jax.random.uniform(phase_key, (VARS, 2), jnp.float32, -math.pi, math.pi)
    cells_y = jnp.arange(NY, dtype=jnp.float32)
    cells_z = jnp.arange(NZ, dtype=jnp.float32)
    wave_y = jnp.cos(0.5 * math.pi * cells_y[None, :] + phases[:, 0:1])
    wave_z = jnp.cos(0.5 * math.pi * cells_z[None, :] + phases[:, 1:2])
    wave = wave_y[:, None, :, None] * wave_z[:, None, None, :]
    return jnp.clip(rough + amplitude * wave, -6.0, 6.0)


def draw_velocity(key, part):
    base = jax.random.fold_in(key, 67)
    sign_key = jax.random.fold_in(base, 1)
    size_key = jax.random.fold_in(base, 2)
    heading = jnp.where(jax.random.bernoulli(sign_key, 0.5, (3, 1, 1, 1)), 1.0, -1.0).astype(jnp.float32)
    lowest = 1.5
    magnitude = jax.random.uniform(size_key, (3, NX, NY, NZ), jnp.float32, lowest, 3.0)
    return heading * magnitude


def normal_values(rng, extent, deviation, bound, kind=jnp.bfloat16):
    drawn = deviation * jax.random.normal(rng, extent, jnp.float32)
    return jnp.clip(drawn, min=-bound, max=bound).astype(kind)


def setup_inputs(seed: int = 0) -> dict:
    seeds = jax.random.split(jax.random.key(seed), 8)
    fields = draw_fields(jax.random.fold_in(seeds[7], 71), 0)
    velocity = draw_velocity(jax.random.fold_in(seeds[7], 71), 0)
    diffusivity = jnp.clip(jnp.exp(jax.random.uniform(seeds[2], (VARS,), jnp.float32, math.log(0.05), math.log(0.5))), 0.05, 0.5)
    coupling = normal_values(seeds[3], (VARS, VARS), 0.2, 1.0, jnp.float32)
    factor_x = draw_factor_x(jax.random.fold_in(seeds[7], 71), 0)
    factor_y = draw_factor_y(jax.random.fold_in(seeds[7], 71), 0)
    factor_z = draw_factor_z(jax.random.fold_in(seeds[7], 71), 0)
    return dict(fields=fields, velocity=velocity, diffusivity=diffusivity, coupling=coupling, factor_x=factor_x, factor_y=factor_y, factor_z=factor_z)


time_step = 0.2

def offset_view(padded, dimension, offset):
    indices = [slice(None)]
    for other in (1, 2, 3):
        if other == dimension:
            first_cell = 2 + offset
            indices.append(slice(first_cell, first_cell + padded.shape[other] - 4))
        else:
            indices.append(slice(2, padded.shape[other] - 2))
    return padded[tuple(indices)]

def tendency(padded, velocity, diffusivity, coupling):
    center = offset_view(padded, 1, 0)
    transport = jnp.zeros_like(center)
    laplace = jnp.zeros_like(center)
    for dimension in (1, 2, 3):
        gradient = (8.0 * (offset_view(padded, dimension, 1) - offset_view(padded, dimension, -1)) - (offset_view(padded, dimension, 2) - offset_view(padded, dimension, -2))) / 12.0
        transport = transport + velocity[dimension - 1][None] * gradient
        laplace = laplace + offset_view(padded, dimension, 1) + offset_view(padded, dimension, -1) - 2.0 * center
    mixing = jnp.einsum('vw,wxyz->vxyz', coupling, center, precision=lax.Precision.HIGHEST)
    return -transport + diffusivity[:, None, None, None] * laplace + center * mixing

def pad_zeros(values):
    return jnp.pad(values, ((0, 0), (2, 2), (2, 2), (2, 2)))

def reference(fields, velocity, diffusivity, coupling, factor_x, factor_y, factor_z):
    state = fields
    for repeat in range(STEPS):
        section = state + time_step * tendency(pad_zeros(state), velocity, diffusivity, coupling)
        state = 0.5 * (state + section + time_step * tendency(pad_zeros(section), velocity, diffusivity, coupling))
    highest = lax.Precision.HIGHEST
    partial_value = jnp.einsum('vxyz,zc->vxyc', state, factor_z, precision=highest)
    partial_value = jnp.einsum('vxyc,yb->vxbc', partial_value, factor_y, precision=highest)
    return jnp.einsum('vxbc,xa->vabc', partial_value, factor_x, precision=highest)
```

```python
import functools
import jax
import jax.numpy as jnp
from jax import lax
from jax.experimental import pallas as pl
from jax.experimental.pallas import tpu as pltpu
from jax.sharding import PartitionSpec as P

STEPS = 2
STAGES = 2 * STEPS
HALO = 2
PAD = 8
MESH = pl.DeviceIdType.MESH
HIGHEST = lax.Precision.HIGHEST


time_step = 0.2
def with_halo(cells, sides, width):
    for axis, dim in sides:
        count = lax.axis_size(axis)
        ends = count - 1
        head = lax.slice_in_dim(cells, 0, width, axis=dim)
        tail = lax.slice_in_dim(cells, cells.shape[dim] - width, cells.shape[dim], axis=dim)
        cells = jnp.concatenate(
            [
                lax.ppermute(tail, axis, [(i, (i + 1) % count) for i in range(ends)]),
                cells,
                lax.ppermute(head, axis, [((i + 1) % count, i) for i in range(ends)]),
            ],
            axis=dim,
        )
    return cells


def offset_view(padded, dimension, offset):
    indices = [slice(None)]
    for other in (1, 2, 3):
        if other == dimension:
            first_cell = 2 + offset
            indices.append(slice(first_cell, first_cell + padded.shape[other] - 4))
        else:
            indices.append(slice(2, padded.shape[other] - 2))
    return padded[tuple(indices)]


def tendency(padded, velocity, diffusivity, coupling):
    center = offset_view(padded, 1, 0)
    transport = jnp.zeros_like(center)
    laplace = jnp.zeros_like(center)
    for dimension in (1, 2, 3):
        gradient = (
            8.0 * (offset_view(padded, dimension, 1) - offset_view(padded, dimension, -1))
            - (offset_view(padded, dimension, 2) - offset_view(padded, dimension, -2))
        ) / 12.0
        transport = transport + velocity[dimension - 1][None] * gradient
        laplace = (
            laplace
            + offset_view(padded, dimension, 1)
            + offset_view(padded, dimension, -1)
            - 2.0 * center
        )
    mixing = jnp.einsum("vw,wxyz->vxyz", coupling, center, precision=lax.Precision.HIGHEST)
    return -transport + diffusivity[:, None, None, None] * laplace + center * mixing


def with_edges(values):
    return with_halo(values, (("gx", 1), ("gy", 2), ("gz", 3)), 2)


def local_plain(fields, velocity, diffusivity, coupling, factor_x, factor_y, factor_z):
    state = fields
    for repeat in range(STEPS):
        section = state + time_step * tendency(with_edges(state), velocity, diffusivity, coupling)
        state = 0.5 * (
            state
            + section
            + time_step * tendency(with_edges(section), velocity, diffusivity, coupling)
        )
    highest = lax.Precision.HIGHEST
    partial_value = jnp.einsum("vxyz,zc->vxyc", state, factor_z, precision=highest)
    partial_value = lax.psum_scatter(partial_value, "gz", scatter_dimension=3, tiled=True)
    partial_value = jnp.einsum("vxyc,yb->vxbc", partial_value, factor_y, precision=highest)
    partial_value = lax.psum_scatter(partial_value, "gy", scatter_dimension=2, tiled=True)
    partial_value = jnp.einsum("vxbc,xa->vabc", partial_value, factor_x, precision=highest)
    core_tensor = lax.psum_scatter(partial_value, "gx", scatter_dimension=1, tiled=True)
    return core_tensor


class Plan:
    def __init__(self, mesh_shape, fields, factor_x):
        self.nx, self.ny, self.nz = (mesh_shape[a] for a in ("gx", "gy", "gz"))
        self.vars, self.lx, self.ly, self.lz = fields
        self.rank = factor_x[1]
        self.ax, self.by, self.cz = self.rank // self.nx, self.rank // self.ny, self.rank // self.nz
        self.edge = [0, 1, self.lx - 2, self.lx - 1]
        self.inner = list(range(2, self.lx - 2))
        self.tiles = self.ly // 8

    def fits(self):
        return (
            self.lz == 128
            and self.ly % 8 == 0
            and self.lx > 4
            and self.lx <= 12
            and len(self.edge) * self.tiles * 4 <= 128
            and len(self.inner) * self.tiles * 4 <= 128
            and self.rank % self.nx == 0 and self.rank % self.ny == 0 and self.rank % self.nz == 0
            and self.cz % 8 == 0
            and self.lx * self.by % 128 == 0
            and self.ax * self.by % 128 == 0
        )


def kernel(
    plan,
    fields,
    velocity,
    diffusivity,
    coupling,
    factor_x,
    factor_y,
    factor_z,
    out,
    cells,
    speed,
    y_out,
    y_in,
    z_out,
    z_in,
    spread_y,
    spread_x,
    yz_out,
    yz_in,
    x_out,
    x_in,
    load_sem,
    x_send,
    x_recv,
    ya_send,
    ya_recv,
    za_send,
    za_recv,
    yb_send,
    yb_recv,
    zb_send,
    zb_recv,
    yz_send,
    yz_recv,
    xs_send,
    xs_recv,
):
    p = plan
    nx, ny, nz = p.nx, p.ny, p.nz
    lx, ly, nv = p.lx, p.ly, p.vars
    mx, my, mz = lax.axis_index("gx"), lax.axis_index("gy"), lax.axis_index("gz")
    rows = slice(PAD, PAD + ly)
    low_x, high_x = mx > 0, mx < nx - 1
    low_y, high_y = my > 0, my < ny - 1
    low_z, high_z = mz > 0, mz < nz - 1

    def remote(src, dst, send, recv, axis, to):
        return pltpu.make_async_remote_copy(
            src_ref=src, dst_ref=dst, send_sem=send, recv_sem=recv,
            device_id={axis: to}, device_id_type=MESH,
        )

    def up(index, count):
        return lax.rem(index + 1, count)

    def down(index, count):
        return lax.rem(index + count - 1, count)

    def x_messages(s, v):
        if s == 0:
            top, bottom = fields.at[v, lx - 2:lx], fields.at[v, 0:2]
        else:
            top = cells.at[s, v, lx:lx + 2, rows]
            bottom = cells.at[s, v, 2:4, rows]
        return [
            (high_x, low_x, remote(
                top, cells.at[s, v, 0:2, rows],
                x_send.at[s, v, 0], x_recv.at[s, v, 0], "gx", up(mx, nx))),
            (low_x, high_x, remote(
                bottom, cells.at[s, v, lx + 2:lx + 4, rows],
                x_send.at[s, v, 1], x_recv.at[s, v, 1], "gx", down(mx, nx))),
        ]

    def yz_messages(s, group, v):
        if group == 0:
            ys, yr = ya_send.at[s, v], ya_recv.at[s, v]
            zs, zr = za_send.at[s, v], za_recv.at[s, v]
            pick = lambda ref, *lead: ref.at[(*lead, v)]
        else:
            ys, yr, zs, zr = yb_send.at[s], yb_recv.at[s], zb_send.at[s], zb_recv.at[s]
            pick = lambda ref, *lead: ref.at[lead]
        return [
            (high_y, low_y, remote(
                pick(y_out, s, group, 1), pick(y_in, s, group, 0),
                ys.at[0], yr.at[0], "gy", up(my, ny))),
            (low_y, high_y, remote(
                pick(y_out, s, group, 0), pick(y_in, s, group, 1),
                ys.at[1], yr.at[1], "gy", down(my, ny))),
            (high_z, low_z, remote(
                pick(z_out, s, group), pick(z_in, s, group, 0),
                zs.at[0], zr.at[0], "gz", up(mz, nz))),
            (low_z, high_z, remote(
                pick(z_out, s, group), pick(z_in, s, group, 1),
                zs.at[1], zr.at[1], "gz", down(mz, nz))),
        ]

    def start(messages):
        for sends, _, copy in messages:
            pl.when(sends)(copy.start)

    def arrive(messages):
        for _, gets, copy in messages:
            pl.when(gets)(copy.wait_recv)

    def sent(messages):
        for sends, _, copy in messages:
            pl.when(sends)(copy.wait_send)

    lane = lax.broadcasted_iota(jnp.int32, (8, 128), 1)
    wide = lax.broadcasted_iota(jnp.int32, (ly, 128), 1)
    groups = (p.edge, p.inner)

    def pack(s, group, v, layers):
        z = jnp.zeros((8, 128), jnp.float32)
        for j, value in enumerate(layers):
            y_out[s, group, 0, v, 2 * j:2 * j + 2] = value[0:2]
            y_out[s, group, 1, v, 2 * j:2 * j + 2] = value[ly - 2:ly]
            for t in range(p.tiles):
                place = 4 * (j * p.tiles + t)
                turned = pltpu.roll(value[8 * t:8 * t + 8], (place + 2) % 128, 1)
                z = jnp.where((lane >= place) & (lane < place + 4), turned, z)
        z_out[s, group, v] = z

    def advance(s, group, v):
        edges = jnp.where(lane % 4 < 2, z_in[s, group, 0, v], z_in[s, group, 1, v])
        spread = time_step * diffusivity[v]
        rates = [time_step * coupling[v, w] for w in range(nv)]
        keep = 1.0 - 6.0 * spread
        layers = groups[group]
        for j, x in enumerate(layers):
            cells[s, v, x + 2, PAD - 2:PAD] = y_in[s, group, 0, v, 2 * j:2 * j + 2]
            cells[s, v, x + 2, PAD + ly:PAD + ly + 2] = y_in[s, group, 1, v, 2 * j:2 * j + 2]
        result = []
        for j, x in enumerate(layers):
            centre = cells[s, v, x + 2, rows]
            beside = jnp.concatenate(
                [pltpu.roll(edges, (126 - 4 * (j * p.tiles + t)) % 128, 1) for t in range(p.tiles)], axis=0)
            near = [
                (cells[s, v, x + 3, rows], cells[s, v, x + 1, rows],
                 cells[s, v, x + 4, rows], cells[s, v, x, rows]),
                (cells[s, v, x + 2, PAD + 1:PAD + 1 + ly], cells[s, v, x + 2, PAD - 1:PAD - 1 + ly],
                 cells[s, v, x + 2, PAD + 2:PAD + 2 + ly], cells[s, v, x + 2, PAD - 2:PAD - 2 + ly]),
                (pltpu.roll(jnp.where(wide == 0, beside, centre), 127, 1),
                 pltpu.roll(jnp.where(wide == 127, beside, centre), 1, 1),
                 pltpu.roll(jnp.where(wide <= 1, beside, centre), 126, 1),
                 pltpu.roll(jnp.where(wide >= 126, beside, centre), 2, 1)),
            ]
            moved = around = None
            for a, (next1, last1, next2, last2) in enumerate(near):
                flow = speed[a, x] * (8.0 * (next1 - last1) - (next2 - last2))
                both = next1 + last1
                moved = flow if moved is None else moved + flow
                around = both if around is None else around + both
            factor = keep
            for w in range(nv):
                factor = factor + rates[w] * cells[s, w, x + 2, rows]
            new = centre * factor + moved + spread * around
            if s % 2 == 1:
                new = 0.5 * (new + cells[s - 1, v, x + 2, rows])
            cells[s + 1, v, x + 2, rows] = new
            result.append(new)
        return result

    def clear(condition, ref, *index):
        @pl.when(jnp.logical_not(condition))
        def _():
            ref[index] = jnp.zeros_like(ref[index])

    for s in range(STAGES):
        clear(low_x, cells, s, slice(None), slice(0, 2))
        clear(high_x, cells, s, slice(None), slice(lx + 2, lx + 4))
        for group in range(2):
            for side, condition in ((0, low_y), (1, high_y)):
                clear(condition, y_in, s, group, side)
            for side, condition in ((0, low_z), (1, high_z)):
                clear(condition, z_in, s, group, side)

    load = pltpu.make_async_copy(fields, cells.at[0, :, 2:lx + 2, rows], load_sem.at[0])
    load.start()
    load_speed = pltpu.make_async_copy(velocity, speed, load_sem.at[1])
    load_speed.start()

    partners = [
        {"gy": lax.rem(my + dy, ny), "gz": lax.rem(mz + dz, nz)}
        for dy in range(ny) for dz in range(nz) if dy or dz
    ]
    line = [{"gx": lax.rem(mx + dx, nx)} for dx in range(1, nx)]
    barrier = pltpu.get_barrier_semaphore()
    for device in partners + line:
        pl.semaphore_signal(barrier, inc=1, device_id=device, device_id_type=MESH)
    pl.semaphore_wait(barrier, len(partners) + len(line))

    for v in range(nv):
        start(x_messages(0, v))
    load.wait()

    def first_pack(v, carry):
        for group in range(2):
            pack(0, group, v, [cells[0, v, x + 2, rows] for x in groups[group]])
        start(yz_messages(0, 0, v))
        return carry

    lax.fori_loop(0, nv, first_pack, 0)
    start(yz_messages(0, 1, None))
    load_speed.wait()
    speed[...] = speed[...] * (-time_step / 12.0)

    chunk_y = lx * p.by
    wide_y = ny * chunk_y
    column = lax.broadcasted_iota(jnp.int32, (p.rank, wide_y), 1)
    row = lax.broadcasted_iota(jnp.int32, (p.rank, wide_y), 0)
    place_y = jnp.where(row == column // chunk_y * p.by + column % p.by, 1.0, 0.0)
    repeated = jnp.dot(factor_y[...], place_y, precision=HIGHEST, preferred_element_type=jnp.float32)
    column = lax.broadcasted_iota(jnp.int32, (ly, wide_y), 1)
    for x in range(lx):
        spread_y[x * ly:(x + 1) * ly] = jnp.where(column % chunk_y // p.by == x, repeated, 0.0)
    chunk_x = p.ax * p.by
    wide_x = nx * chunk_x
    column = lax.broadcasted_iota(jnp.int32, (p.rank, wide_x), 1)
    row = lax.broadcasted_iota(jnp.int32, (p.rank, wide_x), 0)
    place_x = jnp.where(row == column // p.by, 1.0, 0.0)
    repeated = jnp.dot(factor_x[...], place_x, precision=HIGHEST, preferred_element_type=jnp.float32)
    column = lax.broadcasted_iota(jnp.int32, (p.by, wide_x), 1)
    row = lax.broadcasted_iota(jnp.int32, (p.by, wide_x), 0)
    for x in range(lx):
        spread_x[x * p.by:(x + 1) * p.by] = jnp.where(column % p.by == row, repeated[x:x + 1], 0.0)

    for s in range(STAGES):
        last = s == STAGES - 1

        def edge_part(v, carry):
            messages = x_messages(s, v) + yz_messages(s, 0, v)
            arrive(messages)
            layers = advance(s, 0, v)
            if not last:
                start(x_messages(s + 1, v))
                pack(s + 1, 0, v, layers)
                start(yz_messages(s + 1, 0, v))
            return carry

        def inner_part(v, carry):
            layers = advance(s, 1, v)
            if not last:
                pack(s + 1, 1, v, layers)
            return carry

        lax.fori_loop(0, nv, edge_part, 0)
        arrive(yz_messages(s, 1, None))
        lax.fori_loop(0, nv, inner_part, 0)
        if not last:
            start(yz_messages(s + 1, 1, None))

    for v in range(nv):
        state = cells[STAGES, v, 2:lx + 2, rows].reshape(lx * ly, p.lz)
        reduced = lax.dot_general(
            factor_z[...], state, (((0,), (1,)), ((), ())),
            precision=HIGHEST, preferred_element_type=jnp.float32)
        reduced = jnp.dot(reduced, spread_y[...], precision=HIGHEST, preferred_element_type=jnp.float32)
        for y in range(ny):
            for z in range(nz):
                yz_out[y * nz + z, v] = reduced[
                    z * p.cz:(z + 1) * p.cz, y * chunk_y:(y + 1) * chunk_y]
    plane = []
    for i, device in enumerate(partners):
        plane.append(pltpu.make_async_remote_copy(
            src_ref=yz_out.at[device["gy"] * nz + device["gz"]], dst_ref=yz_in.at[i],
            send_sem=yz_send.at[i], recv_sem=yz_recv.at[i],
            device_id=device, device_id_type=MESH))
        plane[-1].start()
    total = yz_out[my * nz + mz]
    for i, copy in enumerate(plane):
        copy.wait_recv()
        total = total + yz_in[i]

    total = total.reshape(nv * p.cz, chunk_y)
    total = jnp.dot(total, spread_x[...], precision=HIGHEST, preferred_element_type=jnp.float32)
    for x in range(nx):
        x_out[x] = total[:, x * chunk_x:(x + 1) * chunk_x].reshape(nv, p.cz, chunk_x)
    along = []
    for i, device in enumerate(line):
        along.append(pltpu.make_async_remote_copy(
            src_ref=x_out.at[device["gx"]], dst_ref=x_in.at[i],
            send_sem=xs_send.at[i], recv_sem=xs_recv.at[i],
            device_id=device, device_id_type=MESH))
        along[-1].start()
    total = x_out[mx]
    for i, copy in enumerate(along):
        copy.wait_recv()
        total = total + x_in[i]
    out[...] = total

    for s in range(STAGES):
        def edge_sent(v, carry):
            sent(x_messages(s, v) + yz_messages(s, 0, v))
            return carry

        lax.fori_loop(0, nv, edge_sent, 0)
        sent(yz_messages(s, 1, None))
    for copy in plane + along:
        copy.wait_send()


def local_kernel(plan, fields, velocity, diffusivity, coupling, factor_x, factor_y, factor_z):
    p = plan
    nv, lx, ly = p.vars, p.lx, p.ly
    chunk_y, chunk_x = lx * p.by, p.ax * p.by
    others = p.ny * p.nz - 1
    vmem = lambda *shape: pltpu.VMEM(shape, jnp.float32)
    dma = lambda *shape: pltpu.SemaphoreType.DMA(shape)
    whole = pl.BlockSpec(memory_space=pltpu.VMEM)
    scalars = pl.BlockSpec(memory_space=pltpu.SMEM)
    result = pl.pallas_call(
        functools.partial(kernel, p),
        out_shape=jax.ShapeDtypeStruct((nv, p.cz, chunk_x), jnp.float32),
        in_specs=[pl.BlockSpec(memory_space=pl.ANY)] * 2 + [scalars] * 2 + [whole] * 3,
        out_specs=whole,
        scratch_shapes=[
            vmem(STAGES + 1, nv, lx + 4, ly + 2 * PAD, p.lz),
            vmem(3, lx, ly, p.lz),
            vmem(STAGES, 2, 2, nv, 8 * -(-max(4, lx - 4) // 4), p.lz),
            vmem(STAGES, 2, 2, nv, 8 * -(-max(4, lx - 4) // 4), p.lz),
            vmem(STAGES, 2, nv, 8, 128),
            vmem(STAGES, 2, 2, nv, 8, 128),
            vmem(lx * ly, p.ny * chunk_y),
            vmem(chunk_y, p.nx * chunk_x),
            vmem(p.ny * p.nz, nv, p.cz, chunk_y),
            vmem(others, nv, p.cz, chunk_y),
            vmem(p.nx, nv, p.cz, chunk_x),
            vmem(p.nx - 1, nv, p.cz, chunk_x),
            dma(2),
            dma(STAGES, nv, 2), dma(STAGES, nv, 2),
            dma(STAGES, nv, 2), dma(STAGES, nv, 2),
            dma(STAGES, nv, 2), dma(STAGES, nv, 2),
            dma(STAGES, 2), dma(STAGES, 2),
            dma(STAGES, 2), dma(STAGES, 2),
            dma(others), dma(others),
            dma(p.nx - 1), dma(p.nx - 1),
        ],
        compiler_params=pltpu.CompilerParams(
            collective_id=0, has_side_effects=True, vmem_limit_bytes=40 * 1024 * 1024),
    )(fields, velocity, diffusivity, coupling, factor_x, factor_y, factor_z)
    result = result.reshape(nv, p.cz, p.ax, p.by)
    return jnp.transpose(result, (0, 2, 3, 1))


def solution(mesh):
    def local(fields, velocity, diffusivity, coupling, factor_x, factor_y, factor_z):
        plan = Plan(mesh.shape, fields.shape, factor_x.shape)
        run = functools.partial(local_kernel, plan) if plan.fits() else local_plain
        return run(fields, velocity, diffusivity, coupling, factor_x, factor_y, factor_z)

    return jax.shard_map(
        local,
        mesh=mesh,
        in_specs=(
            P(None, "gx", "gy", "gz"),
            P(None, "gx", "gy", "gz"),
            P(),
            P(),
            P("gx", None),
            P("gy", None),
            P("gz", None),
        ),
        out_specs=P(None, "gx", "gy", "gz"),
        check_vma=False,
    )
```

```python
import functools
import jax
import jax.numpy as jnp
from jax import lax
from jax.experimental import pallas as pl
from jax.experimental.pallas import tpu as pltpu
from jax.sharding import PartitionSpec as P

STEPS = 2
STAGES = 2 * STEPS
HALO = 2
PAIR = 2
PAD = 8
MESH = pl.DeviceIdType.MESH
HIGHEST = lax.Precision.HIGHEST


time_step = 0.2
def with_halo(cells, sides, width):
    for axis, dim in sides:
        count = lax.axis_size(axis)
        ends = count - 1
        head = lax.slice_in_dim(cells, 0, width, axis=dim)
        tail = lax.slice_in_dim(cells, cells.shape[dim] - width, cells.shape[dim], axis=dim)
        cells = jnp.concatenate(
            [
                lax.ppermute(tail, axis, [(i, (i + 1) % count) for i in range(ends)]),
                cells,
                lax.ppermute(head, axis, [((i + 1) % count, i) for i in range(ends)]),
            ],
            axis=dim,
        )
    return cells


def offset_view(padded, dimension, offset):
    indices = [slice(None)]
    for other in (1, 2, 3):
        if other == dimension:
            first_cell = 2 + offset
            indices.append(slice(first_cell, first_cell + padded.shape[other] - 4))
        else:
            indices.append(slice(2, padded.shape[other] - 2))
    return padded[tuple(indices)]


def tendency(padded, velocity, diffusivity, coupling):
    center = offset_view(padded, 1, 0)
    transport = jnp.zeros_like(center)
    laplace = jnp.zeros_like(center)
    for dimension in (1, 2, 3):
        gradient = (
            8.0 * (offset_view(padded, dimension, 1) - offset_view(padded, dimension, -1))
            - (offset_view(padded, dimension, 2) - offset_view(padded, dimension, -2))
        ) / 12.0
        transport = transport + velocity[dimension - 1][None] * gradient
        laplace = (
            laplace
            + offset_view(padded, dimension, 1)
            + offset_view(padded, dimension, -1)
            - 2.0 * center
        )
    mixing = jnp.einsum("vw,wxyz->vxyz", coupling, center, precision=lax.Precision.HIGHEST)
    return -transport + diffusivity[:, None, None, None] * laplace + center * mixing


def with_edges(values):
    return with_halo(values, (("gx", 1), ("gy", 2), ("gz", 3)), 2)


def local_plain(fields, velocity, diffusivity, coupling, factor_x, factor_y, factor_z):
    state = fields
    for repeat in range(STEPS):
        section = state + time_step * tendency(with_edges(state), velocity, diffusivity, coupling)
        state = 0.5 * (
            state
            + section
            + time_step * tendency(with_edges(section), velocity, diffusivity, coupling)
        )
    highest = lax.Precision.HIGHEST
    partial_value = jnp.einsum("vxyz,zc->vxyc", state, factor_z, precision=highest)
    partial_value = lax.psum_scatter(partial_value, "gz", scatter_dimension=3, tiled=True)
    partial_value = jnp.einsum("vxyc,yb->vxbc", partial_value, factor_y, precision=highest)
    partial_value = lax.psum_scatter(partial_value, "gy", scatter_dimension=2, tiled=True)
    partial_value = jnp.einsum("vxbc,xa->vabc", partial_value, factor_x, precision=highest)
    core_tensor = lax.psum_scatter(partial_value, "gx", scatter_dimension=1, tiled=True)
    return core_tensor


class Plan:
    def __init__(self, mesh_shape, fields, factor_x):
        self.nx, self.ny, self.nz = (mesh_shape[a] for a in ("gx", "gy", "gz"))
        self.vars, self.lx, self.ly, self.lz = fields
        self.rank = factor_x[1]
        self.ax, self.by, self.cz = self.rank // self.nx, self.rank // self.ny, self.rank // self.nz
        self.edge = [0, 1, self.lx - 2, self.lx - 1]
        self.inner = list(range(2, self.lx - 2))
        self.tiles = self.ly // 8

    def fits(self):
        return (
            self.lz == 128
            and self.ly % 8 == 0
            and min(self.nx, self.ny, self.nz) > 1
            and self.vars % PAIR == 0
            and self.lx > 4
            and self.lx <= 12
            and len(self.edge) * self.tiles * 4 <= 128
            and len(self.inner) * self.tiles * 4 <= 128
            and self.rank % self.nx == 0 and self.rank % self.ny == 0 and self.rank % self.nz == 0
            and self.cz % 8 == 0
            and self.lx * self.by % 128 == 0
            and self.ax * self.by % 128 == 0
        )


def kernel(
    plan,
    fields,
    velocity,
    diffusivity,
    coupling,
    factor_x,
    factor_y,
    factor_z,
    out,
    cells,
    speed,
    y_out,
    y_in,
    z_out,
    z_in,
    spread_y,
    spread_x,
    yz_out,
    yz_in,
    x_out,
    x_in,
    load_sem,
    x_send,
    x_recv,
    y_send,
    y_recv,
    z_send,
    z_recv,
    yz_send,
    yz_recv,
    xs_send,
    xs_recv,
):
    p = plan
    nx, ny, nz = p.nx, p.ny, p.nz
    lx, ly, nv = p.lx, p.ly, p.vars
    mx, my, mz = lax.axis_index("gx"), lax.axis_index("gy"), lax.axis_index("gz")
    rows = slice(PAD, PAD + ly)
    low_x, high_x = mx > 0, mx < nx - 1
    low_y, high_y = my > 0, my < ny - 1
    low_z, high_z = mz > 0, mz < nz - 1

    def remote(src, dst, send, recv, axis, to):
        return pltpu.make_async_remote_copy(
            src_ref=src, dst_ref=dst, send_sem=send, recv_sem=recv,
            device_id={axis: to}, device_id_type=MESH,
        )

    def up(index, count):
        return lax.rem(index + 1, count)

    def down(index, count):
        return lax.rem(index + count - 1, count)

    def x_messages(s, v):
        if s == 0:
            top, bottom = fields.at[v, lx - 2:lx], fields.at[v, 0:2]
        else:
            top = cells.at[s, v, lx:lx + 2, rows]
            bottom = cells.at[s, v, 2:4, rows]
        return [
            (high_x, low_x, remote(
                top, cells.at[s, v, 0:2, rows],
                x_send.at[0], x_recv.at[s, v, 0], "gx", up(mx, nx))),
            (low_x, high_x, remote(
                bottom, cells.at[s, v, lx + 2:lx + 4, rows],
                x_send.at[1], x_recv.at[s, v, 1], "gx", down(mx, nx))),
        ]

    chunks = nv // PAIR

    def yz_messages(s, group, c):
        if group == 0:
            which, place = pl.ds(c * PAIR, PAIR), c
        else:
            which, place = slice(None), chunks
        result = [
            (None, None, remote(
                z_out.at[s, group, which], z_in.at[s, group, 0, which],
                z_send.at[0], z_recv.at[s, place, 0], "gz", up(mz, nz))),
            (None, None, remote(
                z_out.at[s, group, which], z_in.at[s, group, 1, which],
                z_send.at[1], z_recv.at[s, place, 1], "gz", down(mz, nz))),
        ]
        if ny == 2:
            result.append((None, None, remote(
                y_out.at[s, group, 1 - my, which], y_in.at[s, group, my, which],
                y_send.at[0], y_recv.at[s, place, 0], "gy", 1 - my)))
        else:
            result += [
                (high_y, low_y, remote(
                    y_out.at[s, group, 1, which], y_in.at[s, group, 0, which],
                    y_send.at[0], y_recv.at[s, place, 0], "gy", up(my, ny))),
                (low_y, high_y, remote(
                    y_out.at[s, group, 0, which], y_in.at[s, group, 1, which],
                    y_send.at[1], y_recv.at[s, place, 1], "gy", down(my, ny))),
            ]
        return result

    def guarded(condition, action):
        if condition is None:
            action()
        else:
            pl.when(condition)(action)

    def start(messages):
        for sends, _, copy in messages:
            guarded(sends, copy.start)

    def arrive(messages):
        for _, gets, copy in messages:
            guarded(gets, copy.wait_recv)

    def all_sent():
        layers = cells.at[0:STAGES, :, 0:2, rows]
        waits = [
            (high_x, remote(layers, layers, x_send.at[0], x_recv.at[0, 0, 0], "gx", up(mx, nx))),
            (low_x, remote(layers, layers, x_send.at[1], x_recv.at[0, 0, 1], "gx", down(mx, nx))),
            (None, remote(z_out, z_out, z_send.at[0], z_recv.at[0, 0, 0], "gz", up(mz, nz))),
            (None, remote(z_out, z_out, z_send.at[1], z_recv.at[0, 0, 1], "gz", down(mz, nz))),
        ]
        half = y_out.at[:, :, 0]
        if ny == 2:
            waits.append((None, remote(half, half, y_send.at[0], y_recv.at[0, 0, 0], "gy", 1 - my)))
        else:
            waits += [
                (high_y, remote(half, half, y_send.at[0], y_recv.at[0, 0, 0], "gy", up(my, ny))),
                (low_y, remote(half, half, y_send.at[1], y_recv.at[0, 0, 1], "gy", down(my, ny))),
            ]
        for condition, copy in waits:
            guarded(condition, copy.wait_send)

    lane = lax.broadcasted_iota(jnp.int32, (8, 128), 1)
    quarter = lax.shift_right_logical(lane, 2)
    lower = jnp.bitwise_and(lane, 3) < 2
    inside = jnp.where(lower, jnp.minimum(mz, 1), jnp.minimum(nz - 1 - mz, 1)) > 0
    groups = (p.edge, p.inner)

    def pack(s, group, v, layers):
        z = jnp.zeros((8, 128), jnp.float32)
        for j, value in enumerate(layers):
            y_out[s, group, 0, v, 2 * j:2 * j + 2] = value[0:2]
            y_out[s, group, 1, v, 2 * j:2 * j + 2] = value[ly - 2:ly]
            for t in range(p.tiles):
                place = 4 * (j * p.tiles + t)
                turned = pltpu.roll(value[8 * t:8 * t + 8], (place + 2) % 128, 1)
                z = jnp.where(quarter == j * p.tiles + t, turned, z)
        z_out[s, group, v] = z

    def advance(s, group, v):
        edges = jnp.where(lower, z_in[s, group, 0, v], z_in[s, group, 1, v])
        edges = jnp.where(inside, edges, 0.0)
        spread = time_step * diffusivity[v]
        rates = [time_step * coupling[v, w] for w in range(nv)]
        keep = 1.0 - 6.0 * spread
        layers = groups[group]
        for j, x in enumerate(layers):
            cells[s, v, x + 2, PAD - 2:PAD] = y_in[s, group, 0, v, 2 * j:2 * j + 2]
            cells[s, v, x + 2, PAD + ly:PAD + ly + 2] = y_in[s, group, 1, v, 2 * j:2 * j + 2]
        result = []
        for j, x in enumerate(layers):
            centre = cells[s, v, x + 2, rows]
            turned = [[], [], [], []]
            for t in range(p.tiles):
                tile = centre[8 * t:8 * t + 8]
                beside = pltpu.roll(edges, (126 - 4 * (j * p.tiles + t)) % 128, 1)
                for i, (mask, shift) in enumerate(
                        ((lane == 0, 127), (lane == 127, 1), (lane <= 1, 126), (lane >= 126, 2))):
                    turned[i].append(pltpu.roll(jnp.where(mask, beside, tile), shift, 1))
            near = [
                (cells[s, v, x + 3, rows], cells[s, v, x + 1, rows],
                 cells[s, v, x + 4, rows], cells[s, v, x, rows]),
                (cells[s, v, x + 2, PAD + 1:PAD + 1 + ly], cells[s, v, x + 2, PAD - 1:PAD - 1 + ly],
                 cells[s, v, x + 2, PAD + 2:PAD + 2 + ly], cells[s, v, x + 2, PAD - 2:PAD - 2 + ly]),
                tuple(jnp.concatenate(parts, axis=0) for parts in turned),
            ]
            moved = around = None
            for a, (next1, last1, next2, last2) in enumerate(near):
                flow = speed[a, x] * (8.0 * (next1 - last1) - (next2 - last2))
                both = next1 + last1
                moved = flow if moved is None else moved + flow
                around = both if around is None else around + both
            factor = keep
            for w in range(nv):
                factor = factor + rates[w] * cells[s, w, x + 2, rows]
            new = centre * factor + moved + spread * around
            if s % 2 == 1:
                new = 0.5 * (new + cells[s - 1, v, x + 2, rows])
            cells[s + 1, v, x + 2, rows] = new
            result.append(new)
        return result

    def clear(condition, ref, *index):
        @pl.when(jnp.logical_not(condition))
        def _():
            ref[index] = jnp.zeros_like(ref[index])

    for s in range(STAGES):
        clear(low_x, cells, s, slice(None), slice(0, 2))
        clear(high_x, cells, s, slice(None), slice(lx + 2, lx + 4))
        for group in range(2):
            for side, condition in ((0, low_y), (1, high_y)):
                clear(condition, y_in, s, group, side)

    load = pltpu.make_async_copy(fields, cells.at[0, :, 2:lx + 2, rows], load_sem.at[0])
    load.start()
    load_speed = pltpu.make_async_copy(velocity, speed, load_sem.at[1])
    load_speed.start()

    partners = [
        {"gy": lax.rem(my + dy, ny), "gz": lax.rem(mz + dz, nz)}
        for dy in range(ny) for dz in range(nz) if dy or dz
    ]
    line = [{"gx": lax.rem(mx + dx, nx)} for dx in range(1, nx)]
    barrier = pltpu.get_barrier_semaphore()
    for device in partners + line:
        pl.semaphore_signal(barrier, inc=1, device_id=device, device_id_type=MESH)
    pl.semaphore_wait(barrier, len(partners) + len(line))

    for v in range(nv):
        start(x_messages(0, v))
    load.wait()

    def first_pack(c, carry):
        for v in (c * PAIR + i for i in range(PAIR)):
            for group in range(2):
                pack(0, group, v, [cells[0, v, x + 2, rows] for x in groups[group]])
        start(yz_messages(0, 0, c))
        return carry

    lax.fori_loop(0, chunks, first_pack, 0)
    start(yz_messages(0, 1, None))
    load_speed.wait()
    speed[...] = speed[...] * (-time_step / 12.0)

    def split(value):
        high = value.astype(jnp.bfloat16)
        return high, (value - high.astype(jnp.float32)).astype(jnp.bfloat16)

    def product(a, b, contract=((1,), (0,))):
        (a_high, a_low), (b_high, b_low) = a, b
        dot = functools.partial(
            lax.dot_general, dimension_numbers=(contract, ((), ())), preferred_element_type=jnp.float32)
        return dot(a_high, b_high) + (dot(a_high, b_low) + dot(a_low, b_high))

    chunk_y = lx * p.by
    wide_y = ny * chunk_y
    column = lax.broadcasted_iota(jnp.int32, (p.rank, wide_y), 1)
    row = lax.broadcasted_iota(jnp.int32, (p.rank, wide_y), 0)
    place_y = jnp.where(row == column // chunk_y * p.by + column % p.by, 1.0, 0.0)
    repeated = jnp.dot(factor_y[...], place_y, precision=HIGHEST, preferred_element_type=jnp.float32)
    column = lax.broadcasted_iota(jnp.int32, (ly, wide_y), 1) % chunk_y // p.by
    for x in range(lx):
        for i, part in enumerate(split(jnp.where(column == x, repeated, 0.0))):
            spread_y[i, x * ly:(x + 1) * ly] = part
    chunk_x = p.ax * p.by
    wide_x = nx * chunk_x
    column = lax.broadcasted_iota(jnp.int32, (p.rank, wide_x), 1)
    row = lax.broadcasted_iota(jnp.int32, (p.rank, wide_x), 0)
    place_x = jnp.where(row == column // p.by, 1.0, 0.0)
    repeated = jnp.dot(factor_x[...], place_x, precision=HIGHEST, preferred_element_type=jnp.float32)
    column = lax.broadcasted_iota(jnp.int32, (p.by, wide_x), 1) % p.by
    row = lax.broadcasted_iota(jnp.int32, (p.by, wide_x), 0)
    for x in range(lx):
        for i, part in enumerate(split(jnp.where(column == row, repeated[x:x + 1], 0.0))):
            spread_x[i, x * p.by:(x + 1) * p.by] = part

    for s in range(STAGES):
        last = s == STAGES - 1

        def project(v):
            state = cells[STAGES, v, 2:lx + 2, rows].reshape(lx * ly, p.lz)
            reduced = product(split(factor_z[...]), split(state), ((1,), (1,)))
            reduced = product(split(reduced), (spread_y[0], spread_y[1]))
            for y in range(ny):
                for z in range(nz):
                    yz_out[y * nz + z, v] = reduced[
                        z * p.cz:(z + 1) * p.cz, y * chunk_y:(y + 1) * chunk_y]

        def edge_part(c, carry):
            for i in range(PAIR):
                v = c * PAIR + i
                if i == 0:
                    arrive(yz_messages(s, 0, c))
                arrive(x_messages(s, v))
                layers = advance(s, 0, v)
                if last:
                    project(v)
                else:
                    start(x_messages(s + 1, v))
                    pack(s + 1, 0, v, layers)
            if not last:
                start(yz_messages(s + 1, 0, c))
            return carry

        def inner_part(v, carry):
            layers = advance(s, 1, v)
            if not last:
                pack(s + 1, 1, v, layers)
            return carry

        if not last:
            lax.fori_loop(0, chunks, edge_part, 0)
        arrive(yz_messages(s, 1, None))
        lax.fori_loop(0, nv, inner_part, 0)
        if not last:
            start(yz_messages(s + 1, 1, None))
        else:
            lax.fori_loop(0, chunks, edge_part, 0)

    plane = []
    for i, device in enumerate(partners):
        plane.append(pltpu.make_async_remote_copy(
            src_ref=yz_out.at[device["gy"] * nz + device["gz"]], dst_ref=yz_in.at[i],
            send_sem=yz_send.at[i], recv_sem=yz_recv.at[i],
            device_id=device, device_id_type=MESH))
        plane[-1].start()
    total = yz_out[my * nz + mz]
    for i, copy in enumerate(plane):
        copy.wait_recv()
        total = total + yz_in[i]

    total = total.reshape(nv * p.cz, chunk_y)
    total = product(split(total), (spread_x[0], spread_x[1]))
    for x in range(nx):
        x_out[x] = total[:, x * chunk_x:(x + 1) * chunk_x].reshape(nv, p.cz, chunk_x)
    along = []
    for i, device in enumerate(line):
        along.append(pltpu.make_async_remote_copy(
            src_ref=x_out.at[device["gx"]], dst_ref=x_in.at[i],
            send_sem=xs_send.at[i], recv_sem=xs_recv.at[i],
            device_id=device, device_id_type=MESH))
        along[-1].start()
    total = x_out[mx]
    for i, copy in enumerate(along):
        copy.wait_recv()
        total = total + x_in[i]
    out[...] = total

    all_sent()
    for copy in plane + along:
        copy.wait_send()


def local_kernel(plan, fields, velocity, diffusivity, coupling, factor_x, factor_y, factor_z):
    p = plan
    nv, lx, ly = p.vars, p.lx, p.ly
    chunk_y, chunk_x = lx * p.by, p.ax * p.by
    others = p.ny * p.nz - 1
    vmem = lambda *shape: pltpu.VMEM(shape, jnp.float32)
    dma = lambda *shape: pltpu.SemaphoreType.DMA(shape)
    whole = pl.BlockSpec(memory_space=pltpu.VMEM)
    scalars = pl.BlockSpec(memory_space=pltpu.SMEM)
    result = pl.pallas_call(
        functools.partial(kernel, p),
        out_shape=jax.ShapeDtypeStruct((nv, p.cz, chunk_x), jnp.float32),
        in_specs=[pl.BlockSpec(memory_space=pltpu.HBM)] * 2 + [scalars] * 2 + [whole] * 3,
        out_specs=whole,
        scratch_shapes=[
            vmem(STAGES + 1, nv, lx + 4, ly + 2 * PAD, p.lz),
            vmem(3, lx, ly, p.lz),
            vmem(STAGES, 2, 2, nv, 8 * -(-max(4, lx - 4) // 4), p.lz),
            vmem(STAGES, 2, 2, nv, 8 * -(-max(4, lx - 4) // 4), p.lz),
            vmem(STAGES, 2, nv, 8, 128),
            vmem(STAGES, 2, 2, nv, 8, 128),
            pltpu.VMEM((2, lx * ly, p.ny * chunk_y), jnp.bfloat16),
            pltpu.VMEM((2, chunk_y, p.nx * chunk_x), jnp.bfloat16),
            vmem(p.ny * p.nz, nv, p.cz, chunk_y),
            vmem(others, nv, p.cz, chunk_y),
            vmem(p.nx, nv, p.cz, chunk_x),
            vmem(p.nx - 1, nv, p.cz, chunk_x),
            dma(2),
            dma(2), dma(STAGES, nv, 2),
            dma(2), dma(STAGES, nv // PAIR + 1, 2),
            dma(2), dma(STAGES, nv // PAIR + 1, 2),
            dma(others), dma(others),
            dma(p.nx - 1), dma(p.nx - 1),
        ],
        compiler_params=pltpu.CompilerParams(
            collective_id=0, has_side_effects=True, vmem_limit_bytes=40 * 1024 * 1024),
    )(fields, velocity, diffusivity, coupling, factor_x, factor_y, factor_z.T)
    result = result.reshape(nv, p.cz, p.ax, p.by)
    return jnp.transpose(result, (0, 2, 3, 1))


def solution(mesh):
    def local(fields, velocity, diffusivity, coupling, factor_x, factor_y, factor_z):
        plan = Plan(mesh.shape, fields.shape, factor_x.shape)
        run = functools.partial(local_kernel, plan) if plan.fits() else local_plain
        return run(fields, velocity, diffusivity, coupling, factor_x, factor_y, factor_z)

    return jax.shard_map(
        local,
        mesh=mesh,
        in_specs=(
            P(None, "gx", "gy", "gz"),
            P(None, "gx", "gy", "gz"),
            P(),
            P(),
            P("gx", None),
            P("gy", None),
            P("gz", None),
        ),
        out_specs=P(None, "gx", "gy", "gz"),
        check_vma=False,
    )
```

```python
import functools
import jax
import jax.numpy as jnp
from jax import lax
from jax.experimental import pallas as pl
from jax.experimental.pallas import tpu as pltpu
from jax.sharding import PartitionSpec as P

STEPS = 2
STAGES = 2 * STEPS
HALO = 2
VMEM_LIMIT = 66 * 1000 * 1000
PAIR = 2
PAD = 8
MESH = pl.DeviceIdType.MESH
HIGHEST = lax.Precision.HIGHEST


time_step = 0.2
def with_halo(cells, sides, width):
    for axis, dim in sides:
        count = lax.axis_size(axis)
        ends = count - 1
        head = lax.slice_in_dim(cells, 0, width, axis=dim)
        tail = lax.slice_in_dim(cells, cells.shape[dim] - width, cells.shape[dim], axis=dim)
        cells = jnp.concatenate(
            [
                lax.ppermute(tail, axis, [(i, (i + 1) % count) for i in range(ends)]),
                cells,
                lax.ppermute(head, axis, [((i + 1) % count, i) for i in range(ends)]),
            ],
            axis=dim,
        )
    return cells


def offset_view(padded, dimension, offset):
    indices = [slice(None)]
    for other in (1, 2, 3):
        if other == dimension:
            first_cell = 2 + offset
            indices.append(slice(first_cell, first_cell + padded.shape[other] - 4))
        else:
            indices.append(slice(2, padded.shape[other] - 2))
    return padded[tuple(indices)]


def tendency(padded, velocity, diffusivity, coupling):
    center = offset_view(padded, 1, 0)
    transport = jnp.zeros_like(center)
    laplace = jnp.zeros_like(center)
    for dimension in (1, 2, 3):
        gradient = (
            8.0 * (offset_view(padded, dimension, 1) - offset_view(padded, dimension, -1))
            - (offset_view(padded, dimension, 2) - offset_view(padded, dimension, -2))
        ) / 12.0
        transport = transport + velocity[dimension - 1][None] * gradient
        laplace = (
            laplace
            + offset_view(padded, dimension, 1)
            + offset_view(padded, dimension, -1)
            - 2.0 * center
        )
    mixing = jnp.einsum("vw,wxyz->vxyz", coupling, center, precision=lax.Precision.HIGHEST)
    return -transport + diffusivity[:, None, None, None] * laplace + center * mixing


def with_edges(values):
    return with_halo(values, (("gx", 1), ("gy", 2), ("gz", 3)), 2)


def local_plain(fields, velocity, diffusivity, coupling, factor_x, factor_y, factor_z):
    state = fields
    for repeat in range(STEPS):
        section = state + time_step * tendency(with_edges(state), velocity, diffusivity, coupling)
        state = 0.5 * (
            state
            + section
            + time_step * tendency(with_edges(section), velocity, diffusivity, coupling)
        )
    highest = lax.Precision.HIGHEST
    partial_value = jnp.einsum("vxyz,zc->vxyc", state, factor_z, precision=highest)
    partial_value = lax.psum_scatter(partial_value, "gz", scatter_dimension=3, tiled=True)
    partial_value = jnp.einsum("vxyc,yb->vxbc", partial_value, factor_y, precision=highest)
    partial_value = lax.psum_scatter(partial_value, "gy", scatter_dimension=2, tiled=True)
    partial_value = jnp.einsum("vxbc,xa->vabc", partial_value, factor_x, precision=highest)
    core_tensor = lax.psum_scatter(partial_value, "gx", scatter_dimension=1, tiled=True)
    return core_tensor


class Plan:
    def __init__(self, mesh_shape, fields, factor_x):
        self.nx, self.ny, self.nz = (mesh_shape[a] for a in ("gx", "gy", "gz"))
        self.vars, self.lx, self.ly, self.lz = fields
        self.rank = factor_x[1]
        self.ax, self.by, self.cz = self.rank // self.nx, self.rank // self.ny, self.rank // self.nz
        self.edge = [0, 1, self.lx - 2, self.lx - 1]
        self.inner = list(range(2, self.lx - 2))
        self.tiles = self.ly // 8

    def fits(self):
        return (
            self.lz == 128
            and self.ly % 8 == 0
            and min(self.nx, self.ny, self.nz) > 1
            and self.vars % PAIR == 0
            and self.lx > 4
            and self.lx <= 12
            and len(self.edge) * self.tiles * 4 <= 128
            and len(self.inner) * self.tiles * 4 <= 128
            and self.rank % self.nx == 0 and self.rank % self.ny == 0 and self.rank % self.nz == 0
            and self.cz % 8 == 0
            and self.lx * self.by % 128 == 0
            and self.ax * self.by % 128 == 0
        )


def kernel(
    plan,
    fields,
    velocity,
    diffusivity_in,
    coupling_in,
    factor_x_in,
    factor_y_in,
    factor_z_in,
    out,
    diffusivity,
    coupling,
    factor_x,
    factor_y,
    factor_z,
    cells,
    speed,
    y_out,
    y_in,
    z_out,
    z_in,
    spread_y,
    spread_x,
    yz_out,
    yz_in,
    x_out,
    x_in,
    load_sem,
    x_send,
    x_recv,
    y_send,
    y_recv,
    z_send,
    z_recv,
    yz_send,
    yz_recv,
    xs_send,
    xs_recv,
):
    p = plan
    nx, ny, nz = p.nx, p.ny, p.nz
    lx, ly, nv = p.lx, p.ly, p.vars
    mx, my, mz = lax.axis_index("gx"), lax.axis_index("gy"), lax.axis_index("gz")
    rows = slice(PAD, PAD + ly)
    low_x, high_x = mx > 0, mx < nx - 1
    low_y, high_y = my > 0, my < ny - 1
    low_z, high_z = mz > 0, mz < nz - 1

    def remote(src, dst, send, recv, axis, to):
        return pltpu.make_async_remote_copy(
            src_ref=src, dst_ref=dst, send_sem=send, recv_sem=recv,
            device_id={axis: to}, device_id_type=MESH,
        )

    def up(index, count):
        return lax.rem(index + 1, count)

    def down(index, count):
        return lax.rem(index + count - 1, count)

    def x_messages(s, v):
        if s == 0:
            top, bottom = fields.at[v, lx - 2:lx], fields.at[v, 0:2]
        else:
            top = cells.at[s, v, lx:lx + 2, rows]
            bottom = cells.at[s, v, 2:4, rows]
        return [
            (high_x, low_x, remote(
                top, cells.at[s, v, 0:2, rows],
                x_send.at[0], x_recv.at[s, v, 0], "gx", up(mx, nx))),
            (low_x, high_x, remote(
                bottom, cells.at[s, v, lx + 2:lx + 4, rows],
                x_send.at[1], x_recv.at[s, v, 1], "gx", down(mx, nx))),
        ]

    chunks = nv // PAIR

    def yz_messages(s, group, c):
        if group == 0:
            which, place = pl.ds(c * PAIR, PAIR), c
        else:
            which, place = slice(None), chunks
        result = [
            (None, None, remote(
                z_out.at[s, group, which], z_in.at[s, group, 0, which],
                z_send.at[0], z_recv.at[s, place, 0], "gz", up(mz, nz))),
            (None, None, remote(
                z_out.at[s, group, which], z_in.at[s, group, 1, which],
                z_send.at[1], z_recv.at[s, place, 1], "gz", down(mz, nz))),
        ]
        if ny == 2:
            result.append((None, None, remote(
                y_out.at[s, group, 1 - my, which], y_in.at[s, group, my, which],
                y_send.at[0], y_recv.at[s, place, 0], "gy", 1 - my)))
        else:
            result += [
                (high_y, low_y, remote(
                    y_out.at[s, group, 1, which], y_in.at[s, group, 0, which],
                    y_send.at[0], y_recv.at[s, place, 0], "gy", up(my, ny))),
                (low_y, high_y, remote(
                    y_out.at[s, group, 0, which], y_in.at[s, group, 1, which],
                    y_send.at[1], y_recv.at[s, place, 1], "gy", down(my, ny))),
            ]
        return result

    def guarded(condition, action):
        if condition is None:
            action()
        else:
            pl.when(condition)(action)

    def start(messages):
        for sends, _, copy in messages:
            guarded(sends, copy.start)

    def arrive(messages):
        for _, gets, copy in messages:
            guarded(gets, copy.wait_recv)

    def all_sent():
        layers = cells.at[0:STAGES, :, 0:2, rows]
        waits = [
            (high_x, remote(layers, layers, x_send.at[0], x_recv.at[0, 0, 0], "gx", up(mx, nx))),
            (low_x, remote(layers, layers, x_send.at[1], x_recv.at[0, 0, 1], "gx", down(mx, nx))),
            (None, remote(z_out, z_out, z_send.at[0], z_recv.at[0, 0, 0], "gz", up(mz, nz))),
            (None, remote(z_out, z_out, z_send.at[1], z_recv.at[0, 0, 1], "gz", down(mz, nz))),
        ]
        half = y_out.at[:, :, 0]
        if ny == 2:
            waits.append((None, remote(half, half, y_send.at[0], y_recv.at[0, 0, 0], "gy", 1 - my)))
        else:
            waits += [
                (high_y, remote(half, half, y_send.at[0], y_recv.at[0, 0, 0], "gy", up(my, ny))),
                (low_y, remote(half, half, y_send.at[1], y_recv.at[0, 0, 1], "gy", down(my, ny))),
            ]
        for condition, copy in waits:
            guarded(condition, copy.wait_send)

    lane = lax.broadcasted_iota(jnp.int32, (8, 128), 1)
    quarter = lax.shift_right_logical(lane, 2)
    lower = jnp.bitwise_and(lane, 3) < 2
    inside = jnp.where(lower, jnp.minimum(mz, 1), jnp.minimum(nz - 1 - mz, 1)) > 0
    groups = (p.edge, p.inner)

    def pack(s, group, v, layers):
        z = jnp.zeros((8, 128), jnp.float32)
        for j, value in enumerate(layers):
            y_out[s, group, 0, v, 2 * j:2 * j + 2] = value[0:2]
            y_out[s, group, 1, v, 2 * j:2 * j + 2] = value[ly - 2:ly]
            for t in range(p.tiles):
                place = 4 * (j * p.tiles + t)
                turned = pltpu.roll(value[8 * t:8 * t + 8], (place + 2) % 128, 1)
                z = jnp.where(quarter == j * p.tiles + t, turned, z)
        z_out[s, group, v] = z

    def advance(s, group, v):
        edges = jnp.where(lower, z_in[s, group, 0, v], z_in[s, group, 1, v])
        edges = jnp.where(inside, edges, 0.0)
        spread = time_step * diffusivity[v]
        rates = [time_step * coupling[v, w] for w in range(nv)]
        keep = 1.0 - 6.0 * spread
        layers = groups[group]
        for j, x in enumerate(layers):
            cells[s, v, x + 2, PAD - 2:PAD] = y_in[s, group, 0, v, 2 * j:2 * j + 2]
            cells[s, v, x + 2, PAD + ly:PAD + ly + 2] = y_in[s, group, 1, v, 2 * j:2 * j + 2]
        result = []
        for j, x in enumerate(layers):
            centre = cells[s, v, x + 2, rows]
            turned = [[], [], [], []]
            for t in range(p.tiles):
                tile = centre[8 * t:8 * t + 8]
                beside = pltpu.roll(edges, (126 - 4 * (j * p.tiles + t)) % 128, 1)
                for i, (mask, shift) in enumerate(
                        ((lane == 0, 127), (lane == 127, 1), (lane <= 1, 126), (lane >= 126, 2))):
                    turned[i].append(pltpu.roll(jnp.where(mask, beside, tile), shift, 1))
            near = [
                (cells[s, v, x + 3, rows], cells[s, v, x + 1, rows],
                 cells[s, v, x + 4, rows], cells[s, v, x, rows]),
                (cells[s, v, x + 2, PAD + 1:PAD + 1 + ly], cells[s, v, x + 2, PAD - 1:PAD - 1 + ly],
                 cells[s, v, x + 2, PAD + 2:PAD + 2 + ly], cells[s, v, x + 2, PAD - 2:PAD - 2 + ly]),
                tuple(jnp.concatenate(parts, axis=0) for parts in turned),
            ]
            moved = around = None
            for a, (next1, last1, next2, last2) in enumerate(near):
                flow = speed[a, x] * (8.0 * (next1 - last1) - (next2 - last2))
                both = next1 + last1
                moved = flow if moved is None else moved + flow
                around = both if around is None else around + both
            factor = keep
            for w in range(nv):
                factor = factor + rates[w] * cells[s, w, x + 2, rows]
            new = centre * factor + moved + spread * around
            if s % 2 == 1:
                new = 0.5 * (new + cells[s - 1, v, x + 2, rows])
            cells[s + 1, v, x + 2, rows] = new
            result.append(new)
        return result

    def fetch(i, source, target):
        copy = pltpu.make_async_copy(source, target, load_sem.at[i])
        copy.start()
        return copy

    partners = [
        {"gy": lax.rem(my + dy, ny), "gz": lax.rem(mz + dz, nz)}
        for dy in range(ny) for dz in range(nz) if dy or dz
    ]
    line = [{"gx": lax.rem(mx + dx, nx)} for dx in range(1, nx)]
    barrier = pltpu.get_barrier_semaphore()
    for device in partners + line:
        pl.semaphore_signal(barrier, inc=1, device_id=device, device_id_type=MESH)
    load = fetch(0, fields, cells.at[0, :, 2:lx + 2, rows])
    load_rest = [
        fetch(1, velocity, speed),
        fetch(2, diffusivity_in, diffusivity),
        fetch(3, coupling_in, coupling),
        fetch(4, factor_x_in, factor_x),
        fetch(5, factor_y_in, factor_y),
        fetch(6, factor_z_in, factor_z),
    ]

    def clear(condition, ref, *index):
        @pl.when(jnp.logical_not(condition))
        def _():
            ref[index] = jnp.zeros_like(ref[index])

    for s in range(STAGES):
        clear(low_x, cells, s, slice(None), slice(0, 2))
        clear(high_x, cells, s, slice(None), slice(lx + 2, lx + 4))
        for group in range(2):
            for side, condition in ((0, low_y), (1, high_y)):
                clear(condition, y_in, s, group, side)

    pl.semaphore_wait(barrier, len(partners) + len(line))

    for v in range(nv):
        start(x_messages(0, v))
    load.wait()

    def first_pack(c, carry):
        for v in (c * PAIR + i for i in range(PAIR)):
            for group in range(2):
                pack(0, group, v, [cells[0, v, x + 2, rows] for x in groups[group]])
        start(yz_messages(0, 0, c))
        return carry

    lax.fori_loop(0, chunks, first_pack, 0)
    start(yz_messages(0, 1, None))
    for copy in load_rest:
        copy.wait()
    speed[...] = speed[...] * (-time_step / 12.0)

    def split(value):
        high = value.astype(jnp.bfloat16)
        return high, (value - high.astype(jnp.float32)).astype(jnp.bfloat16)

    def product(a, b, contract=((1,), (0,))):
        (a_high, a_low), (b_high, b_low) = a, b
        dot = functools.partial(
            lax.dot_general, dimension_numbers=(contract, ((), ())), preferred_element_type=jnp.float32)
        return dot(a_high, b_high) + (dot(a_high, b_low) + dot(a_low, b_high))

    chunk_y = lx * p.by
    wide_y = ny * chunk_y
    column = lax.broadcasted_iota(jnp.int32, (p.rank, wide_y), 1)
    row = lax.broadcasted_iota(jnp.int32, (p.rank, wide_y), 0)
    place_y = jnp.where(row == column // chunk_y * p.by + column % p.by, 1.0, 0.0)
    repeated = jnp.dot(factor_y[...], place_y, precision=HIGHEST, preferred_element_type=jnp.float32)
    column = lax.broadcasted_iota(jnp.int32, (ly, wide_y), 1) % chunk_y // p.by
    for x in range(lx):
        for i, part in enumerate(split(jnp.where(column == x, repeated, 0.0))):
            spread_y[i, x * ly:(x + 1) * ly] = part
    chunk_x = p.ax * p.by
    wide_x = nx * chunk_x
    column = lax.broadcasted_iota(jnp.int32, (p.rank, wide_x), 1)
    row = lax.broadcasted_iota(jnp.int32, (p.rank, wide_x), 0)
    place_x = jnp.where(row == column // p.by, 1.0, 0.0)
    repeated = jnp.dot(factor_x[...], place_x, precision=HIGHEST, preferred_element_type=jnp.float32)
    column = lax.broadcasted_iota(jnp.int32, (p.by, wide_x), 1) % p.by
    row = lax.broadcasted_iota(jnp.int32, (p.by, wide_x), 0)
    for x in range(lx):
        for i, part in enumerate(split(jnp.where(column == row, repeated[x:x + 1], 0.0))):
            spread_x[i, x * p.by:(x + 1) * p.by] = part

    for s in range(STAGES):
        last = s == STAGES - 1

        def project(v):
            state = cells[STAGES, v, 2:lx + 2, rows].reshape(lx * ly, p.lz)
            reduced = product(split(factor_z[...]), split(state), ((1,), (1,)))
            reduced = product(split(reduced), (spread_y[0], spread_y[1]))
            for y in range(ny):
                for z in range(nz):
                    yz_out[y * nz + z, v] = reduced[
                        z * p.cz:(z + 1) * p.cz, y * chunk_y:(y + 1) * chunk_y]

        def edge_part(c, carry):
            for i in range(PAIR):
                v = c * PAIR + i
                if i == 0:
                    arrive(yz_messages(s, 0, c))
                arrive(x_messages(s, v))
                layers = advance(s, 0, v)
                if last:
                    project(v)
                else:
                    start(x_messages(s + 1, v))
                    pack(s + 1, 0, v, layers)
            if not last:
                start(yz_messages(s + 1, 0, c))
            return carry

        def inner_part(v, carry):
            layers = advance(s, 1, v)
            if not last:
                pack(s + 1, 1, v, layers)
            return carry

        if not last:
            lax.fori_loop(0, chunks, edge_part, 0)
        arrive(yz_messages(s, 1, None))
        lax.fori_loop(0, nv, inner_part, 0)
        if not last:
            start(yz_messages(s + 1, 1, None))
        else:
            lax.fori_loop(0, chunks, edge_part, 0)

    plane = []
    for i, device in enumerate(partners):
        plane.append(pltpu.make_async_remote_copy(
            src_ref=yz_out.at[device["gy"] * nz + device["gz"]], dst_ref=yz_in.at[i],
            send_sem=yz_send.at[i], recv_sem=yz_recv.at[i],
            device_id=device, device_id_type=MESH))
        plane[-1].start()
    total = yz_out[my * nz + mz]
    for i, copy in enumerate(plane):
        copy.wait_recv()
        total = total + yz_in[i]

    total = total.reshape(nv * p.cz, chunk_y)
    total = product(split(total), (spread_x[0], spread_x[1]))
    for x in range(nx):
        x_out[x] = total[:, x * chunk_x:(x + 1) * chunk_x].reshape(nv, p.cz, chunk_x)
    along = []
    for i, device in enumerate(line):
        along.append(pltpu.make_async_remote_copy(
            src_ref=x_out.at[device["gx"]], dst_ref=x_in.at[i],
            send_sem=xs_send.at[i], recv_sem=xs_recv.at[i],
            device_id=device, device_id_type=MESH))
        along[-1].start()
    total = x_out[mx]
    for i, copy in enumerate(along):
        copy.wait_recv()
        total = total + x_in[i]
    out[...] = total

    all_sent()
    for copy in plane + along:
        copy.wait_send()


def local_kernel(plan, fields, velocity, diffusivity, coupling, factor_x, factor_y, factor_z):
    p = plan
    nv, lx, ly = p.vars, p.lx, p.ly
    chunk_y, chunk_x = lx * p.by, p.ax * p.by
    others = p.ny * p.nz - 1
    vmem = lambda *shape: pltpu.VMEM(shape, jnp.float32)
    dma = lambda *shape: pltpu.SemaphoreType.DMA(shape)
    whole = pl.BlockSpec(memory_space=pltpu.VMEM)
    result = pl.pallas_call(
        functools.partial(kernel, p),
        out_shape=jax.ShapeDtypeStruct((nv, p.cz, chunk_x), jnp.float32),
        in_specs=[pl.BlockSpec(memory_space=pl.ANY)] * 7,
        out_specs=whole,
        scratch_shapes=[
            pltpu.SMEM(diffusivity.shape, jnp.float32),
            pltpu.SMEM(coupling.shape, jnp.float32),
            vmem(*factor_x.shape),
            vmem(*factor_y.shape),
            vmem(*factor_z.shape[::-1]),
            vmem(STAGES + 1, nv, lx + 4, ly + 2 * PAD, p.lz),
            vmem(3, lx, ly, p.lz),
            vmem(STAGES, 2, 2, nv, 8 * -(-max(4, lx - 4) // 4), p.lz),
            vmem(STAGES, 2, 2, nv, 8 * -(-max(4, lx - 4) // 4), p.lz),
            vmem(STAGES, 2, nv, 8, 128),
            vmem(STAGES, 2, 2, nv, 8, 128),
            pltpu.VMEM((2, lx * ly, p.ny * chunk_y), jnp.bfloat16),
            pltpu.VMEM((2, chunk_y, p.nx * chunk_x), jnp.bfloat16),
            vmem(p.ny * p.nz, nv, p.cz, chunk_y),
            vmem(others, nv, p.cz, chunk_y),
            vmem(p.nx, nv, p.cz, chunk_x),
            vmem(p.nx - 1, nv, p.cz, chunk_x),
            dma(7),
            dma(2), dma(STAGES, nv, 2),
            dma(2), dma(STAGES, nv // PAIR + 1, 2),
            dma(2), dma(STAGES, nv // PAIR + 1, 2),
            dma(others), dma(others),
            dma(p.nx - 1), dma(p.nx - 1),
        ],
        compiler_params=pltpu.CompilerParams(
            collective_id=0, has_side_effects=True, vmem_limit_bytes=VMEM_LIMIT),
    )(fields, velocity, diffusivity, coupling, factor_x, factor_y, factor_z.T)
    result = result.reshape(nv, p.cz, p.ax, p.by)
    return jnp.transpose(result, (0, 2, 3, 1))


def solution(mesh):
    def local(fields, velocity, diffusivity, coupling, factor_x, factor_y, factor_z):
        plan = Plan(mesh.shape, fields.shape, factor_x.shape)
        run = functools.partial(local_kernel, plan) if plan.fits() else local_plain
        return run(fields, velocity, diffusivity, coupling, factor_x, factor_y, factor_z)

    return jax.shard_map(
        local,
        mesh=mesh,
        in_specs=(
            P(None, "gx", "gy", "gz"),
            P(None, "gx", "gy", "gz"),
            P(),
            P(),
            P("gx", None),
            P("gy", None),
            P("gz", None),
        ),
        out_specs=P(None, "gx", "gy", "gz"),
        check_vma=False,
    )
```

```python
import functools
import jax
import jax.numpy as jnp
from jax import lax
from jax.experimental import pallas as pl
from jax.experimental.pallas import tpu as pltpu
from jax.sharding import PartitionSpec as P

STEPS = 2
STAGES = 2 * STEPS
HALO = 2
VMEM_LIMIT = 66 * 1000 * 1000
PAD = 8
MESH = pl.DeviceIdType.MESH
HIGHEST = lax.Precision.HIGHEST


time_step = 0.2
def with_halo(cells, sides, width):
    for axis, dim in sides:
        count = lax.axis_size(axis)
        ends = count - 1
        head = lax.slice_in_dim(cells, 0, width, axis=dim)
        tail = lax.slice_in_dim(cells, cells.shape[dim] - width, cells.shape[dim], axis=dim)
        cells = jnp.concatenate(
            [
                lax.ppermute(tail, axis, [(i, (i + 1) % count) for i in range(ends)]),
                cells,
                lax.ppermute(head, axis, [((i + 1) % count, i) for i in range(ends)]),
            ],
            axis=dim,
        )
    return cells


def offset_view(padded, dimension, offset):
    indices = [slice(None)]
    for other in (1, 2, 3):
        if other == dimension:
            first_cell = 2 + offset
            indices.append(slice(first_cell, first_cell + padded.shape[other] - 4))
        else:
            indices.append(slice(2, padded.shape[other] - 2))
    return padded[tuple(indices)]


def tendency(padded, velocity, diffusivity, coupling):
    center = offset_view(padded, 1, 0)
    transport = jnp.zeros_like(center)
    laplace = jnp.zeros_like(center)
    for dimension in (1, 2, 3):
        gradient = (
            8.0 * (offset_view(padded, dimension, 1) - offset_view(padded, dimension, -1))
            - (offset_view(padded, dimension, 2) - offset_view(padded, dimension, -2))
        ) / 12.0
        transport = transport + velocity[dimension - 1][None] * gradient
        laplace = (
            laplace
            + offset_view(padded, dimension, 1)
            + offset_view(padded, dimension, -1)
            - 2.0 * center
        )
    mixing = jnp.einsum("vw,wxyz->vxyz", coupling, center, precision=lax.Precision.HIGHEST)
    return -transport + diffusivity[:, None, None, None] * laplace + center * mixing


def with_edges(values):
    return with_halo(values, (("gx", 1), ("gy", 2), ("gz", 3)), 2)


def local_plain(fields, velocity, diffusivity, coupling, factor_x, factor_y, factor_z):
    state = fields
    for repeat in range(STEPS):
        section = state + time_step * tendency(with_edges(state), velocity, diffusivity, coupling)
        state = 0.5 * (
            state
            + section
            + time_step * tendency(with_edges(section), velocity, diffusivity, coupling)
        )
    highest = lax.Precision.HIGHEST
    partial_value = jnp.einsum("vxyz,zc->vxyc", state, factor_z, precision=highest)
    partial_value = lax.psum_scatter(partial_value, "gz", scatter_dimension=3, tiled=True)
    partial_value = jnp.einsum("vxyc,yb->vxbc", partial_value, factor_y, precision=highest)
    partial_value = lax.psum_scatter(partial_value, "gy", scatter_dimension=2, tiled=True)
    partial_value = jnp.einsum("vxbc,xa->vabc", partial_value, factor_x, precision=highest)
    core_tensor = lax.psum_scatter(partial_value, "gx", scatter_dimension=1, tiled=True)
    return core_tensor


class Plan:
    def __init__(self, mesh_shape, fields, factor_x):
        self.nx, self.ny, self.nz = (mesh_shape[a] for a in ("gx", "gy", "gz"))
        self.vars, self.lx, self.ly, self.lz = fields
        self.rank = factor_x[1]
        self.ax, self.by, self.cz = self.rank // self.nx, self.rank // self.ny, self.rank // self.nz
        self.edge = [0, 1, self.lx - 2, self.lx - 1]
        self.inner = list(range(2, self.lx - 2))
        self.tiles = self.ly // 8

    def fits(self):
        return (
            self.lz == 128
            and self.ly % 8 == 0
            and min(self.nx, self.ny, self.nz) > 1
            and self.lx > 4
            and self.lx * self.tiles * 4 <= 128
            and self.rank % self.nx == 0 and self.rank % self.ny == 0 and self.rank % self.nz == 0
            and self.cz % 8 == 0
            and self.lx * self.by % 128 == 0
            and self.ax * self.by % 128 == 0
        )


def kernel(
    plan,
    fields,
    velocity,
    diffusivity_in,
    coupling_in,
    factor_x_in,
    factor_y_in,
    factor_z_in,
    out,
    diffusivity,
    coupling,
    factor_x,
    factor_y,
    factor_z,
    cells,
    speed,
    y_out,
    y_in,
    z_out,
    z_in,
    spread_y,
    spread_x,
    yz_out,
    yz_in,
    x_out,
    x_in,
    load_sem,
    x_send,
    x_recv,
    y_send,
    y_recv,
    z_send,
    z_recv,
    yz_send,
    yz_recv,
    xs_send,
    xs_recv,
):
    p = plan
    nx, ny, nz = p.nx, p.ny, p.nz
    lx, ly, nv = p.lx, p.ly, p.vars
    mx, my, mz = lax.axis_index("gx"), lax.axis_index("gy"), lax.axis_index("gz")
    rows = slice(PAD, PAD + ly)
    low_x, high_x = mx > 0, mx < nx - 1
    low_y, high_y = my > 0, my < ny - 1
    low_z, high_z = mz > 0, mz < nz - 1

    def remote(src, dst, send, recv, axis, to):
        return pltpu.make_async_remote_copy(
            src_ref=src, dst_ref=dst, send_sem=send, recv_sem=recv,
            device_id={axis: to}, device_id_type=MESH,
        )

    def up(index, count):
        return lax.rem(index + 1, count)

    def down(index, count):
        return lax.rem(index + count - 1, count)

    def x_messages(s, v):
        if s == 0:
            top, bottom = fields.at[v, lx - 2:lx], fields.at[v, 0:2]
        else:
            top = cells.at[s, v, lx:lx + 2, rows]
            bottom = cells.at[s, v, 2:4, rows]
        return [
            (high_x, low_x, remote(
                top, cells.at[s, v, 0:2, rows],
                x_send.at[0], x_recv.at[s, v, 0], "gx", up(mx, nx))),
            (low_x, high_x, remote(
                bottom, cells.at[s, v, lx + 2:lx + 4, rows],
                x_send.at[1], x_recv.at[s, v, 1], "gx", down(mx, nx))),
        ]

    def yz_messages(s, v):
        result = [
            (None, None, remote(
                z_out.at[s, v], z_in.at[s, 0, v],
                z_send.at[0], z_recv.at[s, v, 0], "gz", up(mz, nz))),
            (None, None, remote(
                z_out.at[s, v], z_in.at[s, 1, v],
                z_send.at[1], z_recv.at[s, v, 1], "gz", down(mz, nz))),
        ]
        if ny == 2:
            result.append((None, None, remote(
                y_out.at[s, 1 - my, v], y_in.at[s, my, v],
                y_send.at[0], y_recv.at[s, v, 0], "gy", 1 - my)))
        else:
            result += [
                (high_y, low_y, remote(
                    y_out.at[s, 1, v], y_in.at[s, 0, v],
                    y_send.at[0], y_recv.at[s, v, 0], "gy", up(my, ny))),
                (low_y, high_y, remote(
                    y_out.at[s, 0, v], y_in.at[s, 1, v],
                    y_send.at[1], y_recv.at[s, v, 1], "gy", down(my, ny))),
            ]
        return result

    def guarded(condition, action):
        if condition is None:
            action()
        else:
            pl.when(condition)(action)

    def start(messages):
        for sends, _, copy in messages:
            guarded(sends, copy.start)

    def arrive(messages):
        for _, gets, copy in messages:
            guarded(gets, copy.wait_recv)

    def all_sent():
        layers = cells.at[0:STAGES, :, 0:2, rows]
        waits = [
            (high_x, remote(layers, layers, x_send.at[0], x_recv.at[0, 0, 0], "gx", up(mx, nx))),
            (low_x, remote(layers, layers, x_send.at[1], x_recv.at[0, 0, 1], "gx", down(mx, nx))),
            (None, remote(z_out, z_out, z_send.at[0], z_recv.at[0, 0, 0], "gz", up(mz, nz))),
            (None, remote(z_out, z_out, z_send.at[1], z_recv.at[0, 0, 1], "gz", down(mz, nz))),
        ]
        half = y_out.at[:, 0]
        if ny == 2:
            waits.append((None, remote(half, half, y_send.at[0], y_recv.at[0, 0, 0], "gy", 1 - my)))
        else:
            waits += [
                (high_y, remote(half, half, y_send.at[0], y_recv.at[0, 0, 0], "gy", up(my, ny))),
                (low_y, remote(half, half, y_send.at[1], y_recv.at[0, 0, 1], "gy", down(my, ny))),
            ]
        for condition, copy in waits:
            guarded(condition, copy.wait_send)

    lane = lax.broadcasted_iota(jnp.int32, (8, 128), 1)
    quarter = lax.shift_right_logical(lane, 2)
    lower = jnp.bitwise_and(lane, 3) < 2
    inside = jnp.where(lower, jnp.minimum(mz, 1), jnp.minimum(nz - 1 - mz, 1)) > 0

    def pack(s, v, x, value, z):
        y_out[s, 0, v, 2 * x:2 * x + 2] = value[0:2]
        y_out[s, 1, v, 2 * x:2 * x + 2] = value[ly - 2:ly]
        for t in range(p.tiles):
            place = x * p.tiles + t
            turned = pltpu.roll(value[8 * t:8 * t + 8], (4 * place + 2) % 128, 1)
            z = jnp.where(quarter == place, turned, z)
        return z

    def advance(s, v, layers, z):
        edges = jnp.where(lower, z_in[s, 0, v], z_in[s, 1, v])
        edges = jnp.where(inside, edges, 0.0)
        spread = time_step * diffusivity[v]
        rates = [time_step * coupling[v, w] for w in range(nv)]
        keep = 1.0 - 6.0 * spread
        for x in layers:
            cells[s, v, x + 2, PAD - 2:PAD] = y_in[s, 0, v, 2 * x:2 * x + 2]
            cells[s, v, x + 2, PAD + ly:PAD + ly + 2] = y_in[s, 1, v, 2 * x:2 * x + 2]
        for x in layers:
            centre = cells[s, v, x + 2, rows]
            turned = [[], [], [], []]
            for t in range(p.tiles):
                tile = centre[8 * t:8 * t + 8]
                beside = pltpu.roll(edges, (126 - 4 * (x * p.tiles + t)) % 128, 1)
                for i, (mask, shift) in enumerate(
                        ((lane == 0, 127), (lane == 127, 1), (lane <= 1, 126), (lane >= 126, 2))):
                    turned[i].append(pltpu.roll(jnp.where(mask, beside, tile), shift, 1))
            near = [
                (cells[s, v, x + 3, rows], cells[s, v, x + 1, rows],
                 cells[s, v, x + 4, rows], cells[s, v, x, rows]),
                (cells[s, v, x + 2, PAD + 1:PAD + 1 + ly], cells[s, v, x + 2, PAD - 1:PAD - 1 + ly],
                 cells[s, v, x + 2, PAD + 2:PAD + 2 + ly], cells[s, v, x + 2, PAD - 2:PAD - 2 + ly]),
                tuple(jnp.concatenate(parts, axis=0) for parts in turned),
            ]
            moved = around = None
            for a, (next1, last1, next2, last2) in enumerate(near):
                flow = speed[a, x] * (8.0 * (next1 - last1) - (next2 - last2))
                both = next1 + last1
                moved = flow if moved is None else moved + flow
                around = both if around is None else around + both
            factor = keep
            for w in range(nv):
                factor = factor + rates[w] * cells[s, w, x + 2, rows]
            new = centre * factor + moved + spread * around
            if s % 2 == 1:
                new = 0.5 * (new + cells[s - 1, v, x + 2, rows])
            cells[s + 1, v, x + 2, rows] = new
            if s + 1 < STAGES:
                z = pack(s + 1, v, x, new, z)
        return z

    def fetch(i, source, target):
        copy = pltpu.make_async_copy(source, target, load_sem.at[i])
        copy.start()
        return copy

    partners = [
        {"gy": lax.rem(my + dy, ny), "gz": lax.rem(mz + dz, nz)}
        for dy in range(ny) for dz in range(nz) if dy or dz
    ]
    line = [{"gx": lax.rem(mx + dx, nx)} for dx in range(1, nx)]
    barrier = pltpu.get_barrier_semaphore()
    for device in partners + line:
        pl.semaphore_signal(barrier, inc=1, device_id=device, device_id_type=MESH)
    load = fetch(0, fields, cells.at[0, :, 2:lx + 2, rows])
    load_rest = [
        fetch(1, velocity, speed),
        fetch(2, diffusivity_in, diffusivity),
        fetch(3, coupling_in, coupling),
        fetch(4, factor_x_in, factor_x),
        fetch(5, factor_y_in, factor_y),
        fetch(6, factor_z_in, factor_z),
    ]

    def clear(condition, ref, *index):
        @pl.when(jnp.logical_not(condition))
        def _():
            ref[index] = jnp.zeros_like(ref[index])

    for s in range(STAGES):
        clear(low_x, cells, s, slice(None), slice(0, 2))
        clear(high_x, cells, s, slice(None), slice(lx + 2, lx + 4))
        clear(low_y, y_in, s, 0)
        clear(high_y, y_in, s, 1)

    pl.semaphore_wait(barrier, len(partners) + len(line))

    for v in range(nv):
        start(x_messages(0, v))
    load.wait()

    blank = jnp.zeros((8, 128), jnp.float32)

    def first_pack(v, carry):
        z = blank
        for x in range(lx):
            z = pack(0, v, x, cells[0, v, x + 2, rows], z)
        z_out[0, v] = z
        start(yz_messages(0, v))
        return carry

    lax.fori_loop(0, nv, first_pack, 0)
    for copy in load_rest:
        copy.wait()
    speed[...] = speed[...] * (-time_step / 12.0)

    def split(value):
        high = value.astype(jnp.bfloat16)
        return high, (value - high.astype(jnp.float32)).astype(jnp.bfloat16)

    def product(a, b, contract=((1,), (0,))):
        (a_high, a_low), (b_high, b_low) = a, b
        dot = functools.partial(
            lax.dot_general, dimension_numbers=(contract, ((), ())), preferred_element_type=jnp.float32)
        return dot(a_high, b_high) + (dot(a_high, b_low) + dot(a_low, b_high))

    chunk_y = lx * p.by
    wide_y = ny * chunk_y
    column = lax.broadcasted_iota(jnp.int32, (p.rank, wide_y), 1)
    row = lax.broadcasted_iota(jnp.int32, (p.rank, wide_y), 0)
    place_y = jnp.where(row == column // chunk_y * p.by + column % p.by, 1.0, 0.0)
    repeated = jnp.dot(factor_y[...], place_y, precision=HIGHEST, preferred_element_type=jnp.float32)
    column = lax.broadcasted_iota(jnp.int32, (ly, wide_y), 1) % chunk_y // p.by
    for x in range(lx):
        for i, part in enumerate(split(jnp.where(column == x, repeated, 0.0))):
            spread_y[i, x * ly:(x + 1) * ly] = part
    chunk_x = p.ax * p.by
    wide_x = nx * chunk_x
    column = lax.broadcasted_iota(jnp.int32, (p.rank, wide_x), 1)
    row = lax.broadcasted_iota(jnp.int32, (p.rank, wide_x), 0)
    place_x = jnp.where(row == column // p.by, 1.0, 0.0)
    repeated = jnp.dot(factor_x[...], place_x, precision=HIGHEST, preferred_element_type=jnp.float32)
    column = lax.broadcasted_iota(jnp.int32, (p.by, wide_x), 1) % p.by
    row = lax.broadcasted_iota(jnp.int32, (p.by, wide_x), 0)
    for x in range(lx):
        for i, part in enumerate(split(jnp.where(column == row, repeated[x:x + 1], 0.0))):
            spread_x[i, x * p.by:(x + 1) * p.by] = part

    for s in range(STAGES):
        last = s == STAGES - 1

        def project(v):
            state = cells[STAGES, v, 2:lx + 2, rows].reshape(lx * ly, p.lz)
            reduced = product(split(factor_z[...]), split(state), ((1,), (1,)))
            reduced = product(split(reduced), (spread_y[0], spread_y[1]))
            for y in range(ny):
                for z in range(nz):
                    yz_out[y * nz + z, v] = reduced[
                        z * p.cz:(z + 1) * p.cz, y * chunk_y:(y + 1) * chunk_y]

        def stage(v, carry):
            arrive(yz_messages(s, v) + x_messages(s, v))
            z = advance(s, v, p.edge, blank)
            if not last:
                start(x_messages(s + 1, v))
            z = advance(s, v, p.inner, z)
            if last:
                project(v)
            else:
                z_out[s + 1, v] = z
                start(yz_messages(s + 1, v))
            return carry

        lax.fori_loop(0, nv, stage, 0)

    plane = []
    for i, device in enumerate(partners):
        plane.append(pltpu.make_async_remote_copy(
            src_ref=yz_out.at[device["gy"] * nz + device["gz"]], dst_ref=yz_in.at[i],
            send_sem=yz_send.at[i], recv_sem=yz_recv.at[i],
            device_id=device, device_id_type=MESH))
        plane[-1].start()
    total = yz_out[my * nz + mz]
    for i, copy in enumerate(plane):
        copy.wait_recv()
        total = total + yz_in[i]

    total = total.reshape(nv * p.cz, chunk_y)
    total = product(split(total), (spread_x[0], spread_x[1]))
    for x in range(nx):
        x_out[x] = total[:, x * chunk_x:(x + 1) * chunk_x].reshape(nv, p.cz, chunk_x)
    along = []
    for i, device in enumerate(line):
        along.append(pltpu.make_async_remote_copy(
            src_ref=x_out.at[device["gx"]], dst_ref=x_in.at[i],
            send_sem=xs_send.at[i], recv_sem=xs_recv.at[i],
            device_id=device, device_id_type=MESH))
        along[-1].start()
    total = x_out[mx]
    for i, copy in enumerate(along):
        copy.wait_recv()
        total = total + x_in[i]
    for a in range(p.ax):
        out[:, a] = total[:, :, a * p.by:(a + 1) * p.by]

    all_sent()
    for copy in plane + along:
        copy.wait_send()


def local_kernel(plan, fields, velocity, diffusivity, coupling, factor_x, factor_y, factor_z):
    p = plan
    nv, lx, ly = p.vars, p.lx, p.ly
    chunk_y, chunk_x = lx * p.by, p.ax * p.by
    others = p.ny * p.nz - 1
    vmem = lambda *shape: pltpu.VMEM(shape, jnp.float32)
    dma = lambda *shape: pltpu.SemaphoreType.DMA(shape)
    whole = pl.BlockSpec(memory_space=pltpu.VMEM)
    result = pl.pallas_call(
        functools.partial(kernel, p),
        out_shape=jax.ShapeDtypeStruct((nv, p.ax, p.cz, p.by), jnp.float32),
        in_specs=[pl.BlockSpec(memory_space=pl.ANY)] * 7,
        out_specs=whole,
        scratch_shapes=[
            pltpu.SMEM(diffusivity.shape, jnp.float32),
            pltpu.SMEM(coupling.shape, jnp.float32),
            vmem(*factor_x.shape),
            vmem(*factor_y.shape),
            vmem(*factor_z.shape[::-1]),
            vmem(STAGES + 1, nv, lx + 4, ly + 2 * PAD, p.lz),
            vmem(3, lx, ly, p.lz),
            vmem(STAGES, 2, nv, 8 * -(-lx // 4), p.lz),
            vmem(STAGES, 2, nv, 8 * -(-lx // 4), p.lz),
            vmem(STAGES, nv, 8, 128),
            vmem(STAGES, 2, nv, 8, 128),
            pltpu.VMEM((2, lx * ly, p.ny * chunk_y), jnp.bfloat16),
            pltpu.VMEM((2, chunk_y, p.nx * chunk_x), jnp.bfloat16),
            vmem(p.ny * p.nz, nv, p.cz, chunk_y),
            vmem(others, nv, p.cz, chunk_y),
            vmem(p.nx, nv, p.cz, chunk_x),
            vmem(p.nx - 1, nv, p.cz, chunk_x),
            dma(7),
            dma(2), dma(STAGES, nv, 2),
            dma(2), dma(STAGES, nv, 2),
            dma(2), dma(STAGES, nv, 2),
            dma(others), dma(others),
            dma(p.nx - 1), dma(p.nx - 1),
        ],
        compiler_params=pltpu.CompilerParams(
            collective_id=0, has_side_effects=True, vmem_limit_bytes=VMEM_LIMIT),
    )(fields, velocity, diffusivity, coupling, factor_x, factor_y, factor_z.T)
    return jnp.transpose(result, (0, 1, 3, 2))


def solution(mesh):
    def local(fields, velocity, diffusivity, coupling, factor_x, factor_y, factor_z):
        plan = Plan(mesh.shape, fields.shape, factor_x.shape)
        run = functools.partial(local_kernel, plan) if plan.fits() else local_plain
        return run(fields, velocity, diffusivity, coupling, factor_x, factor_y, factor_z)

    return jax.shard_map(
        local,
        mesh=mesh,
        in_specs=(
            P(None, "gx", "gy", "gz"),
            P(None, "gx", "gy", "gz"),
            P(),
            P(),
            P("gx", None),
            P("gy", None),
            P("gz", None),
        ),
        out_specs=P(None, "gx", "gy", "gz"),
        check_vma=False,
    )
```

```python
import functools
import jax
import jax.numpy as jnp
from jax import lax
from jax.experimental import pallas as pl
from jax.experimental.pallas import tpu as pltpu
from jax.sharding import PartitionSpec as P

STEPS = 2
STAGES = 2 * STEPS
HALO = 2
VMEM_LIMIT = 66 * 1000 * 1000
MESH = pl.DeviceIdType.MESH
HIGHEST = lax.Precision.HIGHEST


time_step = 0.2
def with_halo(cells, sides, width):
    for axis, dim in sides:
        count = lax.axis_size(axis)
        ends = count - 1
        head = lax.slice_in_dim(cells, 0, width, axis=dim)
        tail = lax.slice_in_dim(cells, cells.shape[dim] - width, cells.shape[dim], axis=dim)
        cells = jnp.concatenate(
            [
                lax.ppermute(tail, axis, [(i, (i + 1) % count) for i in range(ends)]),
                cells,
                lax.ppermute(head, axis, [((i + 1) % count, i) for i in range(ends)]),
            ],
            axis=dim,
        )
    return cells


def offset_view(padded, dimension, offset):
    indices = [slice(None)]
    for other in (1, 2, 3):
        if other == dimension:
            first_cell = 2 + offset
            indices.append(slice(first_cell, first_cell + padded.shape[other] - 4))
        else:
            indices.append(slice(2, padded.shape[other] - 2))
    return padded[tuple(indices)]


def tendency(padded, velocity, diffusivity, coupling):
    center = offset_view(padded, 1, 0)
    transport = jnp.zeros_like(center)
    laplace = jnp.zeros_like(center)
    for dimension in (1, 2, 3):
        gradient = (
            8.0 * (offset_view(padded, dimension, 1) - offset_view(padded, dimension, -1))
            - (offset_view(padded, dimension, 2) - offset_view(padded, dimension, -2))
        ) / 12.0
        transport = transport + velocity[dimension - 1][None] * gradient
        laplace = (
            laplace
            + offset_view(padded, dimension, 1)
            + offset_view(padded, dimension, -1)
            - 2.0 * center
        )
    mixing = jnp.einsum("vw,wxyz->vxyz", coupling, center, precision=lax.Precision.HIGHEST)
    return -transport + diffusivity[:, None, None, None] * laplace + center * mixing


def with_edges(values):
    return with_halo(values, (("gx", 1), ("gy", 2), ("gz", 3)), 2)


def local_plain(fields, velocity, diffusivity, coupling, factor_x, factor_y, factor_z):
    state = fields
    for repeat in range(STEPS):
        section = state + time_step * tendency(with_edges(state), velocity, diffusivity, coupling)
        state = 0.5 * (
            state
            + section
            + time_step * tendency(with_edges(section), velocity, diffusivity, coupling)
        )
    highest = lax.Precision.HIGHEST
    partial_value = jnp.einsum("vxyz,zc->vxyc", state, factor_z, precision=highest)
    partial_value = lax.psum_scatter(partial_value, "gz", scatter_dimension=3, tiled=True)
    partial_value = jnp.einsum("vxyc,yb->vxbc", partial_value, factor_y, precision=highest)
    partial_value = lax.psum_scatter(partial_value, "gy", scatter_dimension=2, tiled=True)
    partial_value = jnp.einsum("vxbc,xa->vabc", partial_value, factor_x, precision=highest)
    core_tensor = lax.psum_scatter(partial_value, "gx", scatter_dimension=1, tiled=True)
    return core_tensor


class Plan:
    def __init__(self, mesh_shape, fields, factor_x):
        self.nx, self.ny, self.nz = (mesh_shape[a] for a in ("gx", "gy", "gz"))
        self.vars, self.lx, self.ly, self.lz = fields
        self.rank = factor_x[1]
        self.ax, self.by, self.cz = self.rank // self.nx, self.rank // self.ny, self.rank // self.nz
        self.edge = [0, 1, self.lx - 2, self.lx - 1]
        self.inner = list(range(2, self.lx - 2))
        self.tiles = self.ly // 8

    def fits(self):
        return (
            self.lz == 128
            and self.ly % 8 == 0
            and self.ly >= 16
            and min(self.nx, self.ny, self.nz) > 1
            and self.lx > 4
            and self.lx * self.tiles * 4 <= 128
            and self.rank % self.nx == 0 and self.rank % self.ny == 0 and self.rank % self.nz == 0
            and self.cz % 8 == 0
            and self.lx * self.by % 128 == 0
            and self.ax * self.by % 128 == 0
        )


def kernel(
    plan,
    fields,
    velocity,
    diffusivity_in,
    coupling_in,
    factor_x_in,
    factor_y_in,
    factor_z_in,
    out,
    diffusivity,
    coupling,
    factor_x,
    factor_y,
    factor_z,
    raw,
    raw_speed,
    cells,
    speed,
    y_out,
    y_in,
    z_out,
    z_in,
    spread_y,
    spread_x,
    yz_out,
    yz_in,
    x_out,
    x_in,
    load_sem,
    x_send,
    x_recv,
    y_send,
    y_recv,
    z_send,
    z_recv,
    yz_send,
    yz_recv,
    xs_send,
    xs_recv,
):
    p = plan
    nx, ny, nz = p.nx, p.ny, p.nz
    lx, ly, nv = p.lx, p.ly, p.vars
    mx, my, mz = lax.axis_index("gx"), lax.axis_index("gy"), lax.axis_index("gz")
    tiles = p.tiles
    low_x, high_x = mx > 0, mx < nx - 1
    low_y, high_y = my > 0, my < ny - 1
    low_z, high_z = mz > 0, mz < nz - 1

    def remote(src, dst, send, recv, axis, to):
        return pltpu.make_async_remote_copy(
            src_ref=src, dst_ref=dst, send_sem=send, recv_sem=recv,
            device_id={axis: to}, device_id_type=MESH,
        )

    def up(index, count):
        return lax.rem(index + 1, count)

    def down(index, count):
        return lax.rem(index + count - 1, count)

    def x_messages(s, v):
        if s == 0:
            top, bottom = fields.at[v, lx - 2:lx], fields.at[v, 0:2]
            below, above = raw.at[v, 0:2], raw.at[v, lx + 2:lx + 4]
        else:
            top, bottom = cells.at[s, v, lx:lx + 2], cells.at[s, v, 2:4]
            below, above = cells.at[s, v, 0:2], cells.at[s, v, lx + 2:lx + 4]
        return [
            (high_x, low_x, remote(
                top, below, x_send.at[0], x_recv.at[s, v, 0], "gx", up(mx, nx))),
            (low_x, high_x, remote(
                bottom, above, x_send.at[1], x_recv.at[s, v, 1], "gx", down(mx, nx))),
        ]

    def yz_messages(s, v):
        result = [
            (None, None, remote(
                z_out.at[s, v], z_in.at[s, 0, v],
                z_send.at[0], z_recv.at[s, v, 0], "gz", up(mz, nz))),
            (None, None, remote(
                z_out.at[s, v], z_in.at[s, 1, v],
                z_send.at[1], z_recv.at[s, v, 1], "gz", down(mz, nz))),
        ]
        if ny == 2:
            result.append((None, None, remote(
                y_out.at[s, 1 - my, v], y_in.at[s, my, v],
                y_send.at[0], y_recv.at[s, v, 0], "gy", 1 - my)))
        else:
            result += [
                (high_y, low_y, remote(
                    y_out.at[s, 1, v], y_in.at[s, 0, v],
                    y_send.at[0], y_recv.at[s, v, 0], "gy", up(my, ny))),
                (low_y, high_y, remote(
                    y_out.at[s, 0, v], y_in.at[s, 1, v],
                    y_send.at[1], y_recv.at[s, v, 1], "gy", down(my, ny))),
            ]
        return result

    def guarded(condition, action):
        if condition is None:
            action()
        else:
            pl.when(condition)(action)

    def start(messages):
        for sends, _, copy in messages:
            guarded(sends, copy.start)

    def arrive(messages):
        for _, gets, copy in messages:
            guarded(gets, copy.wait_recv)

    def all_sent():
        layers = cells.at[0:STAGES, :, 0:2]
        waits = [
            (high_x, remote(layers, layers, x_send.at[0], x_recv.at[0, 0, 0], "gx", up(mx, nx))),
            (low_x, remote(layers, layers, x_send.at[1], x_recv.at[0, 0, 1], "gx", down(mx, nx))),
            (None, remote(z_out, z_out, z_send.at[0], z_recv.at[0, 0, 0], "gz", up(mz, nz))),
            (None, remote(z_out, z_out, z_send.at[1], z_recv.at[0, 0, 1], "gz", down(mz, nz))),
        ]
        half = y_out.at[:, 0]
        if ny == 2:
            waits.append((None, remote(half, half, y_send.at[0], y_recv.at[0, 0, 0], "gy", 1 - my)))
        else:
            waits += [
                (high_y, remote(half, half, y_send.at[0], y_recv.at[0, 0, 0], "gy", up(my, ny))),
                (low_y, remote(half, half, y_send.at[1], y_recv.at[0, 0, 1], "gy", down(my, ny))),
            ]
        for condition, copy in waits:
            guarded(condition, copy.wait_send)

    lane = lax.broadcasted_iota(jnp.int32, (8, 128), 1)
    sublane = lax.broadcasted_iota(jnp.int32, (8, 128), 0)
    quarter = lax.shift_right_logical(lane, 2)
    lower = jnp.bitwise_and(lane, 3) < 2
    inside = jnp.where(lower, jnp.minimum(mz, 1), jnp.minimum(nz - 1 - mz, 1)) > 0

    def pack(s, v, x, value, z):
        for i in range(2):
            y_out[s, 0, v, 2 * x + i:2 * x + i + 1] = value[i, 0:1]
            y_out[s, 1, v, 2 * x + i:2 * x + i + 1] = value[tiles - 2 + i, 7:8]
        for t in range(p.tiles):
            place = x * p.tiles + t
            turned = pltpu.roll(value[t], (4 * place + 2) % 128, 1)
            z = jnp.where(quarter == place, turned, z)
        return z

    def advance(s, v, layers, z):
        edges = jnp.where(lower, z_in[s, 0, v], z_in[s, 1, v])
        edges = jnp.where(inside, edges, 0.0)
        spread = time_step * diffusivity[v]
        rates = [time_step * coupling[v, w] for w in range(nv)]
        keep = 1.0 - 6.0 * spread
        for x in layers:
            centre = cells[s, v, x + 2]
            along = [
                jnp.where(sublane == 0, y_in[s, 0, v, 2 * x + i:2 * x + i + 1],
                          pltpu.roll(centre[tiles - 2 + i], 1, 0)) for i in range(2)
            ] + [centre[t] for t in range(tiles)] + [
                jnp.where(sublane == 7, y_in[s, 1, v, 2 * x + i:2 * x + i + 1],
                          pltpu.roll(centre[i], 7, 0)) for i in range(2)
            ]
            shifted = lambda offset: jnp.stack(along[2 + offset:2 + offset + tiles])
            turned = [[], [], [], []]
            for t in range(p.tiles):
                tile = centre[t]
                beside = pltpu.roll(edges, (126 - 4 * (x * p.tiles + t)) % 128, 1)
                for i, (mask, shift) in enumerate(
                        ((lane == 0, 127), (lane == 127, 1), (lane <= 1, 126), (lane >= 126, 2))):
                    turned[i].append(pltpu.roll(jnp.where(mask, beside, tile), shift, 1))
            near = [
                (cells[s, v, x + 3], cells[s, v, x + 1], cells[s, v, x + 4], cells[s, v, x]),
                (shifted(1), shifted(-1), shifted(2), shifted(-2)),
                tuple(jnp.stack(parts) for parts in turned),
            ]
            moved = around = None
            for a, (next1, last1, next2, last2) in enumerate(near):
                flow = speed[a, x] * (8.0 * (next1 - last1) - (next2 - last2))
                both = next1 + last1
                moved = flow if moved is None else moved + flow
                around = both if around is None else around + both
            factor = keep
            for w in range(nv):
                factor = factor + rates[w] * cells[s, w, x + 2]
            new = centre * factor + moved + spread * around
            if s % 2 == 1:
                new = 0.5 * (new + cells[s - 1, v, x + 2])
            cells[s + 1, v, x + 2] = new
            if s + 1 < STAGES:
                z = pack(s + 1, v, x, new, z)
        return z

    def fetch(i, source, target):
        copy = pltpu.make_async_copy(source, target, load_sem.at[i])
        copy.start()
        return copy

    partners = [
        {"gy": lax.rem(my + dy, ny), "gz": lax.rem(mz + dz, nz)}
        for dy in range(ny) for dz in range(nz) if dy or dz
    ]
    line = [{"gx": lax.rem(mx + dx, nx)} for dx in range(1, nx)]
    barrier = pltpu.get_barrier_semaphore()
    for device in partners + line:
        pl.semaphore_signal(barrier, inc=1, device_id=device, device_id_type=MESH)
    load = fetch(0, fields, raw.at[:, 2:lx + 2])
    load_rest = [
        fetch(1, velocity, raw_speed),
        fetch(2, diffusivity_in, diffusivity),
        fetch(3, coupling_in, coupling),
        fetch(4, factor_x_in, factor_x),
        fetch(5, factor_y_in, factor_y),
        fetch(6, factor_z_in, factor_z),
    ]

    def clear(condition, ref, *index):
        @pl.when(jnp.logical_not(condition))
        def _():
            ref[index] = jnp.zeros_like(ref[index])

    for s in range(STAGES):
        edge = cells if s else raw
        lead = (s,) if s else ()
        clear(low_x, edge, *lead, slice(None), slice(0, 2))
        clear(high_x, edge, *lead, slice(None), slice(lx + 2, lx + 4))
        clear(low_y, y_in, s, 0)
        clear(high_y, y_in, s, 1)

    pl.semaphore_wait(barrier, len(partners) + len(line))

    for v in range(nv):
        start(x_messages(0, v))
    load.wait()

    blank = jnp.zeros((8, 128), jnp.float32)

    def arrange(v, x):
        for t in range(tiles):
            cells[0, v, x, t] = raw[v, x, pl.ds(t, 8, stride=tiles)]

    def first_pack(v, carry):
        z = blank
        for x in range(lx):
            arrange(v, x + 2)
            z = pack(0, v, x, cells[0, v, x + 2], z)
        z_out[0, v] = z
        start(yz_messages(0, v))
        return carry

    lax.fori_loop(0, nv, first_pack, 0)
    for copy in load_rest:
        copy.wait()

    def arrange_speed(a, carry):
        for x in range(lx):
            for t in range(tiles):
                speed[a, x, t] = raw_speed[a, x, pl.ds(t, 8, stride=tiles)] * (-time_step / 12.0)
        return carry

    lax.fori_loop(0, 3, arrange_speed, 0)

    def split(value):
        high = value.astype(jnp.bfloat16)
        return high, (value - high.astype(jnp.float32)).astype(jnp.bfloat16)

    def product(a, b, contract=((1,), (0,))):
        (a_high, a_low), (b_high, b_low) = a, b
        dot = functools.partial(
            lax.dot_general, dimension_numbers=(contract, ((), ())), preferred_element_type=jnp.float32)
        return dot(a_high, b_high) + (dot(a_high, b_low) + dot(a_low, b_high))

    chunk_y = lx * p.by
    wide_y = ny * chunk_y
    column = lax.broadcasted_iota(jnp.int32, (p.rank, wide_y), 1)
    row = lax.broadcasted_iota(jnp.int32, (p.rank, wide_y), 0)
    place_y = jnp.where(row == column // chunk_y * p.by + column % p.by, 1.0, 0.0)
    column = lax.broadcasted_iota(jnp.int32, (ly, ly), 1)
    row = lax.broadcasted_iota(jnp.int32, (ly, ly), 0)
    order = jnp.where(column == row % 8 * tiles + row // 8, 1.0, 0.0)
    ordered = jnp.dot(order, factor_y[...], precision=HIGHEST, preferred_element_type=jnp.float32)
    repeated = jnp.dot(ordered, place_y, precision=HIGHEST, preferred_element_type=jnp.float32)
    column = lax.broadcasted_iota(jnp.int32, (ly, wide_y), 1) % chunk_y // p.by
    for x in range(lx):
        for i, part in enumerate(split(jnp.where(column == x, repeated, 0.0))):
            spread_y[i, x * ly:(x + 1) * ly] = part
    chunk_x = p.ax * p.by
    wide_x = nx * chunk_x
    column = lax.broadcasted_iota(jnp.int32, (p.rank, wide_x), 1)
    row = lax.broadcasted_iota(jnp.int32, (p.rank, wide_x), 0)
    place_x = jnp.where(row == column // p.by, 1.0, 0.0)
    repeated = jnp.dot(factor_x[...], place_x, precision=HIGHEST, preferred_element_type=jnp.float32)
    column = lax.broadcasted_iota(jnp.int32, (p.by, wide_x), 1) % p.by
    row = lax.broadcasted_iota(jnp.int32, (p.by, wide_x), 0)
    for x in range(lx):
        for i, part in enumerate(split(jnp.where(column == row, repeated[x:x + 1], 0.0))):
            spread_x[i, x * p.by:(x + 1) * p.by] = part

    for s in range(STAGES):
        last = s == STAGES - 1

        def project(v):
            state = cells[STAGES, v, 2:lx + 2].reshape(lx * ly, p.lz)
            reduced = product(split(factor_z[...]), split(state), ((1,), (1,)))
            reduced = product(split(reduced), (spread_y[0], spread_y[1]))
            for y in range(ny):
                for z in range(nz):
                    yz_out[y * nz + z, v] = reduced[
                        z * p.cz:(z + 1) * p.cz, y * chunk_y:(y + 1) * chunk_y]

        def stage(v, carry):
            arrive(yz_messages(s, v) + x_messages(s, v))
            if s == 0:
                for x in (0, 1, lx + 2, lx + 3):
                    arrange(v, x)
            z = advance(s, v, p.edge, blank)
            if not last:
                start(x_messages(s + 1, v))
            z = advance(s, v, p.inner, z)
            if last:
                project(v)
            else:
                z_out[s + 1, v] = z
                start(yz_messages(s + 1, v))
            return carry

        lax.fori_loop(0, nv, stage, 0)

    plane = []
    for i, device in enumerate(partners):
        plane.append(pltpu.make_async_remote_copy(
            src_ref=yz_out.at[device["gy"] * nz + device["gz"]], dst_ref=yz_in.at[i],
            send_sem=yz_send.at[i], recv_sem=yz_recv.at[i],
            device_id=device, device_id_type=MESH))
        plane[-1].start()
    total = yz_out[my * nz + mz]
    for i, copy in enumerate(plane):
        copy.wait_recv()
        total = total + yz_in[i]

    total = total.reshape(nv * p.cz, chunk_y)
    total = product(split(total), (spread_x[0], spread_x[1]))
    for x in range(nx):
        x_out[x] = total[:, x * chunk_x:(x + 1) * chunk_x].reshape(nv, p.cz, chunk_x)
    along = []
    for i, device in enumerate(line):
        along.append(pltpu.make_async_remote_copy(
            src_ref=x_out.at[device["gx"]], dst_ref=x_in.at[i],
            send_sem=xs_send.at[i], recv_sem=xs_recv.at[i],
            device_id=device, device_id_type=MESH))
        along[-1].start()
    total = x_out[mx]
    for i, copy in enumerate(along):
        copy.wait_recv()
        total = total + x_in[i]
    for a in range(p.ax):
        out[:, a] = total[:, :, a * p.by:(a + 1) * p.by]

    all_sent()
    for copy in plane + along:
        copy.wait_send()


def local_kernel(plan, fields, velocity, diffusivity, coupling, factor_x, factor_y, factor_z):
    p = plan
    nv, lx, ly = p.vars, p.lx, p.ly
    chunk_y, chunk_x = lx * p.by, p.ax * p.by
    others = p.ny * p.nz - 1
    vmem = lambda *shape: pltpu.VMEM(shape, jnp.float32)
    dma = lambda *shape: pltpu.SemaphoreType.DMA(shape)
    whole = pl.BlockSpec(memory_space=pltpu.VMEM)
    result = pl.pallas_call(
        functools.partial(kernel, p),
        out_shape=jax.ShapeDtypeStruct((nv, p.ax, p.cz, p.by), jnp.float32),
        in_specs=[pl.BlockSpec(memory_space=pl.ANY)] * 7,
        out_specs=whole,
        scratch_shapes=[
            pltpu.SMEM(diffusivity.shape, jnp.float32),
            pltpu.SMEM(coupling.shape, jnp.float32),
            vmem(*factor_x.shape),
            vmem(*factor_y.shape),
            vmem(*factor_z.shape[::-1]),
            vmem(nv, lx + 4, ly, p.lz),
            vmem(3, lx, ly, p.lz),
            vmem(STAGES + 1, nv, lx + 4, p.tiles, 8, p.lz),
            vmem(3, lx, p.tiles, 8, p.lz),
            vmem(STAGES, 2, nv, 8 * -(-lx // 4), p.lz),
            vmem(STAGES, 2, nv, 8 * -(-lx // 4), p.lz),
            vmem(STAGES, nv, 8, 128),
            vmem(STAGES, 2, nv, 8, 128),
            pltpu.VMEM((2, lx * ly, p.ny * chunk_y), jnp.bfloat16),
            pltpu.VMEM((2, chunk_y, p.nx * chunk_x), jnp.bfloat16),
            vmem(p.ny * p.nz, nv, p.cz, chunk_y),
            vmem(others, nv, p.cz, chunk_y),
            vmem(p.nx, nv, p.cz, chunk_x),
            vmem(p.nx - 1, nv, p.cz, chunk_x),
            dma(7),
            dma(2), dma(STAGES, nv, 2),
            dma(2), dma(STAGES, nv, 2),
            dma(2), dma(STAGES, nv, 2),
            dma(others), dma(others),
            dma(p.nx - 1), dma(p.nx - 1),
        ],
        compiler_params=pltpu.CompilerParams(
            collective_id=0, has_side_effects=True, vmem_limit_bytes=VMEM_LIMIT),
    )(fields, velocity, diffusivity, coupling, factor_x, factor_y, factor_z.T)
    return jnp.transpose(result, (0, 1, 3, 2))


def solution(mesh):
    def local(fields, velocity, diffusivity, coupling, factor_x, factor_y, factor_z):
        plan = Plan(mesh.shape, fields.shape, factor_x.shape)
        run = functools.partial(local_kernel, plan) if plan.fits() else local_plain
        return run(fields, velocity, diffusivity, coupling, factor_x, factor_y, factor_z)

    return jax.shard_map(
        local,
        mesh=mesh,
        in_specs=(
            P(None, "gx", "gy", "gz"),
            P(None, "gx", "gy", "gz"),
            P(),
            P(),
            P("gx", None),
            P("gy", None),
            P("gz", None),
        ),
        out_specs=P(None, "gx", "gy", "gz"),
        check_vma=False,
    )
```

```python
import functools
import jax
import jax.numpy as jnp
from jax import lax
from jax.experimental import pallas as pl
from jax.experimental.pallas import tpu as pltpu
from jax.sharding import PartitionSpec as P

STEPS = 2
STAGES = 2 * STEPS
HALO = 2
VMEM_LIMIT = 66 * 1000 * 1000
MESH = pl.DeviceIdType.MESH
HIGHEST = lax.Precision.HIGHEST


time_step = 0.2
def with_halo(cells, sides, width):
    for axis, dim in sides:
        count = lax.axis_size(axis)
        ends = count - 1
        head = lax.slice_in_dim(cells, 0, width, axis=dim)
        tail = lax.slice_in_dim(cells, cells.shape[dim] - width, cells.shape[dim], axis=dim)
        cells = jnp.concatenate(
            [
                lax.ppermute(tail, axis, [(i, (i + 1) % count) for i in range(ends)]),
                cells,
                lax.ppermute(head, axis, [((i + 1) % count, i) for i in range(ends)]),
            ],
            axis=dim,
        )
    return cells


def offset_view(padded, dimension, offset):
    indices = [slice(None)]
    for other in (1, 2, 3):
        if other == dimension:
            first_cell = 2 + offset
            indices.append(slice(first_cell, first_cell + padded.shape[other] - 4))
        else:
            indices.append(slice(2, padded.shape[other] - 2))
    return padded[tuple(indices)]


def tendency(padded, velocity, diffusivity, coupling):
    center = offset_view(padded, 1, 0)
    transport = jnp.zeros_like(center)
    laplace = jnp.zeros_like(center)
    for dimension in (1, 2, 3):
        gradient = (
            8.0 * (offset_view(padded, dimension, 1) - offset_view(padded, dimension, -1))
            - (offset_view(padded, dimension, 2) - offset_view(padded, dimension, -2))
        ) / 12.0
        transport = transport + velocity[dimension - 1][None] * gradient
        laplace = (
            laplace
            + offset_view(padded, dimension, 1)
            + offset_view(padded, dimension, -1)
            - 2.0 * center
        )
    mixing = jnp.einsum("vw,wxyz->vxyz", coupling, center, precision=lax.Precision.HIGHEST)
    return -transport + diffusivity[:, None, None, None] * laplace + center * mixing


def with_edges(values):
    return with_halo(values, (("gx", 1), ("gy", 2), ("gz", 3)), 2)


def local_plain(fields, velocity, diffusivity, coupling, factor_x, factor_y, factor_z):
    state = fields
    for repeat in range(STEPS):
        section = state + time_step * tendency(with_edges(state), velocity, diffusivity, coupling)
        state = 0.5 * (
            state
            + section
            + time_step * tendency(with_edges(section), velocity, diffusivity, coupling)
        )
    highest = lax.Precision.HIGHEST
    partial_value = jnp.einsum("vxyz,zc->vxyc", state, factor_z, precision=highest)
    partial_value = lax.psum_scatter(partial_value, "gz", scatter_dimension=3, tiled=True)
    partial_value = jnp.einsum("vxyc,yb->vxbc", partial_value, factor_y, precision=highest)
    partial_value = lax.psum_scatter(partial_value, "gy", scatter_dimension=2, tiled=True)
    partial_value = jnp.einsum("vxbc,xa->vabc", partial_value, factor_x, precision=highest)
    core_tensor = lax.psum_scatter(partial_value, "gx", scatter_dimension=1, tiled=True)
    return core_tensor


class Plan:
    def __init__(self, mesh_shape, fields, factor_x):
        self.nx, self.ny, self.nz = (mesh_shape[a] for a in ("gx", "gy", "gz"))
        self.vars, self.lx, self.ly, self.lz = fields
        self.rank = factor_x[1]
        self.ax, self.by, self.cz = self.rank // self.nx, self.rank // self.ny, self.rank // self.nz
        self.edge = [0, 1, self.lx - 2, self.lx - 1]
        self.inner = list(range(2, self.lx - 2))
        self.tiles = self.ly // 8

    def fits(self):
        return (
            self.lz == 128
            and self.ly % 8 == 0
            and self.ly >= 16
            and min(self.nx, self.ny, self.nz) > 1
            and self.lx > 4
            and self.lx * self.tiles * 4 <= 128
            and self.rank % self.nx == 0 and self.rank % self.ny == 0 and self.rank % self.nz == 0
            and self.cz % 8 == 0
            and self.lx * self.by % 128 == 0
            and self.ax * self.by % 128 == 0
        )


def kernel(
    plan,
    fields,
    velocity,
    diffusivity_in,
    coupling_in,
    factor_x_in,
    factor_y_in,
    factor_z_in,
    out,
    diffusivity,
    coupling,
    factor_x,
    factor_y,
    factor_z,
    raw,
    raw_speed,
    cells,
    speed,
    y_out,
    y_in,
    z_out,
    z_in,
    spread_y,
    spread_x,
    yz_out,
    yz_in,
    x_out,
    x_in,
    load_sem,
    x_send,
    x_recv,
    y_send,
    y_recv,
    z_send,
    z_recv,
    yz_send,
    yz_recv,
    xs_send,
    xs_recv,
):
    p = plan
    nx, ny, nz = p.nx, p.ny, p.nz
    lx, ly, nv = p.lx, p.ly, p.vars
    mx, my, mz = lax.axis_index("gx"), lax.axis_index("gy"), lax.axis_index("gz")
    tiles = p.tiles
    low_x, high_x = mx > 0, mx < nx - 1
    low_y, high_y = my > 0, my < ny - 1
    low_z, high_z = mz > 0, mz < nz - 1

    def remote(src, dst, send, recv, axis, to):
        return pltpu.make_async_remote_copy(
            src_ref=src, dst_ref=dst, send_sem=send, recv_sem=recv,
            device_id={axis: to}, device_id_type=MESH,
        )

    def up(index, count):
        return lax.rem(index + 1, count)

    def down(index, count):
        return lax.rem(index + count - 1, count)

    def x_messages(s, v):
        if s == 0:
            top, bottom = fields.at[v, lx - 2:lx], fields.at[v, 0:2]
            below, above = raw.at[v, 0:2], raw.at[v, lx + 2:lx + 4]
        else:
            top, bottom = cells.at[s, v, lx:lx + 2], cells.at[s, v, 2:4]
            below, above = cells.at[s, v, 0:2], cells.at[s, v, lx + 2:lx + 4]
        return [
            (high_x, low_x, remote(
                top, below, x_send.at[0], x_recv.at[s, v, 0], "gx", up(mx, nx))),
            (low_x, high_x, remote(
                bottom, above, x_send.at[1], x_recv.at[s, v, 1], "gx", down(mx, nx))),
        ]

    def yz_messages(s, v):
        result = [
            (None, None, remote(
                z_out.at[s, v], z_in.at[s, 0, v],
                z_send.at[0], z_recv.at[s, v, 0], "gz", up(mz, nz))),
            (None, None, remote(
                z_out.at[s, v], z_in.at[s, 1, v],
                z_send.at[1], z_recv.at[s, v, 1], "gz", down(mz, nz))),
        ]
        if ny == 2:
            result.append((None, None, remote(
                y_out.at[s, 1 - my, v], y_in.at[s, my, v],
                y_send.at[0], y_recv.at[s, v, 0], "gy", 1 - my)))
        else:
            result += [
                (high_y, low_y, remote(
                    y_out.at[s, 1, v], y_in.at[s, 0, v],
                    y_send.at[0], y_recv.at[s, v, 0], "gy", up(my, ny))),
                (low_y, high_y, remote(
                    y_out.at[s, 0, v], y_in.at[s, 1, v],
                    y_send.at[1], y_recv.at[s, v, 1], "gy", down(my, ny))),
            ]
        return result

    def guarded(condition, action):
        if condition is None:
            action()
        else:
            pl.when(condition)(action)

    def start(messages):
        for sends, _, copy in messages:
            guarded(sends, copy.start)

    def arrive(messages):
        for _, gets, copy in messages:
            guarded(gets, copy.wait_recv)

    def all_sent():
        layers = cells.at[0:STAGES, :, 0:2]
        waits = [
            (high_x, remote(layers, layers, x_send.at[0], x_recv.at[0, 0, 0], "gx", up(mx, nx))),
            (low_x, remote(layers, layers, x_send.at[1], x_recv.at[0, 0, 1], "gx", down(mx, nx))),
            (None, remote(z_out, z_out, z_send.at[0], z_recv.at[0, 0, 0], "gz", up(mz, nz))),
            (None, remote(z_out, z_out, z_send.at[1], z_recv.at[0, 0, 1], "gz", down(mz, nz))),
        ]
        half = y_out.at[:, 0]
        if ny == 2:
            waits.append((None, remote(half, half, y_send.at[0], y_recv.at[0, 0, 0], "gy", 1 - my)))
        else:
            waits += [
                (high_y, remote(half, half, y_send.at[0], y_recv.at[0, 0, 0], "gy", up(my, ny))),
                (low_y, remote(half, half, y_send.at[1], y_recv.at[0, 0, 1], "gy", down(my, ny))),
            ]
        for condition, copy in waits:
            guarded(condition, copy.wait_send)

    lane = lax.broadcasted_iota(jnp.int32, (8, 128), 1)
    sublane = lax.broadcasted_iota(jnp.int32, (8, 128), 0)
    quarter = lax.shift_right_logical(lane, 2)
    lower = jnp.bitwise_and(lane, 3) < 2
    inside = jnp.where(lower, jnp.minimum(mz, 1), jnp.minimum(nz - 1 - mz, 1)) > 0

    def pack(s, v, x, value, z):
        for i in range(2):
            y_out[s, 0, v, 2 * x + i:2 * x + i + 1] = value[i, 0:1]
            y_out[s, 1, v, 2 * x + i:2 * x + i + 1] = value[tiles - 2 + i, 7:8]
        for t in range(p.tiles):
            place = x * p.tiles + t
            turned = pltpu.roll(value[t], (4 * place + 2) % 128, 1)
            z = jnp.where(quarter == place, turned, z)
        return z

    def advance(s, v, layers, z):
        edges = jnp.where(lower, z_in[s, 0, v], z_in[s, 1, v])
        edges = jnp.where(inside, edges, 0.0)
        spread = time_step * diffusivity[v]
        rates = [time_step * coupling[v, w] for w in range(nv)]
        keep = 1.0 - 6.0 * spread
        for x in layers:
            centre = cells[s, v, x + 2]
            along = [
                jnp.where(sublane == 0, y_in[s, 0, v, 2 * x + i:2 * x + i + 1],
                          pltpu.roll(centre[tiles - 2 + i], 1, 0)) for i in range(2)
            ] + [centre[t] for t in range(tiles)] + [
                jnp.where(sublane == 7, y_in[s, 1, v, 2 * x + i:2 * x + i + 1],
                          pltpu.roll(centre[i], 7, 0)) for i in range(2)
            ]
            shifted = lambda offset: jnp.stack(along[2 + offset:2 + offset + tiles])
            turned = [[], [], [], []]
            for t in range(p.tiles):
                tile = centre[t]
                beside = pltpu.roll(edges, (126 - 4 * (x * p.tiles + t)) % 128, 1)
                for i, (mask, shift) in enumerate(
                        ((lane == 0, 127), (lane == 127, 1), (lane <= 1, 126), (lane >= 126, 2))):
                    turned[i].append(pltpu.roll(jnp.where(mask, beside, tile), shift, 1))
            near = [
                (cells[s, v, x + 3], cells[s, v, x + 1], cells[s, v, x + 4], cells[s, v, x]),
                (shifted(1), shifted(-1), shifted(2), shifted(-2)),
                tuple(jnp.stack(parts) for parts in turned),
            ]
            moved = around = None
            for a, (next1, last1, next2, last2) in enumerate(near):
                flow = speed[a, x] * (8.0 * (next1 - last1) - (next2 - last2))
                both = next1 + last1
                moved = flow if moved is None else moved + flow
                around = both if around is None else around + both
            factor = keep
            for w in range(nv):
                factor = factor + rates[w] * cells[s, w, x + 2]
            new = centre * factor + moved + spread * around
            if s % 2 == 1:
                new = 0.5 * (new + cells[s - 1, v, x + 2])
            cells[s + 1, v, x + 2] = new
            if s + 1 < STAGES:
                z = pack(s + 1, v, x, new, z)
        return z

    def fetch(i, source, target):
        copy = pltpu.make_async_copy(source, target, load_sem.at[i])
        copy.start()
        return copy

    partners = [
        {"gy": lax.rem(my + dy, ny), "gz": lax.rem(mz + dz, nz)}
        for dy in range(ny) for dz in range(nz) if dy or dz
    ]
    line = [{"gx": lax.rem(mx + dx, nx)} for dx in range(1, nx)]
    barrier = pltpu.get_barrier_semaphore()
    for device in partners + line:
        pl.semaphore_signal(barrier, inc=1, device_id=device, device_id_type=MESH)
    load = fetch(0, fields, raw.at[:, 2:lx + 2])
    load_rest = [
        fetch(1, velocity, raw_speed),
        fetch(2, diffusivity_in, diffusivity),
        fetch(3, coupling_in, coupling),
        fetch(4, factor_x_in, factor_x),
        fetch(5, factor_y_in, factor_y),
        fetch(6, factor_z_in, factor_z),
    ]

    def clear(condition, ref, *index):
        @pl.when(jnp.logical_not(condition))
        def _():
            ref[index] = jnp.zeros_like(ref[index])

    for s in range(STAGES):
        edge = cells if s else raw
        lead = (s,) if s else ()
        clear(low_x, edge, *lead, slice(None), slice(0, 2))
        clear(high_x, edge, *lead, slice(None), slice(lx + 2, lx + 4))
        clear(low_y, y_in, s, 0)
        clear(high_y, y_in, s, 1)

    pl.semaphore_wait(barrier, len(partners) + len(line))

    for v in range(nv):
        start(x_messages(0, v))
    load.wait()

    blank = jnp.zeros((8, 128), jnp.float32)

    def arrange(v, x):
        for t in range(tiles):
            cells[0, v, x, t] = raw[v, x, pl.ds(t, 8, stride=tiles)]

    def first_pack(v, carry):
        z = blank
        for x in range(lx):
            arrange(v, x + 2)
            z = pack(0, v, x, cells[0, v, x + 2], z)
        z_out[0, v] = z
        start(yz_messages(0, v))
        return carry

    lax.fori_loop(0, nv, first_pack, 0)
    for copy in load_rest:
        copy.wait()

    def arrange_speed(a, carry):
        for x in range(lx):
            for t in range(tiles):
                speed[a, x, t] = raw_speed[a, x, pl.ds(t, 8, stride=tiles)] * (-time_step / 12.0)
        return carry

    lax.fori_loop(0, 3, arrange_speed, 0)

    def split(value):
        high = value.astype(jnp.bfloat16)
        return high, (value - high.astype(jnp.float32)).astype(jnp.bfloat16)

    def product(a, b, contract=((1,), (0,))):
        (a_high, a_low), (b_high, b_low) = a, b
        dot = functools.partial(
            lax.dot_general, dimension_numbers=(contract, ((), ())), preferred_element_type=jnp.float32)
        return dot(a_high, b_high) + (dot(a_high, b_low) + dot(a_low, b_high))

    chunk_y = lx * p.by
    wide_y = ny * chunk_y
    column = lax.broadcasted_iota(jnp.int32, (p.rank, wide_y), 1)
    row = lax.broadcasted_iota(jnp.int32, (p.rank, wide_y), 0)
    place_y = jnp.where(row == column // chunk_y * p.by + column % p.by, 1.0, 0.0)
    column = lax.broadcasted_iota(jnp.int32, (ly, ly), 1)
    row = lax.broadcasted_iota(jnp.int32, (ly, ly), 0)
    order = jnp.where(column == row % 8 * tiles + row // 8, 1.0, 0.0)
    ordered = jnp.dot(order, factor_y[...], precision=HIGHEST, preferred_element_type=jnp.float32)
    repeated = jnp.dot(ordered, place_y, precision=HIGHEST, preferred_element_type=jnp.float32)
    column = lax.broadcasted_iota(jnp.int32, (ly, wide_y), 1) % chunk_y // p.by
    for x in range(lx):
        for i, part in enumerate(split(jnp.where(column == x, repeated, 0.0))):
            spread_y[i, x * ly:(x + 1) * ly] = part
    chunk_x = p.ax * p.by
    wide_x = nx * chunk_x
    column = lax.broadcasted_iota(jnp.int32, (p.rank, wide_x), 1)
    row = lax.broadcasted_iota(jnp.int32, (p.rank, wide_x), 0)
    place_x = jnp.where(row == column // p.by, 1.0, 0.0)
    repeated = jnp.dot(factor_x[...], place_x, precision=HIGHEST, preferred_element_type=jnp.float32)
    column = lax.broadcasted_iota(jnp.int32, (p.by, wide_x), 1) % p.by
    row = lax.broadcasted_iota(jnp.int32, (p.by, wide_x), 0)
    for x in range(lx):
        for i, part in enumerate(split(jnp.where(column == row, repeated[x:x + 1], 0.0))):
            spread_x[i, x * p.by:(x + 1) * p.by] = part

    def plane_message(i, which):
        device = partners[i]
        return pltpu.make_async_remote_copy(
            src_ref=yz_out.at[device["gy"] * nz + device["gz"], which], dst_ref=yz_in.at[i, which],
            send_sem=yz_send.at[i], recv_sem=yz_recv.at[i],
            device_id=device, device_id_type=MESH)

    for s in range(STAGES):
        last = s == STAGES - 1

        def project(v):
            state = cells[STAGES, v, 2:lx + 2].reshape(lx * ly, p.lz)
            reduced = product(split(factor_z[...]), split(state), ((1,), (1,)))
            reduced = product(split(reduced), (spread_y[0], spread_y[1]))
            for y in range(ny):
                for z in range(nz):
                    yz_out[y * nz + z, v] = reduced[
                        z * p.cz:(z + 1) * p.cz, y * chunk_y:(y + 1) * chunk_y]

        def stage(v, carry):
            arrive(yz_messages(s, v) + x_messages(s, v))
            if s == 0:
                for x in (0, 1, lx + 2, lx + 3):
                    arrange(v, x)
            z = advance(s, v, p.edge, blank)
            if not last:
                start(x_messages(s + 1, v))
            z = advance(s, v, p.inner, z)
            if last:
                project(v)
                for i in range(len(partners)):
                    plane_message(i, v).start()
            else:
                z_out[s + 1, v] = z
                start(yz_messages(s + 1, v))
            return carry

        lax.fori_loop(0, nv, stage, 0)

    plane = [plane_message(i, slice(None)) for i in range(len(partners))]
    total = yz_out[my * nz + mz]
    for i, copy in enumerate(plane):
        copy.wait_recv()
        total = total + yz_in[i]

    total = total.reshape(nv * p.cz, chunk_y)
    total = product(split(total), (spread_x[0], spread_x[1]))
    for x in range(nx):
        x_out[x] = total[:, x * chunk_x:(x + 1) * chunk_x].reshape(nv, p.cz, chunk_x)
    along = []
    for i, device in enumerate(line):
        along.append(pltpu.make_async_remote_copy(
            src_ref=x_out.at[device["gx"]], dst_ref=x_in.at[i],
            send_sem=xs_send.at[i], recv_sem=xs_recv.at[i],
            device_id=device, device_id_type=MESH))
        along[-1].start()
    total = x_out[mx]
    for i, copy in enumerate(along):
        copy.wait_recv()
        total = total + x_in[i]
    for a in range(p.ax):
        out[:, a] = total[:, :, a * p.by:(a + 1) * p.by]

    all_sent()
    for copy in plane + along:
        copy.wait_send()


def local_kernel(plan, fields, velocity, diffusivity, coupling, factor_x, factor_y, factor_z):
    p = plan
    nv, lx, ly = p.vars, p.lx, p.ly
    chunk_y, chunk_x = lx * p.by, p.ax * p.by
    others = p.ny * p.nz - 1
    vmem = lambda *shape: pltpu.VMEM(shape, jnp.float32)
    dma = lambda *shape: pltpu.SemaphoreType.DMA(shape)
    whole = pl.BlockSpec(memory_space=pltpu.VMEM)
    result = pl.pallas_call(
        functools.partial(kernel, p),
        out_shape=pltpu.VMEM((nv, p.ax, p.cz, p.by), jnp.float32),
        in_specs=[pl.BlockSpec(memory_space=pl.ANY)] * 7,
        out_specs=whole,
        scratch_shapes=[
            pltpu.SMEM(diffusivity.shape, jnp.float32),
            pltpu.SMEM(coupling.shape, jnp.float32),
            vmem(*factor_x.shape),
            vmem(*factor_y.shape),
            vmem(*factor_z.shape[::-1]),
            vmem(nv, lx + 4, ly, p.lz),
            vmem(3, lx, ly, p.lz),
            vmem(STAGES + 1, nv, lx + 4, p.tiles, 8, p.lz),
            vmem(3, lx, p.tiles, 8, p.lz),
            vmem(STAGES, 2, nv, 8 * -(-lx // 4), p.lz),
            vmem(STAGES, 2, nv, 8 * -(-lx // 4), p.lz),
            vmem(STAGES, nv, 8, 128),
            vmem(STAGES, 2, nv, 8, 128),
            pltpu.VMEM((2, lx * ly, p.ny * chunk_y), jnp.bfloat16),
            pltpu.VMEM((2, chunk_y, p.nx * chunk_x), jnp.bfloat16),
            vmem(p.ny * p.nz, nv, p.cz, chunk_y),
            vmem(others, nv, p.cz, chunk_y),
            vmem(p.nx, nv, p.cz, chunk_x),
            vmem(p.nx - 1, nv, p.cz, chunk_x),
            dma(7),
            dma(2), dma(STAGES, nv, 2),
            dma(2), dma(STAGES, nv, 2),
            dma(2), dma(STAGES, nv, 2),
            dma(others), dma(others),
            dma(p.nx - 1), dma(p.nx - 1),
        ],
        compiler_params=pltpu.CompilerParams(
            collective_id=0, has_side_effects=True, vmem_limit_bytes=VMEM_LIMIT),
    )(fields, velocity, diffusivity, coupling, factor_x, factor_y, factor_z.T)
    return jnp.transpose(result, (0, 1, 3, 2))


def solution(mesh):
    def local(fields, velocity, diffusivity, coupling, factor_x, factor_y, factor_z):
        plan = Plan(mesh.shape, fields.shape, factor_x.shape)
        run = functools.partial(local_kernel, plan) if plan.fits() else local_plain
        return run(fields, velocity, diffusivity, coupling, factor_x, factor_y, factor_z)

    return jax.shard_map(
        local,
        mesh=mesh,
        in_specs=(
            P(None, "gx", "gy", "gz"),
            P(None, "gx", "gy", "gz"),
            P(),
            P(),
            P("gx", None),
            P("gy", None),
            P("gz", None),
        ),
        out_specs=P(None, "gx", "gy", "gz"),
        check_vma=False,
    )
```

```python
import functools
import jax
import jax.numpy as jnp
from jax import lax
from jax.experimental import pallas as pl
from jax.experimental.pallas import tpu as pltpu
from jax.sharding import PartitionSpec as P

STEPS = 2
STAGES = 2 * STEPS
HALO = 2
GROUP = 2
VMEM_LIMIT = 66 * 1000 * 1000
MESH = pl.DeviceIdType.MESH
HIGHEST = lax.Precision.HIGHEST


time_step = 0.2
def with_halo(cells, sides, width):
    for axis, dim in sides:
        count = lax.axis_size(axis)
        ends = count - 1
        head = lax.slice_in_dim(cells, 0, width, axis=dim)
        tail = lax.slice_in_dim(cells, cells.shape[dim] - width, cells.shape[dim], axis=dim)
        cells = jnp.concatenate(
            [
                lax.ppermute(tail, axis, [(i, (i + 1) % count) for i in range(ends)]),
                cells,
                lax.ppermute(head, axis, [((i + 1) % count, i) for i in range(ends)]),
            ],
            axis=dim,
        )
    return cells


def offset_view(padded, dimension, offset):
    indices = [slice(None)]
    for other in (1, 2, 3):
        if other == dimension:
            first_cell = 2 + offset
            indices.append(slice(first_cell, first_cell + padded.shape[other] - 4))
        else:
            indices.append(slice(2, padded.shape[other] - 2))
    return padded[tuple(indices)]


def tendency(padded, velocity, diffusivity, coupling):
    center = offset_view(padded, 1, 0)
    transport = jnp.zeros_like(center)
    laplace = jnp.zeros_like(center)
    for dimension in (1, 2, 3):
        gradient = (
            8.0 * (offset_view(padded, dimension, 1) - offset_view(padded, dimension, -1))
            - (offset_view(padded, dimension, 2) - offset_view(padded, dimension, -2))
        ) / 12.0
        transport = transport + velocity[dimension - 1][None] * gradient
        laplace = (
            laplace
            + offset_view(padded, dimension, 1)
            + offset_view(padded, dimension, -1)
            - 2.0 * center
        )
    mixing = jnp.einsum("vw,wxyz->vxyz", coupling, center, precision=lax.Precision.HIGHEST)
    return -transport + diffusivity[:, None, None, None] * laplace + center * mixing


def with_edges(values):
    return with_halo(values, (("gx", 1), ("gy", 2), ("gz", 3)), 2)


def local_plain(fields, velocity, diffusivity, coupling, factor_x, factor_y, factor_z):
    state = fields
    for repeat in range(STEPS):
        section = state + time_step * tendency(with_edges(state), velocity, diffusivity, coupling)
        state = 0.5 * (
            state
            + section
            + time_step * tendency(with_edges(section), velocity, diffusivity, coupling)
        )
    highest = lax.Precision.HIGHEST
    partial_value = jnp.einsum("vxyz,zc->vxyc", state, factor_z, precision=highest)
    partial_value = lax.psum_scatter(partial_value, "gz", scatter_dimension=3, tiled=True)
    partial_value = jnp.einsum("vxyc,yb->vxbc", partial_value, factor_y, precision=highest)
    partial_value = lax.psum_scatter(partial_value, "gy", scatter_dimension=2, tiled=True)
    partial_value = jnp.einsum("vxbc,xa->vabc", partial_value, factor_x, precision=highest)
    core_tensor = lax.psum_scatter(partial_value, "gx", scatter_dimension=1, tiled=True)
    return core_tensor


class Plan:
    def __init__(self, mesh_shape, fields, factor_x):
        self.nx, self.ny, self.nz = (mesh_shape[a] for a in ("gx", "gy", "gz"))
        self.vars, self.lx, self.ly, self.lz = fields
        self.rank = factor_x[1]
        self.ax, self.by, self.cz = self.rank // self.nx, self.rank // self.ny, self.rank // self.nz
        self.edge = [0, 1, self.lx - 2, self.lx - 1]
        self.inner = list(range(2, self.lx - 2))
        self.tiles = self.ly // 8

    def fits(self):
        return (
            self.lz == 128
            and self.ly % 8 == 0
            and self.ly >= 16
            and min(self.nx, self.ny, self.nz) > 1
            and self.vars % GROUP == 0
            and self.lx > 4
            and self.lx * self.tiles * 4 <= 128
            and self.rank % self.nx == 0 and self.rank % self.ny == 0 and self.rank % self.nz == 0
            and self.cz % 8 == 0
            and self.lx * self.by % 128 == 0
            and self.ax * self.by % 128 == 0
        )


def kernel(
    plan,
    fields,
    velocity,
    diffusivity_in,
    coupling_in,
    factor_x_in,
    factor_y_in,
    factor_z_in,
    out,
    diffusivity,
    coupling,
    factor_x,
    factor_y,
    factor_z,
    raw,
    raw_speed,
    cells,
    speed,
    y_out,
    y_in,
    z_out,
    z_in,
    spread_y,
    spread_x,
    yz_out,
    yz_in,
    x_out,
    x_in,
    load_sem,
    x_send,
    x_recv,
    y_send,
    y_recv,
    z_send,
    z_recv,
    yz_send,
    yz_recv,
    xs_send,
    xs_recv,
):
    p = plan
    nx, ny, nz = p.nx, p.ny, p.nz
    lx, ly, nv = p.lx, p.ly, p.vars
    mx, my, mz = lax.axis_index("gx"), lax.axis_index("gy"), lax.axis_index("gz")
    tiles = p.tiles
    low_x, high_x = mx > 0, mx < nx - 1
    low_y, high_y = my > 0, my < ny - 1
    low_z, high_z = mz > 0, mz < nz - 1

    def remote(src, dst, send, recv, axis, to):
        return pltpu.make_async_remote_copy(
            src_ref=src, dst_ref=dst, send_sem=send, recv_sem=recv,
            device_id={axis: to}, device_id_type=MESH,
        )

    def up(index, count):
        return lax.rem(index + 1, count)

    def down(index, count):
        return lax.rem(index + count - 1, count)

    def x_messages(s, c):
        v = pl.ds(c * GROUP, GROUP)
        if s == 0:
            top, bottom = fields.at[v, lx - 2:lx], fields.at[v, 0:2]
            below, above = raw.at[v, 0:2], raw.at[v, lx + 2:lx + 4]
        else:
            top, bottom = cells.at[s, v, lx:lx + 2], cells.at[s, v, 2:4]
            below, above = cells.at[s, v, 0:2], cells.at[s, v, lx + 2:lx + 4]
        return [
            (high_x, low_x, remote(
                top, below, x_send.at[0], x_recv.at[s, c, 0], "gx", up(mx, nx))),
            (low_x, high_x, remote(
                bottom, above, x_send.at[1], x_recv.at[s, c, 1], "gx", down(mx, nx))),
        ]

    def yz_messages(s, c):
        v = pl.ds(c * GROUP, GROUP)
        result = [
            (None, None, remote(
                z_out.at[s, v], z_in.at[s, 0, v],
                z_send.at[0], z_recv.at[s, c, 0], "gz", up(mz, nz))),
            (None, None, remote(
                z_out.at[s, v], z_in.at[s, 1, v],
                z_send.at[1], z_recv.at[s, c, 1], "gz", down(mz, nz))),
        ]
        if ny == 2:
            result.append((None, None, remote(
                y_out.at[s, 1 - my, v], y_in.at[s, my, v],
                y_send.at[0], y_recv.at[s, c, 0], "gy", 1 - my)))
        else:
            result += [
                (high_y, low_y, remote(
                    y_out.at[s, 1, v], y_in.at[s, 0, v],
                    y_send.at[0], y_recv.at[s, c, 0], "gy", up(my, ny))),
                (low_y, high_y, remote(
                    y_out.at[s, 0, v], y_in.at[s, 1, v],
                    y_send.at[1], y_recv.at[s, c, 1], "gy", down(my, ny))),
            ]
        return result

    def guarded(condition, action):
        if condition is None:
            action()
        else:
            pl.when(condition)(action)

    def start(messages):
        for sends, _, copy in messages:
            guarded(sends, copy.start)

    def arrive(messages):
        for _, gets, copy in messages:
            guarded(gets, copy.wait_recv)

    def all_sent():
        layers = cells.at[0:STAGES, :, 0:2]
        waits = [
            (high_x, remote(layers, layers, x_send.at[0], x_recv.at[0, 0, 0], "gx", up(mx, nx))),
            (low_x, remote(layers, layers, x_send.at[1], x_recv.at[0, 0, 1], "gx", down(mx, nx))),
            (None, remote(z_out, z_out, z_send.at[0], z_recv.at[0, 0, 0], "gz", up(mz, nz))),
            (None, remote(z_out, z_out, z_send.at[1], z_recv.at[0, 0, 1], "gz", down(mz, nz))),
        ]
        half = y_out.at[:, 0]
        if ny == 2:
            waits.append((None, remote(half, half, y_send.at[0], y_recv.at[0, 0, 0], "gy", 1 - my)))
        else:
            waits += [
                (high_y, remote(half, half, y_send.at[0], y_recv.at[0, 0, 0], "gy", up(my, ny))),
                (low_y, remote(half, half, y_send.at[1], y_recv.at[0, 0, 1], "gy", down(my, ny))),
            ]
        for condition, copy in waits:
            guarded(condition, copy.wait_send)

    lane = lax.broadcasted_iota(jnp.int32, (8, 128), 1)
    sublane = lax.broadcasted_iota(jnp.int32, (8, 128), 0)
    quarter = lax.shift_right_logical(lane, 2)
    lower = jnp.bitwise_and(lane, 3) < 2
    inside = jnp.where(lower, jnp.minimum(mz, 1), jnp.minimum(nz - 1 - mz, 1)) > 0

    def pack(s, v, x, value, z):
        for i in range(2):
            y_out[s, 0, v, 2 * x + i:2 * x + i + 1] = value[i, 0:1]
            y_out[s, 1, v, 2 * x + i:2 * x + i + 1] = value[tiles - 2 + i, 7:8]
        for t in range(p.tiles):
            place = x * p.tiles + t
            turned = pltpu.roll(value[t], (4 * place + 2) % 128, 1)
            z = jnp.where(quarter == place, turned, z)
        return z

    def advance(s, c, layers, packed):
        packed = list(packed)
        variables = [c * GROUP + i for i in range(GROUP)]
        terms = [coefficients(s, v) for v in variables]
        ready = []
        for x in layers:
            values = [cells[s, w, x + 2] for w in range(nv)]
            speeds = [speed[a, x] for a in range(3)]
            for i, v in enumerate(variables):
                ready.append((i, v, x, advance_layer(s, v, x, terms[i], values, speeds)))
        for i, v, x, new in ready:
            cells[s + 1, v, x + 2] = new
            if s + 1 < STAGES:
                packed[i] = pack(s + 1, v, x, new, packed[i])
        return packed

    def coefficients(s, v):
        edges = jnp.where(lower, z_in[s, 0, v], z_in[s, 1, v])
        edges = jnp.where(inside, edges, 0.0)
        spread = time_step * diffusivity[v]
        rates = [time_step * coupling[v, w] for w in range(nv)]
        return edges, spread, rates, 1.0 - 6.0 * spread

    def advance_layer(s, v, x, term, values, speeds):
        edges, spread, rates, keep = term
        centre = cells[s, v, x + 2]
        along = [
            jnp.where(sublane == 0, y_in[s, 0, v, 2 * x + i:2 * x + i + 1],
                      pltpu.roll(centre[tiles - 2 + i], 1, 0)) for i in range(2)
        ] + [centre[t] for t in range(tiles)] + [
            jnp.where(sublane == 7, y_in[s, 1, v, 2 * x + i:2 * x + i + 1],
                      pltpu.roll(centre[i], 7, 0)) for i in range(2)
        ]
        shifted = lambda offset: jnp.stack(along[2 + offset:2 + offset + tiles])
        turned = [[], [], [], []]
        for t in range(p.tiles):
            tile = centre[t]
            beside = pltpu.roll(edges, (126 - 4 * (x * p.tiles + t)) % 128, 1)
            for i, (mask, shift) in enumerate(
                    ((lane == 0, 127), (lane == 127, 1), (lane <= 1, 126), (lane >= 126, 2))):
                turned[i].append(pltpu.roll(jnp.where(mask, beside, tile), shift, 1))
        near = [
            (cells[s, v, x + 3], cells[s, v, x + 1], cells[s, v, x + 4], cells[s, v, x]),
            (shifted(1), shifted(-1), shifted(2), shifted(-2)),
            tuple(jnp.stack(parts) for parts in turned),
        ]
        moved = around = None
        for a, (next1, last1, next2, last2) in enumerate(near):
            flow = speeds[a] * (8.0 * (next1 - last1) - (next2 - last2))
            both = next1 + last1
            moved = flow if moved is None else moved + flow
            around = both if around is None else around + both
        factor = keep
        for w in range(nv):
            factor = factor + rates[w] * values[w]
        new = centre * factor + moved + spread * around
        if s % 2 == 1:
            new = 0.5 * (new + cells[s - 1, v, x + 2])
        return new

    def fetch(i, source, target):
        copy = pltpu.make_async_copy(source, target, load_sem.at[i])
        copy.start()
        return copy

    partners = [
        {"gy": lax.rem(my + dy, ny), "gz": lax.rem(mz + dz, nz)}
        for dy in range(ny) for dz in range(nz) if dy or dz
    ]
    line = [{"gx": lax.rem(mx + dx, nx)} for dx in range(1, nx)]
    barrier = pltpu.get_barrier_semaphore()
    for device in partners + line:
        pl.semaphore_signal(barrier, inc=1, device_id=device, device_id_type=MESH)
    load = fetch(0, fields, raw.at[:, 2:lx + 2])
    load_rest = [
        fetch(1, velocity, raw_speed),
        fetch(2, diffusivity_in, diffusivity),
        fetch(3, coupling_in, coupling),
        fetch(4, factor_x_in, factor_x),
        fetch(5, factor_y_in, factor_y),
        fetch(6, factor_z_in, factor_z),
    ]

    def clear(condition, ref, *index):
        @pl.when(jnp.logical_not(condition))
        def _():
            ref[index] = jnp.zeros_like(ref[index])

    for s in range(STAGES):
        edge = cells if s else raw
        lead = (s,) if s else ()
        clear(low_x, edge, *lead, slice(None), slice(0, 2))
        clear(high_x, edge, *lead, slice(None), slice(lx + 2, lx + 4))
        clear(low_y, y_in, s, 0)
        clear(high_y, y_in, s, 1)

    pl.semaphore_wait(barrier, len(partners) + len(line))

    for c in range(nv // GROUP):
        start(x_messages(0, c))
    load.wait()

    blank = jnp.zeros((8, 128), jnp.float32)

    def arrange(v, x):
        for t in range(tiles):
            cells[0, v, x, t] = raw[v, x, pl.ds(t, 8, stride=tiles)]

    def first_pack(c, carry):
        for v in (c * GROUP + i for i in range(GROUP)):
            z = blank
            for x in range(lx):
                arrange(v, x + 2)
                z = pack(0, v, x, cells[0, v, x + 2], z)
            z_out[0, v] = z
        start(yz_messages(0, c))
        return carry

    lax.fori_loop(0, nv // GROUP, first_pack, 0)
    for copy in load_rest:
        copy.wait()

    def arrange_speed(a, carry):
        for x in range(lx):
            for t in range(tiles):
                speed[a, x, t] = raw_speed[a, x, pl.ds(t, 8, stride=tiles)] * (-time_step / 12.0)
        return carry

    lax.fori_loop(0, 3, arrange_speed, 0)

    def split(value):
        high = value.astype(jnp.bfloat16)
        return high, (value - high.astype(jnp.float32)).astype(jnp.bfloat16)

    def product(a, b, contract=((1,), (0,))):
        (a_high, a_low), (b_high, b_low) = a, b
        dot = functools.partial(
            lax.dot_general, dimension_numbers=(contract, ((), ())), preferred_element_type=jnp.float32)
        return dot(a_high, b_high) + (dot(a_high, b_low) + dot(a_low, b_high))

    chunk_y = lx * p.by
    wide_y = ny * chunk_y
    column = lax.broadcasted_iota(jnp.int32, (p.rank, wide_y), 1)
    row = lax.broadcasted_iota(jnp.int32, (p.rank, wide_y), 0)
    place_y = jnp.where(row == column // chunk_y * p.by + column % p.by, 1.0, 0.0)
    column = lax.broadcasted_iota(jnp.int32, (ly, ly), 1)
    row = lax.broadcasted_iota(jnp.int32, (ly, ly), 0)
    order = jnp.where(column == row % 8 * tiles + row // 8, 1.0, 0.0)
    ordered = jnp.dot(order, factor_y[...], precision=HIGHEST, preferred_element_type=jnp.float32)
    repeated = jnp.dot(ordered, place_y, precision=HIGHEST, preferred_element_type=jnp.float32)
    column = lax.broadcasted_iota(jnp.int32, (ly, wide_y), 1) % chunk_y // p.by
    for x in range(lx):
        for i, part in enumerate(split(jnp.where(column == x, repeated, 0.0))):
            spread_y[i, x * ly:(x + 1) * ly] = part
    chunk_x = p.ax * p.by
    wide_x = nx * chunk_x
    column = lax.broadcasted_iota(jnp.int32, (p.rank, wide_x), 1)
    row = lax.broadcasted_iota(jnp.int32, (p.rank, wide_x), 0)
    place_x = jnp.where(row == column // p.by, 1.0, 0.0)
    repeated = jnp.dot(factor_x[...], place_x, precision=HIGHEST, preferred_element_type=jnp.float32)
    column = lax.broadcasted_iota(jnp.int32, (p.by, wide_x), 1) % p.by
    row = lax.broadcasted_iota(jnp.int32, (p.by, wide_x), 0)
    for x in range(lx):
        for i, part in enumerate(split(jnp.where(column == row, repeated[x:x + 1], 0.0))):
            spread_x[i, x * p.by:(x + 1) * p.by] = part

    def plane_message(i, which):
        device = partners[i]
        return pltpu.make_async_remote_copy(
            src_ref=yz_out.at[device["gy"] * nz + device["gz"], which], dst_ref=yz_in.at[i, which],
            send_sem=yz_send.at[i], recv_sem=yz_recv.at[i],
            device_id=device, device_id_type=MESH)

    for s in range(STAGES):
        last = s == STAGES - 1

        def project(v):
            state = cells[STAGES, v, 2:lx + 2].reshape(lx * ly, p.lz)
            reduced = product(split(factor_z[...]), split(state), ((1,), (1,)))
            reduced = product(split(reduced), (spread_y[0], spread_y[1]))
            for y in range(ny):
                for z in range(nz):
                    yz_out[y * nz + z, v] = reduced[
                        z * p.cz:(z + 1) * p.cz, y * chunk_y:(y + 1) * chunk_y]

        def stage(c, carry):
            variables = [c * GROUP + i for i in range(GROUP)]
            arrive(yz_messages(s, c) + x_messages(s, c))
            if s == 0:
                for v in variables:
                    for x in (0, 1, lx + 2, lx + 3):
                        arrange(v, x)
            packed = advance(s, c, p.edge, [blank] * GROUP)
            if not last:
                start(x_messages(s + 1, c))
            packed = advance(s, c, p.inner, packed)
            if last:
                for v in variables:
                    project(v)
                for i in range(len(partners)):
                    plane_message(i, pl.ds(c * GROUP, GROUP)).start()
            else:
                for v, z in zip(variables, packed):
                    z_out[s + 1, v] = z
                start(yz_messages(s + 1, c))
            return carry

        lax.fori_loop(0, nv // GROUP, stage, 0)

    plane = [plane_message(i, slice(None)) for i in range(len(partners))]
    total = yz_out[my * nz + mz]
    for i, copy in enumerate(plane):
        copy.wait_recv()
        total = total + yz_in[i]

    total = total.reshape(nv * p.cz, chunk_y)
    total = product(split(total), (spread_x[0], spread_x[1]))
    for x in range(nx):
        x_out[x] = total[:, x * chunk_x:(x + 1) * chunk_x].reshape(nv, p.cz, chunk_x)
    along = []
    for i, device in enumerate(line):
        along.append(pltpu.make_async_remote_copy(
            src_ref=x_out.at[device["gx"]], dst_ref=x_in.at[i],
            send_sem=xs_send.at[i], recv_sem=xs_recv.at[i],
            device_id=device, device_id_type=MESH))
        along[-1].start()
    total = x_out[mx]
    for i, copy in enumerate(along):
        copy.wait_recv()
        total = total + x_in[i]
    for a in range(p.ax):
        out[:, a] = total[:, :, a * p.by:(a + 1) * p.by]

    all_sent()
    for copy in plane + along:
        copy.wait_send()


def local_kernel(plan, fields, velocity, diffusivity, coupling, factor_x, factor_y, factor_z):
    p = plan
    nv, lx, ly = p.vars, p.lx, p.ly
    chunk_y, chunk_x = lx * p.by, p.ax * p.by
    others = p.ny * p.nz - 1
    vmem = lambda *shape: pltpu.VMEM(shape, jnp.float32)
    dma = lambda *shape: pltpu.SemaphoreType.DMA(shape)
    whole = pl.BlockSpec(memory_space=pltpu.VMEM)
    result = pl.pallas_call(
        functools.partial(kernel, p),
        out_shape=pltpu.VMEM((nv, p.ax, p.cz, p.by), jnp.float32),
        in_specs=[pl.BlockSpec(memory_space=pl.ANY)] * 7,
        out_specs=whole,
        scratch_shapes=[
            pltpu.SMEM(diffusivity.shape, jnp.float32),
            pltpu.SMEM(coupling.shape, jnp.float32),
            vmem(*factor_x.shape),
            vmem(*factor_y.shape),
            vmem(*factor_z.shape[::-1]),
            vmem(nv, lx + 4, ly, p.lz),
            vmem(3, lx, ly, p.lz),
            vmem(STAGES + 1, nv, lx + 4, p.tiles, 8, p.lz),
            vmem(3, lx, p.tiles, 8, p.lz),
            vmem(STAGES, 2, nv, 8 * -(-lx // 4), p.lz),
            vmem(STAGES, 2, nv, 8 * -(-lx // 4), p.lz),
            vmem(STAGES, nv, 8, 128),
            vmem(STAGES, 2, nv, 8, 128),
            pltpu.VMEM((2, lx * ly, p.ny * chunk_y), jnp.bfloat16),
            pltpu.VMEM((2, chunk_y, p.nx * chunk_x), jnp.bfloat16),
            vmem(p.ny * p.nz, nv, p.cz, chunk_y),
            vmem(others, nv, p.cz, chunk_y),
            vmem(p.nx, nv, p.cz, chunk_x),
            vmem(p.nx - 1, nv, p.cz, chunk_x),
            dma(7),
            dma(2), dma(STAGES, nv, 2),
            dma(2), dma(STAGES, nv, 2),
            dma(2), dma(STAGES, nv, 2),
            dma(others), dma(others),
            dma(p.nx - 1), dma(p.nx - 1),
        ],
        compiler_params=pltpu.CompilerParams(
            collective_id=0, has_side_effects=True, vmem_limit_bytes=VMEM_LIMIT),
    )(fields, velocity, diffusivity, coupling, factor_x, factor_y, factor_z.T)
    return jnp.transpose(result, (0, 1, 3, 2))


def solution(mesh):
    def local(fields, velocity, diffusivity, coupling, factor_x, factor_y, factor_z):
        plan = Plan(mesh.shape, fields.shape, factor_x.shape)
        run = functools.partial(local_kernel, plan) if plan.fits() else local_plain
        return run(fields, velocity, diffusivity, coupling, factor_x, factor_y, factor_z)

    return jax.shard_map(
        local,
        mesh=mesh,
        in_specs=(
            P(None, "gx", "gy", "gz"),
            P(None, "gx", "gy", "gz"),
            P(),
            P(),
            P("gx", None),
            P("gy", None),
            P("gz", None),
        ),
        out_specs=P(None, "gx", "gy", "gz"),
        check_vma=False,
    )
```

```python
import functools
import jax
import jax.numpy as jnp
from jax import lax
from jax.experimental import pallas as pl
from jax.experimental.pallas import tpu as pltpu
from jax.sharding import PartitionSpec as P

STEPS = 2
STAGES = 2 * STEPS
HALO = 2
GROUP = 1
VMEM_LIMIT = 66 * 1000 * 1000
MESH = pl.DeviceIdType.MESH
HIGHEST = lax.Precision.HIGHEST


time_step = 0.2
def with_halo(cells, sides, width):
    for axis, dim in sides:
        count = lax.axis_size(axis)
        ends = count - 1
        head = lax.slice_in_dim(cells, 0, width, axis=dim)
        tail = lax.slice_in_dim(cells, cells.shape[dim] - width, cells.shape[dim], axis=dim)
        cells = jnp.concatenate(
            [
                lax.ppermute(tail, axis, [(i, (i + 1) % count) for i in range(ends)]),
                cells,
                lax.ppermute(head, axis, [((i + 1) % count, i) for i in range(ends)]),
            ],
            axis=dim,
        )
    return cells


def offset_view(padded, dimension, offset):
    indices = [slice(None)]
    for other in (1, 2, 3):
        if other == dimension:
            first_cell = 2 + offset
            indices.append(slice(first_cell, first_cell + padded.shape[other] - 4))
        else:
            indices.append(slice(2, padded.shape[other] - 2))
    return padded[tuple(indices)]


def tendency(padded, velocity, diffusivity, coupling):
    center = offset_view(padded, 1, 0)
    transport = jnp.zeros_like(center)
    laplace = jnp.zeros_like(center)
    for dimension in (1, 2, 3):
        gradient = (
            8.0 * (offset_view(padded, dimension, 1) - offset_view(padded, dimension, -1))
            - (offset_view(padded, dimension, 2) - offset_view(padded, dimension, -2))
        ) / 12.0
        transport = transport + velocity[dimension - 1][None] * gradient
        laplace = (
            laplace
            + offset_view(padded, dimension, 1)
            + offset_view(padded, dimension, -1)
            - 2.0 * center
        )
    mixing = jnp.einsum("vw,wxyz->vxyz", coupling, center, precision=lax.Precision.HIGHEST)
    return -transport + diffusivity[:, None, None, None] * laplace + center * mixing


def with_edges(values):
    return with_halo(values, (("gx", 1), ("gy", 2), ("gz", 3)), 2)


def local_plain(fields, velocity, diffusivity, coupling, factor_x, factor_y, factor_z):
    state = fields
    for repeat in range(STEPS):
        section = state + time_step * tendency(with_edges(state), velocity, diffusivity, coupling)
        state = 0.5 * (
            state
            + section
            + time_step * tendency(with_edges(section), velocity, diffusivity, coupling)
        )
    highest = lax.Precision.HIGHEST
    partial_value = jnp.einsum("vxyz,zc->vxyc", state, factor_z, precision=highest)
    partial_value = lax.psum_scatter(partial_value, "gz", scatter_dimension=3, tiled=True)
    partial_value = jnp.einsum("vxyc,yb->vxbc", partial_value, factor_y, precision=highest)
    partial_value = lax.psum_scatter(partial_value, "gy", scatter_dimension=2, tiled=True)
    partial_value = jnp.einsum("vxbc,xa->vabc", partial_value, factor_x, precision=highest)
    core_tensor = lax.psum_scatter(partial_value, "gx", scatter_dimension=1, tiled=True)
    return core_tensor


class Plan:
    def __init__(self, mesh_shape, fields, factor_x):
        self.nx, self.ny, self.nz = (mesh_shape[a] for a in ("gx", "gy", "gz"))
        self.vars, self.lx, self.ly, self.lz = fields
        self.rank = factor_x[1]
        self.ax, self.by, self.cz = self.rank // self.nx, self.rank // self.ny, self.rank // self.nz
        self.edge = [0, 1, self.lx - 2, self.lx - 1]
        self.inner = list(range(2, self.lx - 2))
        self.tiles = self.ly // 8

    def fits(self):
        return (
            self.lz == 128
            and self.ly % 8 == 0
            and self.ly >= 16
            and min(self.nx, self.ny, self.nz) > 1
            and self.vars % GROUP == 0
            and self.lx > 4
            and self.lx * self.tiles * 4 <= 128
            and self.rank % self.nx == 0 and self.rank % self.ny == 0 and self.rank % self.nz == 0
            and self.cz % 8 == 0
            and self.lx * self.by % 128 == 0
            and self.ax * self.by % 128 == 0
        )


def kernel(
    plan,
    fields,
    velocity,
    diffusivity_in,
    coupling_in,
    factor_x_in,
    factor_y_in,
    factor_z_in,
    out,
    diffusivity,
    coupling,
    factor_x,
    factor_y,
    factor_z,
    raw,
    raw_speed,
    cells,
    speed,
    y_out,
    y_in,
    z_out,
    z_in,
    spread_y,
    spread_x,
    yz_out,
    yz_in,
    x_out,
    x_in,
    load_sem,
    x_send,
    x_recv,
    y_send,
    y_recv,
    z_send,
    z_recv,
    yz_send,
    yz_recv,
    xs_send,
    xs_recv,
):
    p = plan
    nx, ny, nz = p.nx, p.ny, p.nz
    lx, ly, nv = p.lx, p.ly, p.vars
    mx, my, mz = lax.axis_index("gx"), lax.axis_index("gy"), lax.axis_index("gz")
    tiles = p.tiles
    low_x, high_x = mx > 0, mx < nx - 1
    low_y, high_y = my > 0, my < ny - 1
    low_z, high_z = mz > 0, mz < nz - 1

    def remote(src, dst, send, recv, axis, to):
        return pltpu.make_async_remote_copy(
            src_ref=src, dst_ref=dst, send_sem=send, recv_sem=recv,
            device_id={axis: to}, device_id_type=MESH,
        )

    def up(index, count):
        return lax.rem(index + 1, count)

    def down(index, count):
        return lax.rem(index + count - 1, count)

    def x_messages(s, c):
        v = pl.ds(c * GROUP, GROUP)
        if s == 0:
            top, bottom = fields.at[v, lx - 2:lx], fields.at[v, 0:2]
            below, above = raw.at[v, 0:2], raw.at[v, lx + 2:lx + 4]
        else:
            top, bottom = cells.at[s, v, lx:lx + 2], cells.at[s, v, 2:4]
            below, above = cells.at[s, v, 0:2], cells.at[s, v, lx + 2:lx + 4]
        return [
            (high_x, low_x, remote(
                top, below, x_send.at[0], x_recv.at[s, c, 0], "gx", up(mx, nx))),
            (low_x, high_x, remote(
                bottom, above, x_send.at[1], x_recv.at[s, c, 1], "gx", down(mx, nx))),
        ]

    def yz_messages(s, c):
        v = pl.ds(c * GROUP, GROUP)
        result = [
            (None, None, remote(
                z_out.at[s, v], z_in.at[s, 0, v],
                z_send.at[0], z_recv.at[s, c, 0], "gz", up(mz, nz))),
            (None, None, remote(
                z_out.at[s, v], z_in.at[s, 1, v],
                z_send.at[1], z_recv.at[s, c, 1], "gz", down(mz, nz))),
        ]
        if ny == 2:
            result.append((None, None, remote(
                y_out.at[s, 1 - my, v], y_in.at[s, my, v],
                y_send.at[0], y_recv.at[s, c, 0], "gy", 1 - my)))
        else:
            result += [
                (high_y, low_y, remote(
                    y_out.at[s, 1, v], y_in.at[s, 0, v],
                    y_send.at[0], y_recv.at[s, c, 0], "gy", up(my, ny))),
                (low_y, high_y, remote(
                    y_out.at[s, 0, v], y_in.at[s, 1, v],
                    y_send.at[1], y_recv.at[s, c, 1], "gy", down(my, ny))),
            ]
        return result

    def guarded(condition, action):
        if condition is None:
            action()
        else:
            pl.when(condition)(action)

    def start(messages):
        for sends, _, copy in messages:
            guarded(sends, copy.start)

    def arrive(messages):
        for _, gets, copy in messages:
            guarded(gets, copy.wait_recv)

    def all_sent():
        layers = cells.at[0:STAGES, :, 0:2]
        waits = [
            (high_x, remote(layers, layers, x_send.at[0], x_recv.at[0, 0, 0], "gx", up(mx, nx))),
            (low_x, remote(layers, layers, x_send.at[1], x_recv.at[0, 0, 1], "gx", down(mx, nx))),
            (None, remote(z_out, z_out, z_send.at[0], z_recv.at[0, 0, 0], "gz", up(mz, nz))),
            (None, remote(z_out, z_out, z_send.at[1], z_recv.at[0, 0, 1], "gz", down(mz, nz))),
        ]
        half = y_out.at[:, 0]
        if ny == 2:
            waits.append((None, remote(half, half, y_send.at[0], y_recv.at[0, 0, 0], "gy", 1 - my)))
        else:
            waits += [
                (high_y, remote(half, half, y_send.at[0], y_recv.at[0, 0, 0], "gy", up(my, ny))),
                (low_y, remote(half, half, y_send.at[1], y_recv.at[0, 0, 1], "gy", down(my, ny))),
            ]
        for condition, copy in waits:
            guarded(condition, copy.wait_send)

    lane = lax.broadcasted_iota(jnp.int32, (8, 128), 1)
    sublane = lax.broadcasted_iota(jnp.int32, (8, 128), 0)
    quarter = lax.shift_right_logical(lane, 2)
    lower = jnp.bitwise_and(lane, 3) < 2
    inside = jnp.where(lower, jnp.minimum(mz, 1), jnp.minimum(nz - 1 - mz, 1)) > 0

    def pack(s, v, x, value, z):
        for i in range(2):
            y_out[s, 0, v, 2 * x + i:2 * x + i + 1] = value[i, 0:1]
            y_out[s, 1, v, 2 * x + i:2 * x + i + 1] = value[tiles - 2 + i, 7:8]
        for t in range(p.tiles):
            place = x * p.tiles + t
            turned = pltpu.roll(value[t], (4 * place + 2) % 128, 1)
            z = jnp.where(quarter == place, turned, z)
        return z

    def advance(s, c, layers, packed):
        packed = list(packed)
        variables = [c * GROUP + i for i in range(GROUP)]
        terms = [coefficients(s, v) for v in variables]
        ready = []
        for x in layers:
            values = [cells[s, w, x + 2] for w in range(nv)]
            speeds = [speed[a, x] for a in range(3)]
            for i, v in enumerate(variables):
                ready.append((i, v, x, advance_layer(s, v, x, terms[i], values, speeds)))
        for i, v, x, new in ready:
            cells[s + 1, v, x + 2] = new
            if s + 1 < STAGES:
                packed[i] = pack(s + 1, v, x, new, packed[i])
        return packed

    def coefficients(s, v):
        edges = jnp.where(lower, z_in[s, 0, v], z_in[s, 1, v])
        edges = jnp.where(inside, edges, 0.0)
        spread = time_step * diffusivity[v]
        rates = [time_step * coupling[v, w] for w in range(nv)]
        return edges, spread, rates, 1.0 - 6.0 * spread

    def advance_layer(s, v, x, term, values, speeds):
        edges, spread, rates, keep = term
        centre = cells[s, v, x + 2]
        along = [
            jnp.where(sublane == 0, y_in[s, 0, v, 2 * x + i:2 * x + i + 1],
                      pltpu.roll(centre[tiles - 2 + i], 1, 0)) for i in range(2)
        ] + [centre[t] for t in range(tiles)] + [
            jnp.where(sublane == 7, y_in[s, 1, v, 2 * x + i:2 * x + i + 1],
                      pltpu.roll(centre[i], 7, 0)) for i in range(2)
        ]
        shifted = lambda offset: jnp.stack(along[2 + offset:2 + offset + tiles])
        turned = [[], [], [], []]
        for t in range(p.tiles):
            tile = centre[t]
            beside = pltpu.roll(edges, (126 - 4 * (x * p.tiles + t)) % 128, 1)
            for i, (mask, shift) in enumerate(
                    ((lane == 0, 127), (lane == 127, 1), (lane <= 1, 126), (lane >= 126, 2))):
                turned[i].append(pltpu.roll(jnp.where(mask, beside, tile), shift, 1))
        near = [
            (cells[s, v, x + 3], cells[s, v, x + 1], cells[s, v, x + 4], cells[s, v, x]),
            (shifted(1), shifted(-1), shifted(2), shifted(-2)),
            tuple(jnp.stack(parts) for parts in turned),
        ]
        moved = around = None
        for a, (next1, last1, next2, last2) in enumerate(near):
            flow = speeds[a] * (8.0 * (next1 - last1) - (next2 - last2))
            both = next1 + last1
            moved = flow if moved is None else moved + flow
            around = both if around is None else around + both
        factor = keep
        for w in range(nv):
            factor = factor + rates[w] * values[w]
        new = centre * factor + moved + spread * around
        if s % 2 == 1:
            new = 0.5 * (new + cells[s - 1, v, x + 2])
        return new

    def fetch(i, source, target):
        copy = pltpu.make_async_copy(source, target, load_sem.at[i])
        copy.start()
        return copy

    partners = [
        {"gy": lax.rem(my + dy, ny), "gz": lax.rem(mz + dz, nz)}
        for dy in range(ny) for dz in range(nz) if dy or dz
    ]
    line = [{"gx": lax.rem(mx + dx, nx)} for dx in range(1, nx)]
    barrier = pltpu.get_barrier_semaphore()
    for device in partners + line:
        pl.semaphore_signal(barrier, inc=1, device_id=device, device_id_type=MESH)
    load = fetch(0, fields, raw.at[:, 2:lx + 2])
    load_rest = [
        fetch(1, velocity, raw_speed),
        fetch(2, diffusivity_in, diffusivity),
        fetch(3, coupling_in, coupling),
        fetch(4, factor_x_in, factor_x),
        fetch(5, factor_y_in, factor_y),
        fetch(6, factor_z_in, factor_z),
    ]

    def clear(condition, ref, *index):
        @pl.when(jnp.logical_not(condition))
        def _():
            ref[index] = jnp.zeros_like(ref[index])

    for s in range(STAGES):
        edge = cells if s else raw
        lead = (s,) if s else ()
        clear(low_x, edge, *lead, slice(None), slice(0, 2))
        clear(high_x, edge, *lead, slice(None), slice(lx + 2, lx + 4))
        clear(low_y, y_in, s, 0)
        clear(high_y, y_in, s, 1)

    pl.semaphore_wait(barrier, len(partners) + len(line))

    for c in range(nv // GROUP):
        start(x_messages(0, c))
    load.wait()

    blank = jnp.zeros((8, 128), jnp.float32)

    def arrange(v, x):
        for t in range(tiles):
            cells[0, v, x, t] = raw[v, x, pl.ds(t, 8, stride=tiles)]

    def first_pack(c, carry):
        for v in (c * GROUP + i for i in range(GROUP)):
            z = blank
            for x in range(lx):
                arrange(v, x + 2)
                z = pack(0, v, x, cells[0, v, x + 2], z)
            z_out[0, v] = z
        start(yz_messages(0, c))
        return carry

    lax.fori_loop(0, nv // GROUP, first_pack, 0)
    for copy in load_rest:
        copy.wait()

    def arrange_speed(a, carry):
        for x in range(lx):
            for t in range(tiles):
                speed[a, x, t] = raw_speed[a, x, pl.ds(t, 8, stride=tiles)] * (-time_step / 12.0)
        return carry

    lax.fori_loop(0, 3, arrange_speed, 0)

    def split(value):
        high = value.astype(jnp.bfloat16)
        return high, (value - high.astype(jnp.float32)).astype(jnp.bfloat16)

    def product(a, b, contract=((1,), (0,))):
        (a_high, a_low), (b_high, b_low) = a, b
        dot = functools.partial(
            lax.dot_general, dimension_numbers=(contract, ((), ())), preferred_element_type=jnp.float32)
        return dot(a_high, b_high) + (dot(a_high, b_low) + dot(a_low, b_high))

    chunk_y = lx * p.by
    wide_y = ny * chunk_y
    column = lax.broadcasted_iota(jnp.int32, (p.rank, wide_y), 1)
    row = lax.broadcasted_iota(jnp.int32, (p.rank, wide_y), 0)
    place_y = jnp.where(row == column // chunk_y * p.by + column % p.by, 1.0, 0.0)
    column = lax.broadcasted_iota(jnp.int32, (ly, ly), 1)
    row = lax.broadcasted_iota(jnp.int32, (ly, ly), 0)
    order = jnp.where(column == row % 8 * tiles + row // 8, 1.0, 0.0)
    ordered = jnp.dot(order, factor_y[...], precision=HIGHEST, preferred_element_type=jnp.float32)
    repeated = jnp.dot(ordered, place_y, precision=HIGHEST, preferred_element_type=jnp.float32)
    column = lax.broadcasted_iota(jnp.int32, (ly, wide_y), 1) % chunk_y // p.by
    for x in range(lx):
        for i, part in enumerate(split(jnp.where(column == x, repeated, 0.0))):
            spread_y[i, x * ly:(x + 1) * ly] = part
    chunk_x = p.ax * p.by
    wide_x = nx * chunk_x
    column = lax.broadcasted_iota(jnp.int32, (p.rank, wide_x), 1)
    row = lax.broadcasted_iota(jnp.int32, (p.rank, wide_x), 0)
    place_x = jnp.where(row == column // p.by, 1.0, 0.0)
    repeated = jnp.dot(factor_x[...], place_x, precision=HIGHEST, preferred_element_type=jnp.float32)
    column = lax.broadcasted_iota(jnp.int32, (p.by, wide_x), 1) % p.by
    row = lax.broadcasted_iota(jnp.int32, (p.by, wide_x), 0)
    for x in range(lx):
        for i, part in enumerate(split(jnp.where(column == row, repeated[x:x + 1], 0.0))):
            spread_x[i, x * p.by:(x + 1) * p.by] = part

    def plane_message(i, which):
        device = partners[i]
        return pltpu.make_async_remote_copy(
            src_ref=yz_out.at[device["gy"] * nz + device["gz"], which], dst_ref=yz_in.at[i, which],
            send_sem=yz_send.at[i], recv_sem=yz_recv.at[i],
            device_id=device, device_id_type=MESH)

    for s in range(STAGES):
        last = s == STAGES - 1

        def project(v):
            state = cells[STAGES, v, 2:lx + 2].reshape(lx * ly, p.lz)
            reduced = product(split(factor_z[...]), split(state), ((1,), (1,)))
            reduced = product(split(reduced), (spread_y[0], spread_y[1]))
            for y in range(ny):
                for z in range(nz):
                    yz_out[y * nz + z, v] = reduced[
                        z * p.cz:(z + 1) * p.cz, y * chunk_y:(y + 1) * chunk_y]

        def stage(c, carry):
            variables = [c * GROUP + i for i in range(GROUP)]
            arrive(yz_messages(s, c) + x_messages(s, c))
            if s == 0:
                for v in variables:
                    for x in (0, 1, lx + 2, lx + 3):
                        arrange(v, x)
            packed = advance(s, c, p.edge, [blank] * GROUP)
            if not last:
                start(x_messages(s + 1, c))
            packed = advance(s, c, p.inner, packed)
            if last:
                for v in variables:
                    project(v)
                for i in range(len(partners)):
                    plane_message(i, pl.ds(c * GROUP, GROUP)).start()
            else:
                for v, z in zip(variables, packed):
                    z_out[s + 1, v] = z
                start(yz_messages(s + 1, c))
            return carry

        lax.fori_loop(0, nv // GROUP, stage, 0)

    plane = [plane_message(i, slice(None)) for i in range(len(partners))]
    total = yz_out[my * nz + mz]
    for i, copy in enumerate(plane):
        copy.wait_recv()
        total = total + yz_in[i]

    total = total.reshape(nv * p.cz, chunk_y)
    total = product(split(total), (spread_x[0], spread_x[1]))
    for x in range(nx):
        x_out[x] = total[:, x * chunk_x:(x + 1) * chunk_x].reshape(nv, p.cz, chunk_x)
    along = []
    for i, device in enumerate(line):
        along.append(pltpu.make_async_remote_copy(
            src_ref=x_out.at[device["gx"]], dst_ref=x_in.at[i],
            send_sem=xs_send.at[i], recv_sem=xs_recv.at[i],
            device_id=device, device_id_type=MESH))
        along[-1].start()
    total = x_out[mx]
    for i, copy in enumerate(along):
        copy.wait_recv()
        total = total + x_in[i]
    for a in range(p.ax):
        out[:, a] = total[:, :, a * p.by:(a + 1) * p.by]

    all_sent()
    for copy in plane + along:
        copy.wait_send()


def local_kernel(plan, fields, velocity, diffusivity, coupling, factor_x, factor_y, factor_z):
    p = plan
    nv, lx, ly = p.vars, p.lx, p.ly
    chunk_y, chunk_x = lx * p.by, p.ax * p.by
    others = p.ny * p.nz - 1
    vmem = lambda *shape: pltpu.VMEM(shape, jnp.float32)
    dma = lambda *shape: pltpu.SemaphoreType.DMA(shape)
    whole = pl.BlockSpec(memory_space=pltpu.VMEM)
    result = pl.pallas_call(
        functools.partial(kernel, p),
        out_shape=pltpu.VMEM((nv, p.ax, p.cz, p.by), jnp.float32),
        in_specs=[pl.BlockSpec(memory_space=pl.ANY)] * 7,
        out_specs=whole,
        scratch_shapes=[
            pltpu.SMEM(diffusivity.shape, jnp.float32),
            pltpu.SMEM(coupling.shape, jnp.float32),
            vmem(*factor_x.shape),
            vmem(*factor_y.shape),
            vmem(*factor_z.shape[::-1]),
            vmem(nv, lx + 4, ly, p.lz),
            vmem(3, lx, ly, p.lz),
            vmem(STAGES + 1, nv, lx + 4, p.tiles, 8, p.lz),
            vmem(3, lx, p.tiles, 8, p.lz),
            vmem(STAGES, 2, nv, 8 * -(-lx // 4), p.lz),
            vmem(STAGES, 2, nv, 8 * -(-lx // 4), p.lz),
            vmem(STAGES, nv, 8, 128),
            vmem(STAGES, 2, nv, 8, 128),
            pltpu.VMEM((2, lx * ly, p.ny * chunk_y), jnp.bfloat16),
            pltpu.VMEM((2, chunk_y, p.nx * chunk_x), jnp.bfloat16),
            vmem(p.ny * p.nz, nv, p.cz, chunk_y),
            vmem(others, nv, p.cz, chunk_y),
            vmem(p.nx, nv, p.cz, chunk_x),
            vmem(p.nx - 1, nv, p.cz, chunk_x),
            dma(7),
            dma(2), dma(STAGES, nv, 2),
            dma(2), dma(STAGES, nv, 2),
            dma(2), dma(STAGES, nv, 2),
            dma(others), dma(others),
            dma(p.nx - 1), dma(p.nx - 1),
        ],
        compiler_params=pltpu.CompilerParams(
            collective_id=0, has_side_effects=True, vmem_limit_bytes=VMEM_LIMIT),
    )(fields, velocity, diffusivity, coupling, factor_x, factor_y, factor_z.T)
    return jnp.transpose(result, (0, 1, 3, 2))


def solution(mesh):
    def local(fields, velocity, diffusivity, coupling, factor_x, factor_y, factor_z):
        plan = Plan(mesh.shape, fields.shape, factor_x.shape)
        run = functools.partial(local_kernel, plan) if plan.fits() else local_plain
        return run(fields, velocity, diffusivity, coupling, factor_x, factor_y, factor_z)

    return jax.shard_map(
        local,
        mesh=mesh,
        in_specs=(
            P(None, "gx", "gy", "gz"),
            P(None, "gx", "gy", "gz"),
            P(),
            P(),
            P("gx", None),
            P("gy", None),
            P("gz", None),
        ),
        out_specs=P(None, "gx", "gy", "gz"),
        check_vma=False,
    )
```

```python
import functools
import jax
import jax.numpy as jnp
from jax import lax
from jax.experimental import pallas as pl
from jax.experimental.pallas import tpu as pltpu
from jax.sharding import PartitionSpec as P

STEPS = 2
STAGES = 2 * STEPS
HALO = 2
GROUP = 1
VMEM_LIMIT = 66 * 1000 * 1000
MESH = pl.DeviceIdType.MESH
HIGHEST = lax.Precision.HIGHEST


time_step = 0.2
def with_halo(cells, sides, width):
    for axis, dim in sides:
        count = lax.axis_size(axis)
        ends = count - 1
        head = lax.slice_in_dim(cells, 0, width, axis=dim)
        tail = lax.slice_in_dim(cells, cells.shape[dim] - width, cells.shape[dim], axis=dim)
        cells = jnp.concatenate(
            [
                lax.ppermute(tail, axis, [(i, (i + 1) % count) for i in range(ends)]),
                cells,
                lax.ppermute(head, axis, [((i + 1) % count, i) for i in range(ends)]),
            ],
            axis=dim,
        )
    return cells


def offset_view(padded, dimension, offset):
    indices = [slice(None)]
    for other in (1, 2, 3):
        if other == dimension:
            first_cell = 2 + offset
            indices.append(slice(first_cell, first_cell + padded.shape[other] - 4))
        else:
            indices.append(slice(2, padded.shape[other] - 2))
    return padded[tuple(indices)]


def tendency(padded, velocity, diffusivity, coupling):
    center = offset_view(padded, 1, 0)
    transport = jnp.zeros_like(center)
    laplace = jnp.zeros_like(center)
    for dimension in (1, 2, 3):
        gradient = (
            8.0 * (offset_view(padded, dimension, 1) - offset_view(padded, dimension, -1))
            - (offset_view(padded, dimension, 2) - offset_view(padded, dimension, -2))
        ) / 12.0
        transport = transport + velocity[dimension - 1][None] * gradient
        laplace = (
            laplace
            + offset_view(padded, dimension, 1)
            + offset_view(padded, dimension, -1)
            - 2.0 * center
        )
    mixing = jnp.einsum("vw,wxyz->vxyz", coupling, center, precision=lax.Precision.HIGHEST)
    return -transport + diffusivity[:, None, None, None] * laplace + center * mixing


def with_edges(values):
    return with_halo(values, (("gx", 1), ("gy", 2), ("gz", 3)), 2)


def local_plain(fields, velocity, diffusivity, coupling, factor_x, factor_y, factor_z):
    state = fields
    for repeat in range(STEPS):
        section = state + time_step * tendency(with_edges(state), velocity, diffusivity, coupling)
        state = 0.5 * (
            state
            + section
            + time_step * tendency(with_edges(section), velocity, diffusivity, coupling)
        )
    highest = lax.Precision.HIGHEST
    partial_value = jnp.einsum("vxyz,zc->vxyc", state, factor_z, precision=highest)
    partial_value = lax.psum_scatter(partial_value, "gz", scatter_dimension=3, tiled=True)
    partial_value = jnp.einsum("vxyc,yb->vxbc", partial_value, factor_y, precision=highest)
    partial_value = lax.psum_scatter(partial_value, "gy", scatter_dimension=2, tiled=True)
    partial_value = jnp.einsum("vxbc,xa->vabc", partial_value, factor_x, precision=highest)
    core_tensor = lax.psum_scatter(partial_value, "gx", scatter_dimension=1, tiled=True)
    return core_tensor


class Plan:
    def __init__(self, mesh_shape, fields, factor_x):
        self.nx, self.ny, self.nz = (mesh_shape[a] for a in ("gx", "gy", "gz"))
        self.vars, self.lx, self.ly, self.lz = fields
        self.rank = factor_x[1]
        self.ax, self.by, self.cz = self.rank // self.nx, self.rank // self.ny, self.rank // self.nz
        self.edge = [0, 1, self.lx - 2, self.lx - 1]
        self.inner = list(range(2, self.lx - 2))
        self.tiles = self.ly // 8

    def fits(self):
        return (
            self.lz == 128
            and self.ly % 8 == 0
            and self.ly >= 16
            and min(self.nx, self.ny, self.nz) > 1
            and self.vars % GROUP == 0
            and self.lx > 4
            and self.lx * self.tiles * 4 <= 128
            and self.rank % self.nx == 0 and self.rank % self.ny == 0 and self.rank % self.nz == 0
            and self.cz % 8 == 0
            and self.lx * self.by % 128 == 0
            and self.ax * self.by % 128 == 0
        )


def kernel(
    plan,
    fields,
    velocity,
    diffusivity_in,
    coupling_in,
    factor_x_in,
    factor_y_in,
    factor_z_in,
    out,
    diffusivity,
    coupling,
    factor_x,
    factor_y,
    factor_z,
    raw,
    raw_speed,
    cells,
    speed,
    y_out,
    y_in,
    z_out,
    z_in,
    spread_y,
    spread_x,
    yz_out,
    yz_in,
    x_out,
    x_in,
    load_sem,
    x_send,
    x_recv,
    y_send,
    y_recv,
    z_send,
    z_recv,
    yz_send,
    yz_recv,
    xs_send,
    xs_recv,
):
    p = plan
    nx, ny, nz = p.nx, p.ny, p.nz
    lx, ly, nv = p.lx, p.ly, p.vars
    mx, my, mz = lax.axis_index("gx"), lax.axis_index("gy"), lax.axis_index("gz")
    tiles = p.tiles
    low_x, high_x = mx > 0, mx < nx - 1
    low_y, high_y = my > 0, my < ny - 1
    low_z, high_z = mz > 0, mz < nz - 1

    def remote(src, dst, send, recv, axis, to):
        return pltpu.make_async_remote_copy(
            src_ref=src, dst_ref=dst, send_sem=send, recv_sem=recv,
            device_id={axis: to}, device_id_type=MESH,
        )

    def up(index, count):
        return lax.rem(index + 1, count)

    def down(index, count):
        return lax.rem(index + count - 1, count)

    def x_messages(s, c):
        v = pl.ds(c * GROUP, GROUP)
        if s == 0:
            top, bottom = fields.at[v, lx - 2:lx], fields.at[v, 0:2]
            below, above = raw.at[v, 0:2], raw.at[v, lx + 2:lx + 4]
        else:
            top, bottom = cells.at[s, v, lx:lx + 2], cells.at[s, v, 2:4]
            below, above = cells.at[s, v, 0:2], cells.at[s, v, lx + 2:lx + 4]
        return [
            (high_x, low_x, remote(
                top, below, x_send.at[0], x_recv.at[s, c, 0], "gx", up(mx, nx))),
            (low_x, high_x, remote(
                bottom, above, x_send.at[1], x_recv.at[s, c, 1], "gx", down(mx, nx))),
        ]

    def yz_messages(s, c):
        v = pl.ds(c * GROUP, GROUP)
        result = [
            (None, None, remote(
                z_out.at[s, v], z_in.at[s, 0, v],
                z_send.at[0], z_recv.at[s, c, 0], "gz", up(mz, nz))),
            (None, None, remote(
                z_out.at[s, v], z_in.at[s, 1, v],
                z_send.at[1], z_recv.at[s, c, 1], "gz", down(mz, nz))),
        ]
        if ny == 2:
            result.append((None, None, remote(
                y_out.at[s, 1 - my, v], y_in.at[s, my, v],
                y_send.at[0], y_recv.at[s, c, 0], "gy", 1 - my)))
        else:
            result += [
                (high_y, low_y, remote(
                    y_out.at[s, 1, v], y_in.at[s, 0, v],
                    y_send.at[0], y_recv.at[s, c, 0], "gy", up(my, ny))),
                (low_y, high_y, remote(
                    y_out.at[s, 0, v], y_in.at[s, 1, v],
                    y_send.at[1], y_recv.at[s, c, 1], "gy", down(my, ny))),
            ]
        return result

    def guarded(condition, action):
        if condition is None:
            action()
        else:
            pl.when(condition)(action)

    def start(messages):
        for sends, _, copy in messages:
            guarded(sends, copy.start)

    def arrive(messages):
        for _, gets, copy in messages:
            guarded(gets, copy.wait_recv)

    def all_sent():
        layers = cells.at[0:STAGES, :, 0:2]
        waits = [
            (high_x, remote(layers, layers, x_send.at[0], x_recv.at[0, 0, 0], "gx", up(mx, nx))),
            (low_x, remote(layers, layers, x_send.at[1], x_recv.at[0, 0, 1], "gx", down(mx, nx))),
            (None, remote(z_out, z_out, z_send.at[0], z_recv.at[0, 0, 0], "gz", up(mz, nz))),
            (None, remote(z_out, z_out, z_send.at[1], z_recv.at[0, 0, 1], "gz", down(mz, nz))),
        ]
        half = y_out.at[:, 0]
        if ny == 2:
            waits.append((None, remote(half, half, y_send.at[0], y_recv.at[0, 0, 0], "gy", 1 - my)))
        else:
            waits += [
                (high_y, remote(half, half, y_send.at[0], y_recv.at[0, 0, 0], "gy", up(my, ny))),
                (low_y, remote(half, half, y_send.at[1], y_recv.at[0, 0, 1], "gy", down(my, ny))),
            ]
        for condition, copy in waits:
            guarded(condition, copy.wait_send)

    lane = lax.broadcasted_iota(jnp.int32, (8, 128), 1)
    sublane = lax.broadcasted_iota(jnp.int32, (8, 128), 0)
    quarter = lax.shift_right_logical(lane, 2)
    lower = jnp.bitwise_and(lane, 3) < 2
    inside = jnp.where(lower, jnp.minimum(mz, 1), jnp.minimum(nz - 1 - mz, 1)) > 0

    def pack(s, v, x, value, z):
        for i in range(2):
            y_out[s, 0, v, 2 * x + i:2 * x + i + 1] = value[i, 0:1]
            y_out[s, 1, v, 2 * x + i:2 * x + i + 1] = value[tiles - 2 + i, 7:8]
        for t in range(p.tiles):
            place = x * p.tiles + t
            turned = pltpu.roll(value[t], (4 * place + 2) % 128, 1)
            z = jnp.where(quarter == place, turned, z)
        return z

    def advance(s, c, layers, packed):
        packed = list(packed)
        variables = [c * GROUP + i for i in range(GROUP)]
        terms = [coefficients(s, v) for v in variables]
        ready = []
        for x in layers:
            values = [cells[s, w, x + 2] for w in range(nv)]
            speeds = [speed[a, x] for a in range(3)]
            for i, v in enumerate(variables):
                ready.append((i, v, x, advance_layer(s, v, x, terms[i], values, speeds)))
        for i, v, x, new in ready:
            cells[s + 1, v, x + 2] = new
            if s + 1 < STAGES:
                packed[i] = pack(s + 1, v, x, new, packed[i])
        return packed

    def coefficients(s, v):
        edges = jnp.where(lower, z_in[s, 0, v], z_in[s, 1, v])
        edges = jnp.where(inside, edges, 0.0)
        spread = time_step * diffusivity[v]
        rates = [time_step * coupling[v, w] for w in range(nv)]
        return edges, spread, rates, 1.0 - 6.0 * spread

    def advance_layer(s, v, x, term, values, speeds):
        edges, spread, rates, keep = term
        centre = cells[s, v, x + 2]
        along = [
            jnp.where(sublane == 0, y_in[s, 0, v, 2 * x + i:2 * x + i + 1],
                      pltpu.roll(centre[tiles - 2 + i], 1, 0)) for i in range(2)
        ] + [centre[t] for t in range(tiles)] + [
            jnp.where(sublane == 7, y_in[s, 1, v, 2 * x + i:2 * x + i + 1],
                      pltpu.roll(centre[i], 7, 0)) for i in range(2)
        ]
        shifted = lambda offset: jnp.stack(along[2 + offset:2 + offset + tiles])
        turned = [[], [], [], []]
        for t in range(p.tiles):
            tile = centre[t]
            beside = pltpu.roll(edges, (126 - 4 * (x * p.tiles + t)) % 128, 1)
            for i, (mask, shift) in enumerate(
                    ((lane == 0, 127), (lane == 127, 1), (lane <= 1, 126), (lane >= 126, 2))):
                turned[i].append(pltpu.roll(jnp.where(mask, beside, tile), shift, 1))
        near = [
            (cells[s, v, x + 3], cells[s, v, x + 1], cells[s, v, x + 4], cells[s, v, x]),
            (shifted(1), shifted(-1), shifted(2), shifted(-2)),
            tuple(jnp.stack(parts) for parts in turned),
        ]
        moved = around = None
        for a, (next1, last1, next2, last2) in enumerate(near):
            flow = speeds[a] * (8.0 * (next1 - last1) - (next2 - last2))
            both = next1 + last1
            moved = flow if moved is None else moved + flow
            around = both if around is None else around + both
        factor = keep
        for w in range(nv):
            factor = factor + rates[w] * values[w]
        new = centre * factor + moved + spread * around
        if s % 2 == 1:
            new = 0.5 * (new + cells[s - 1, v, x + 2])
        return new

    def fetch(i, source, target):
        copy = pltpu.make_async_copy(source, target, load_sem.at[i])
        copy.start()
        return copy

    partners = [
        {"gy": lax.rem(my + dy, ny), "gz": lax.rem(mz + dz, nz)}
        for dy in range(ny) for dz in range(nz) if dy or dz
    ]
    line = [{"gx": lax.rem(mx + dx, nx)} for dx in range(1, nx)]
    barrier = pltpu.get_barrier_semaphore()
    for device in partners + line:
        pl.semaphore_signal(barrier, inc=1, device_id=device, device_id_type=MESH)
    load = fetch(0, fields, raw.at[:, 2:lx + 2])
    load_rest = [
        fetch(1, velocity, raw_speed),
        fetch(2, diffusivity_in, diffusivity),
        fetch(3, coupling_in, coupling),
        fetch(4, factor_x_in, factor_x),
        fetch(5, factor_y_in, factor_y),
        fetch(6, factor_z_in, factor_z),
    ]

    def clear(condition, ref, *index):
        @pl.when(jnp.logical_not(condition))
        def _():
            ref[index] = jnp.zeros_like(ref[index])

    for s in range(STAGES):
        edge = cells if s else raw
        lead = (s,) if s else ()
        clear(low_x, edge, *lead, slice(None), slice(0, 2))
        clear(high_x, edge, *lead, slice(None), slice(lx + 2, lx + 4))
        clear(low_y, y_in, s, 0)
        clear(high_y, y_in, s, 1)

    pl.semaphore_wait(barrier, len(partners) + len(line))

    for c in range(nv // GROUP):
        start(x_messages(0, c))
    load.wait()

    blank = jnp.zeros((8, 128), jnp.float32)

    def arrange(v, x):
        for t in range(tiles):
            cells[0, v, x, t] = raw[v, x, pl.ds(t, 8, stride=tiles)]

    def first_pack(c, carry):
        for v in (c * GROUP + i for i in range(GROUP)):
            z = blank
            for x in range(lx):
                arrange(v, x + 2)
                z = pack(0, v, x, cells[0, v, x + 2], z)
            z_out[0, v] = z
        start(yz_messages(0, c))
        return carry

    lax.fori_loop(0, nv // GROUP, first_pack, 0)
    for copy in load_rest:
        copy.wait()

    def arrange_speed(a, carry):
        for x in range(lx):
            for t in range(tiles):
                speed[a, x, t] = raw_speed[a, x, pl.ds(t, 8, stride=tiles)] * (-time_step / 12.0)
        return carry

    lax.fori_loop(0, 3, arrange_speed, 0)

    def split(value):
        high = value.astype(jnp.bfloat16)
        return high, (value - high.astype(jnp.float32)).astype(jnp.bfloat16)

    def product(a, b, contract=((1,), (0,))):
        (a_high, a_low), (b_high, b_low) = a, b
        dot = functools.partial(
            lax.dot_general, dimension_numbers=(contract, ((), ())), preferred_element_type=jnp.float32)
        return dot(a_high, b_high) + (dot(a_high, b_low) + dot(a_low, b_high))

    chunk_y = lx * p.by
    wide_y = ny * chunk_y
    column = lax.broadcasted_iota(jnp.int32, (p.rank, wide_y), 1)
    row = lax.broadcasted_iota(jnp.int32, (p.rank, wide_y), 0)
    place_y = jnp.where(row == column // chunk_y * p.by + column % p.by, 1.0, 0.0)
    column = lax.broadcasted_iota(jnp.int32, (ly, ly), 1)
    row = lax.broadcasted_iota(jnp.int32, (ly, ly), 0)
    order = jnp.where(column == row % 8 * tiles + row // 8, 1.0, 0.0)
    ordered = jnp.dot(order, factor_y[...], precision=HIGHEST, preferred_element_type=jnp.float32)
    repeated = jnp.dot(ordered, place_y, precision=HIGHEST, preferred_element_type=jnp.float32)
    column = lax.broadcasted_iota(jnp.int32, (ly, wide_y), 1) % chunk_y // p.by
    for x in range(lx):
        for i, part in enumerate(split(jnp.where(column == x, repeated, 0.0))):
            spread_y[i, x * ly:(x + 1) * ly] = part
    chunk_x = p.ax * p.by
    wide_x = nx * chunk_x
    column = lax.broadcasted_iota(jnp.int32, (p.rank, wide_x), 1)
    row = lax.broadcasted_iota(jnp.int32, (p.rank, wide_x), 0)
    place_x = jnp.where(row == column // p.by, 1.0, 0.0)
    repeated = jnp.dot(factor_x[...], place_x, precision=HIGHEST, preferred_element_type=jnp.float32)
    column = lax.broadcasted_iota(jnp.int32, (p.by, wide_x), 1) % p.by
    row = lax.broadcasted_iota(jnp.int32, (p.by, wide_x), 0)
    for x in range(lx):
        for i, part in enumerate(split(jnp.where(column == row, repeated[x:x + 1], 0.0))):
            spread_x[i, x * p.by:(x + 1) * p.by] = part

    def plane_message(i, which):
        device = partners[i]
        return pltpu.make_async_remote_copy(
            src_ref=yz_out.at[device["gy"] * nz + device["gz"], which], dst_ref=yz_in.at[i, which],
            send_sem=yz_send.at[i], recv_sem=yz_recv.at[i],
            device_id=device, device_id_type=MESH)

    groups = nv // GROUP

    def project(v):
        state = cells[STAGES, v, 2:lx + 2].reshape(lx * ly, p.lz)
        reduced = product(split(factor_z[...]), split(state), ((1,), (1,)))
        reduced = product(split(reduced), (spread_y[0], spread_y[1]))
        for y in range(ny):
            for z in range(nz):
                yz_out[y * nz + z, v] = reduced[
                    z * p.cz:(z + 1) * p.cz, y * chunk_y:(y + 1) * chunk_y]

    def edge_layers(s, c):
        variables = [c * GROUP + i for i in range(GROUP)]
        arrive(yz_messages(s, c) + x_messages(s, c))
        if s == 0:
            for v in variables:
                for x in (0, 1, lx + 2, lx + 3):
                    arrange(v, x)
        packed = advance(s, c, p.edge, [blank] * GROUP)
        if s + 1 < STAGES:
            start(x_messages(s + 1, c))
            for v, z in zip(variables, packed):
                z_out[s + 1, v] = z

    def inner_layers(s, c):
        variables = [c * GROUP + i for i in range(GROUP)]
        if s + 1 < STAGES:
            packed = advance(s, c, p.inner, [z_out[s + 1, v] for v in variables])
            for v, z in zip(variables, packed):
                z_out[s + 1, v] = z
            start(yz_messages(s + 1, c))
        else:
            advance(s, c, p.inner, [blank] * GROUP)
            for v in variables:
                project(v)
            for i in range(len(partners)):
                plane_message(i, pl.ds(c * GROUP, GROUP)).start()

    for s in range(STAGES):
        edge_layers(s, 0)
        if s > 0:
            inner_layers(s - 1, groups - 1)

        def stage(c, carry):
            edge_layers(s, c)
            inner_layers(s, c - 1)
            return carry

        lax.fori_loop(1, groups, stage, 0)
    inner_layers(STAGES - 1, groups - 1)

    plane = [plane_message(i, slice(None)) for i in range(len(partners))]
    total = yz_out[my * nz + mz]
    for i, copy in enumerate(plane):
        copy.wait_recv()
        total = total + yz_in[i]

    total = total.reshape(nv * p.cz, chunk_y)
    total = product(split(total), (spread_x[0], spread_x[1]))
    for x in range(nx):
        x_out[x] = total[:, x * chunk_x:(x + 1) * chunk_x].reshape(nv, p.cz, chunk_x)
    along = []
    for i, device in enumerate(line):
        along.append(pltpu.make_async_remote_copy(
            src_ref=x_out.at[device["gx"]], dst_ref=x_in.at[i],
            send_sem=xs_send.at[i], recv_sem=xs_recv.at[i],
            device_id=device, device_id_type=MESH))
        along[-1].start()
    total = x_out[mx]
    for i, copy in enumerate(along):
        copy.wait_recv()
        total = total + x_in[i]
    for a in range(p.ax):
        out[:, a] = total[:, :, a * p.by:(a + 1) * p.by]

    all_sent()
    for copy in plane + along:
        copy.wait_send()


def local_kernel(plan, fields, velocity, diffusivity, coupling, factor_x, factor_y, factor_z):
    p = plan
    nv, lx, ly = p.vars, p.lx, p.ly
    chunk_y, chunk_x = lx * p.by, p.ax * p.by
    others = p.ny * p.nz - 1
    vmem = lambda *shape: pltpu.VMEM(shape, jnp.float32)
    dma = lambda *shape: pltpu.SemaphoreType.DMA(shape)
    whole = pl.BlockSpec(memory_space=pltpu.VMEM)
    result = pl.pallas_call(
        functools.partial(kernel, p),
        out_shape=pltpu.VMEM((nv, p.ax, p.cz, p.by), jnp.float32),
        in_specs=[pl.BlockSpec(memory_space=pl.ANY)] * 7,
        out_specs=whole,
        scratch_shapes=[
            pltpu.SMEM(diffusivity.shape, jnp.float32),
            pltpu.SMEM(coupling.shape, jnp.float32),
            vmem(*factor_x.shape),
            vmem(*factor_y.shape),
            vmem(*factor_z.shape[::-1]),
            vmem(nv, lx + 4, ly, p.lz),
            vmem(3, lx, ly, p.lz),
            vmem(STAGES + 1, nv, lx + 4, p.tiles, 8, p.lz),
            vmem(3, lx, p.tiles, 8, p.lz),
            vmem(STAGES, 2, nv, 8 * -(-lx // 4), p.lz),
            vmem(STAGES, 2, nv, 8 * -(-lx // 4), p.lz),
            vmem(STAGES, nv, 8, 128),
            vmem(STAGES, 2, nv, 8, 128),
            pltpu.VMEM((2, lx * ly, p.ny * chunk_y), jnp.bfloat16),
            pltpu.VMEM((2, chunk_y, p.nx * chunk_x), jnp.bfloat16),
            vmem(p.ny * p.nz, nv, p.cz, chunk_y),
            vmem(others, nv, p.cz, chunk_y),
            vmem(p.nx, nv, p.cz, chunk_x),
            vmem(p.nx - 1, nv, p.cz, chunk_x),
            dma(7),
            dma(2), dma(STAGES, nv, 2),
            dma(2), dma(STAGES, nv, 2),
            dma(2), dma(STAGES, nv, 2),
            dma(others), dma(others),
            dma(p.nx - 1), dma(p.nx - 1),
        ],
        compiler_params=pltpu.CompilerParams(
            collective_id=0, has_side_effects=True, vmem_limit_bytes=VMEM_LIMIT),
    )(fields, velocity, diffusivity, coupling, factor_x, factor_y, factor_z.T)
    return jnp.transpose(result, (0, 1, 3, 2))


def solution(mesh):
    def local(fields, velocity, diffusivity, coupling, factor_x, factor_y, factor_z):
        plan = Plan(mesh.shape, fields.shape, factor_x.shape)
        run = functools.partial(local_kernel, plan) if plan.fits() else local_plain
        return run(fields, velocity, diffusivity, coupling, factor_x, factor_y, factor_z)

    return jax.shard_map(
        local,
        mesh=mesh,
        in_specs=(
            P(None, "gx", "gy", "gz"),
            P(None, "gx", "gy", "gz"),
            P(),
            P(),
            P("gx", None),
            P("gy", None),
            P("gz", None),
        ),
        out_specs=P(None, "gx", "gy", "gz"),
        check_vma=False,
    )
```
